128 devices in a mesh: gx: 16 (over z, y), gy: 8 (over x, core).
Axes of the slice: x: 4, y: 4, z: 4, core: 2. Of those that a mesh axis runs over, the one named last changes fastest.
Arguments:
- fields: float32 [4, 1, 2048, 2048], P(None, None, 'gx', 'gy'), may hold values from -1200 to 1200
- viscosity: float32 [1, 2048, 2048], P(None, 'gx', 'gy'), may hold values from 0.25 to 4
- diffusivity: float32 [1, 2048, 2048], P(None, 'gx', 'gy'), may hold values from 0.25 to 4
Outputs:
- updated: float32 [4, 1, 2048, 2048], P(None, None, 'gx', 'gy')
The draws below stay inside these ranges and needn't reach their ends.
All inputs are finite; a program needn't handle non-finite values.
Results may differ from the reference program's by a relative error of at most 0.0003.
Values sent between devices are 32-bit elements; how exact they have to be, the bound alone decides.
No kernel may reach another device: no remote copies, remote signals or barrier semaphores. Data moves between devices by JAX's collectives and lax.ppermute only.
A program may use at most 64 MiB of HBM per device.

```python
import math
import jax
import jax.numpy as jnp
from jax import lax

F = 4
Z = 1
CX = 128
CY = 256
NX = 2048
NY = 2048


def draw_fields(key, part):
    key = jax.random.fold_in(key, 11)
    full_shape = (F, Z, NX, NY)
    return 300.0 * jax.random.truncated_normal(key, -4.0, 4.0, full_shape, jnp.float32)


def block_levels(own_key, extent, split, low, high):
    def one(axis_at, blocks):
        draws = jax.random.uniform(jax.random.fold_in(jax.random.fold_in(own_key, 6), axis_at), (blocks,), jnp.float32, low / len(split), high / len(split))
        return jnp.repeat(jnp.exp(draws), extent[axis_at] // blocks).reshape((-1,) + (1,) * (len(extent) - axis_at - 1))

    loudness = one(*split[0])
    for cut in split[1:]:
        loudness = loudness * one(*cut)
    return loudness


def setup_inputs(seed: int = 0) -> dict:
    arg_keys = jax.random.split(jax.random.key(seed), 4)
    return {
        "fields": draw_fields(jax.random.fold_in(arg_keys[3], 71), 0),
        "viscosity": jnp.clip(jnp.exp(math.log(4.0) - 2.7725887 * jax.random.uniform(arg_keys[1], (Z, NX, NY), jnp.float32) ** block_levels(arg_keys[1], (Z, NX, NY), ((1, 16), (2, 8)), -0.2, 0.2)), 0.25, 4.0),
        "diffusivity": jnp.clip(jnp.exp(math.log(4.0) - 2.7725887 * jax.random.uniform(arg_keys[2], (Z, NX, NY), jnp.float32) ** block_levels(arg_keys[2], (Z, NX, NY), ((1, 16), (2, 8)), -0.2, 0.2)), 0.25, 4.0),
    }


def couplings(padded_coef, strength):
    faces = strength * 0.5 * (padded_coef[:-1] + padded_coef[1:])
    return faces[:-1], faces[1:]


def thomas_lines(right_side, coef, strength):
    padded_coef = jnp.pad(coef, ((1, 1), (0, 0)))
    lower_face, upper_face = couplings(padded_coef, strength)
    row_index = lax.broadcasted_iota(jnp.int32, right_side.shape, 0)
    surplus_all = 1.0 + jnp.where(row_index == 0, lower_face, 0.0)

    def forward(carry, row_items):
        prev_excess, prev_diagonal, prev_value = carry
        link_down, link_up, surplus, source = row_items
        new_excess = surplus + link_down * prev_excess / prev_diagonal
        new_diagonal = new_excess + link_up
        new_value = (source + link_down * prev_value) / new_diagonal
        return (new_excess, new_diagonal, new_value), (link_up / new_diagonal, new_value)

    zeros = jnp.zeros_like(right_side[0])
    start = (zeros, zeros + 1.0, zeros)
    _, (ratios, values) = lax.scan(forward, start, (lower_face, upper_face, surplus_all, right_side))

    def backward(following, row_items):
        ratio, value = row_items
        current = value + ratio * following
        return current, current

    _, solved = lax.scan(backward, zeros, (ratios, values), reverse=True)
    return solved


def reference(fields, viscosity, diffusivity):
    coef_all = jnp.concatenate([jnp.broadcast_to(viscosity[None], (3,) + viscosity.shape), diffusivity[None]], axis=0)
    full_shape = fields.shape
    field_planes = fields.reshape((-1,) + full_shape[2:])
    coef_planes = coef_all.reshape((-1,) + full_shape[2:])

    def one_plane(items):
        field_plane, coef_plane = items
        swept = thomas_lines(field_plane, coef_plane, float(CX * CX))
        return thomas_lines(swept.T, coef_plane.T, float(CY * CY)).T

    return lax.map(one_plane, (field_planes, coef_planes)).reshape(full_shape)
```

```python
import functools

import jax
import jax.numpy as jnp
from jax import lax
from jax.experimental import pallas as pl
from jax.experimental.pallas import tpu as pltpu
from jax.sharding import PartitionSpec as P


FIELDS = 4
KIND = (0, 0, 0, 1)
LANES = 128
SUB = 8
COEF_ROWS = 5
QUANTITIES = 2 * COEF_ROWS + 2 * FIELDS


def recip(value):
    guess = pl.reciprocal(value, approx=True)
    return guess * (2.0 - value * guess)


def up(rows, step):
    step %= rows.shape[0]
    return pltpu.roll(rows, rows.shape[0] - step, 0) if step else rows


def down(rows, step):
    return pltpu.roll(rows, step, 0)


def row_index(rows):
    return lax.broadcasted_iota(jnp.int32, (rows, LANES), 0)


def pair(left, ground_u, link, ground_v, right):
    total_u, total_v = left + ground_u, right + ground_v
    scale = recip(total_u * total_v + link * (total_u + total_v))
    return (total_v + link) * scale, link * scale, (total_u + link) * scale


def join(link, ground_a, ground_b, face, shift):
    right, ground_v = up(link, shift), up(ground_a, shift)
    uu, uv, vv = pair(link, ground_b, face, ground_v, right)
    u_left, v_left, u_right, v_right = link * uu, link * uv, right * uv, right * vv
    joined = (
        v_left * right,
        ground_a + ground_b * u_left + ground_v * v_left,
        up(ground_b, shift) + ground_b * u_right + ground_v * v_right,
    )
    return joined, (uu, uv, vv, u_left, v_left, u_right, v_right)


def join_sources(source_a, source_b, weights, shift):
    _, _, _, u_left, v_left, u_right, v_right = weights
    source_v = up(source_a, shift)
    return (
        source_a + source_b * u_left + source_v * v_left,
        up(source_b, shift) + source_b * u_right + source_v * v_right,
    )


def eliminate(coefs, half):
    count = len(coefs)
    ground = [1.0] * count
    links = [half * (coefs[i] + coefs[i + 1]) for i in range(count - 1)]
    nodes, plan = list(range(count)), []
    while len(nodes) > 2:
        kept, kept_links, i = [nodes[0]], [], 1
        while i <= len(nodes) - 2:
            low, cell, high = kept[-1], nodes[i], nodes[i + 1]
            scale = recip(links[i - 1] + links[i] + ground[cell])
            to_low, to_high = links[i - 1] * scale, links[i] * scale
            ground[low] = ground[low] + to_low * ground[cell]
            ground[high] = ground[high] + to_high * ground[cell]
            kept.append(high)
            kept_links.append(to_low * links[i])
            plan.append((cell, low, high, scale, to_low, to_high))
            i += 2
        if i == len(nodes) - 1:
            kept.append(nodes[i])
            kept_links.append(links[i - 1])
        nodes, links = kept, kept_links
    face = half * (coefs[-1] + up(coefs[0], 1))
    chain, joins = (links[0], ground[0], ground[-1]), []
    for shift in (1, 2, 4):
        chain, weights = join(*chain, up(face, shift - 1), shift)
        joins.append((shift, weights))
    return plan, joins, chain


def push_sources(plan, joins, sources):
    sources = list(sources)
    for cell, low, high, _, to_low, to_high in plan:
        sources[low] = sources[low] + to_low * sources[cell]
        sources[high] = sources[high] + to_high * sources[cell]
    ends, history = (sources[0], sources[-1]), []
    for shift, weights in joins:
        history.append(ends)
        ends = join_sources(*ends, weights, shift)
    return sources, history, ends


def pull_values(plan, joins, count, end_a, end_b, sources=None, history=None):
    row = row_index(SUB)
    for index in reversed(range(len(joins))):
        shift, (uu, uv, vv, u_left, v_left, u_right, v_right) = joins[index]
        value_u = u_left * end_a + u_right * end_b
        value_v = v_left * end_a + v_right * end_b
        if history is not None:
            source_u, source_v = history[index][1], up(history[index][0], shift)
            value_u = value_u + uu * source_u + uv * source_v
            value_v = value_v + uv * source_u + vv * source_v
        on_right = (row // shift) % 2 == 1
        end_a = jnp.where(on_right, down(value_v, shift), end_a)
        end_b = jnp.where(on_right, down(end_b, shift), value_u)
    values = [None] * count
    values[0], values[-1] = end_a, end_b
    for cell, low, high, scale, to_low, to_high in reversed(plan):
        value = to_low * values[low] + to_high * values[high]
        values[cell] = value if sources is None else value + scale * sources[cell]
    return values


def responses(plan, joins, count):
    one = jnp.ones((SUB, LANES), jnp.float32)
    zero = jnp.zeros((SUB, LANES), jnp.float32)
    return (
        pull_values(plan, joins, count, one, zero),
        pull_values(plan, joins, count, zero, one),
    )


def inside(plan, joins, count, sources):
    zero = jnp.zeros((SUB, LANES), jnp.float32)
    pushed, history, _ = push_sources(plan, joins, sources)
    return pull_values(plan, joins, count, zero, zero, pushed, history)


def load_cells(ref, count):
    return [ref[pl.ds(t, SUB, stride=count), :] for t in range(count)]


def store_cells(ref, values):
    for t, value in enumerate(values):
        ref[pl.ds(t, SUB, stride=len(values)), :] = value


def tiles(array):
    x_cells, y_cells = array.shape[-2:]
    split = array.reshape(-1, x_cells // SUB, SUB, y_cells // LANES, LANES)
    return split.transpose(0, 1, 3, 2, 4).reshape(-1, LANES)


def untiles(flat, shape):
    split = flat.reshape(-1, shape[-2] // SUB, shape[-1] // LANES, SUB, LANES)
    return split.transpose(0, 1, 3, 2, 4).reshape(shape)


def tile_at(field, x_tile, block, x_cells, blocks):
    return ((field * (x_cells // SUB) + x_tile) * blocks + block) * SUB


def load_x_cells(ref, field, block, x_cells, blocks):
    count = x_cells // SUB
    return [
        ref[pl.ds(tile_at(field, t // SUB, block, x_cells, blocks) + t % SUB, SUB, stride=count * blocks), :]
        for t in range(count)
    ]


def load_block(ref, field, block, x_cells, blocks):
    return jnp.concatenate(
        [ref[pl.ds(tile_at(field, i, block, x_cells, blocks), SUB), :] for i in range(x_cells // SUB)]
    )


def load_turned(ref, field, x_cells, blocks, turned):
    for block in range(blocks):
        turned[pl.ds(block * LANES, LANES), :] = load_block(ref, field, block, x_cells, blocks).T


def solve_ring(quantity, ranks, rank, half):
    row = row_index(ranks)
    device = lax.rem(row + (rank + 1), ranks)
    first, last = device == 0, device == ranks - 1
    results = []
    for kind in range(2):
        first_coef, last_coef, link, ground_a, ground_b = [
            quantity(kind * COEF_ROWS + i) for i in range(COEF_ROWS)
        ]
        ground_a = ground_a + jnp.where(first, half * first_coef, 0.0)
        ground_b = ground_b + jnp.where(last, half * last_coef, 0.0)
        face = jnp.where(last, 0.0, half * (last_coef + up(first_coef, 1)))
        own = [up(x, ranks - 1) for x in (link, ground_a, ground_b)]
        left, right = up(face, ranks - 1), up(face, ranks - 2)
        fields = [f for f in range(FIELDS) if KIND[f] == kind]
        sources = [
            (quantity(2 * COEF_ROWS + 2 * f), quantity(2 * COEF_ROWS + 2 * f + 1)) for f in fields
        ]
        own_sources = [[up(x, ranks - 1) for x in pair_] for pair_ in sources]
        chain, shift = (link, ground_a, ground_b), 1
        while shift < ranks:
            joined, weights = join(*chain, up(face, shift - 1), shift)
            joined_sources = [join_sources(*s, weights, shift) for s in sources]
            if shift == 1:
                alone = row == ranks - 2
                joined = [jnp.where(alone, a, b) for a, b in zip(chain, joined)]
                joined_sources = [
                    [jnp.where(alone, a, b) for a, b in zip(old, new)]
                    for old, new in zip(sources, joined_sources)
                ]
            chain, sources, shift = joined, joined_sources, 2 * shift
        link, ground_u, ground_v = chain
        uu, uv, vv = pair(left, ground_u, link, ground_v, right)
        u_b, v_b, u_a, v_a = left * uu, left * uv, right * uv, right * vv
        link = own[0] + v_b * right
        ground_a = own[1] + ground_u * u_a + ground_v * v_a
        ground_b = own[2] + ground_u * u_b + ground_v * v_b
        scale = recip(ground_a * ground_b + link * (ground_a + ground_b))
        aa, ab, bb = (ground_b + link) * scale, link * scale, (ground_a + link) * scale
        for (source_u, source_v), (source_a, source_b) in zip(sources, own_sources):
            source_a = source_a + source_u * u_a + source_v * v_a
            source_b = source_b + source_u * u_b + source_v * v_b
            results.append((aa * source_a + ab * source_b, ab * source_a + bb * source_b))
    return results


def rotate(received, turned, ranks, rows, rank):
    for k in range(ranks):
        source = pl.multiple_of(lax.rem(rank + 1 + k, ranks) * rows, SUB)
        turned[pl.ds(k * rows, rows), :] = received[pl.ds(source, rows), :]


def coef_rows(coefs, chain):
    return (coefs[0][:1], coefs[-1][SUB - 1 :], chain[0][:1], chain[1][:1], chain[2][:1])


def x_ends_kernel(half, x_cells, blocks, ranks, rows, fields, viscosity, diffusivity, message, line):
    line[...] = jnp.zeros_like(line)
    for block in range(blocks):

        def put(quantity, value):
            at = quantity * blocks + block
            line[at : at + 1, :] = value

        for kind, coef in enumerate((viscosity, diffusivity)):
            coefs = load_x_cells(coef, 0, block, x_cells, blocks)
            plan, joins, chain = eliminate(coefs, half)
            for i, value in enumerate(coef_rows(coefs, chain)):
                put(kind * COEF_ROWS + i, value)
            for f in range(FIELDS):
                if KIND[f] == kind:
                    _, _, ends = push_sources(plan, joins, load_x_cells(fields, f, block, x_cells, blocks))
                    put(2 * COEF_ROWS + 2 * f, ends[0][:1])
                    put(2 * COEF_ROWS + 2 * f + 1, ends[1][:1])
    for k in range(ranks):
        message[pl.ds(k * rows, rows), :] = line[...]


def local_kernel(
    half_x, half_y, x_cells, blocks,
    fields, viscosity, diffusivity, inner, x_a, x_b, y_a, y_b, y_rows, turned, result,
):
    count, y_count = x_cells // SUB, blocks * LANES // SUB
    y_rows[...] = jnp.zeros_like(y_rows)
    for kind, coef in enumerate((viscosity, diffusivity)):
        for block in range(blocks):
            plan, joins, _ = eliminate(load_x_cells(coef, 0, block, x_cells, blocks), half_x)
            from_a, from_b = responses(plan, joins, count)
            store_cells(x_a.at[kind, block], from_a)
            store_cells(x_b.at[kind, block], from_b)
            for f in range(FIELDS):
                if KIND[f] == kind:
                    sources = load_x_cells(fields, f, block, x_cells, blocks)
                    store_cells(inner.at[f, block], inside(plan, joins, count, sources))
        load_turned(coef, 0, x_cells, blocks, turned)
        coefs = load_cells(turned, y_count)
        plan, joins, chain = eliminate(coefs, half_y)
        for i, value in enumerate(coef_rows(coefs, chain)):
            y_rows[kind * COEF_ROWS + i : kind * COEF_ROWS + i + 1, :] = value
        for out, values in zip((y_a, y_b), responses(plan, joins, y_count)):
            store_cells(result, values)
            for block in range(blocks):
                out[kind, block] = result[pl.ds(block * LANES, LANES), :].T


def x_join_kernel(
    half, axis, ranks, rows, y_ranks, y_rows_count,
    received, inner, x_a, x_b, y_a, y_b, y_rows, swept, message, turned, line,
):
    blocks, x_cells = inner.shape[1:3]
    rank = lax.axis_index(axis)
    rotate(received, turned, ranks, rows, rank)
    for block in range(blocks):
        ends = solve_ring(
            lambda q: turned[pl.ds(q * blocks + block, ranks, stride=rows), :], ranks, rank, half
        )
        for f in range(FIELDS):
            end_a, end_b = ends[f]
            swept[f, block] = inner[f, block] + x_a[KIND[f], block] * end_a[:1] + x_b[KIND[f], block] * end_b[:1]
    line[...] = y_rows[...]
    diagonal = row_index(x_cells) == lax.broadcasted_iota(jnp.int32, (x_cells, LANES), 1)
    for f in range(FIELDS):
        for end, weights in enumerate((y_a, y_b)):
            total = sum(weights[KIND[f], block] * swept[f, block] for block in range(blocks))
            sums = jnp.sum(total, axis=1, keepdims=True)
            at = 2 * COEF_ROWS + 2 * f + end
            line[at : at + 1, :] = jnp.sum(jnp.where(diagonal, sums, 0.0), axis=0, keepdims=True)
    for k in range(y_ranks):
        message[pl.ds(k * y_rows_count, y_rows_count), :] = line[...]


def y_inside_kernel(half, swept, viscosity, diffusivity, inner, turned, result):
    blocks, x_cells = swept.shape[1:3]
    count = blocks * LANES // SUB
    for kind, coef in enumerate((viscosity, diffusivity)):
        load_turned(coef, 0, x_cells, blocks, turned)
        plan, joins, _ = eliminate(load_cells(turned, count), half)
        for f in range(FIELDS):
            if KIND[f] == kind:
                for block in range(blocks):
                    turned[pl.ds(block * LANES, LANES), :] = swept[f, block].T
                store_cells(result, inside(plan, joins, count, load_cells(turned, count)))
                for block in range(blocks):
                    inner[f, block] = result[pl.ds(block * LANES, LANES), :].T


def y_join_kernel(half, axis, ranks, rows, received, inner, y_a, y_b, updated, turned):
    blocks, x_cells = inner.shape[1:3]
    rank = lax.axis_index(axis)
    rotate(received, turned, ranks, rows, rank)
    ends = solve_ring(lambda q: turned[pl.ds(q, ranks, stride=rows), :], ranks, rank, half)
    for f in range(FIELDS):
        end_a, end_b = [jnp.broadcast_to(e[:1], (x_cells, LANES)).T for e in ends[f]]
        for block in range(blocks):
            value = inner[f, block] + y_a[KIND[f], block] * end_a + y_b[KIND[f], block] * end_b
            for i in range(x_cells // SUB):
                updated[pl.ds(tile_at(f, i, block, x_cells, blocks), SUB), :] = value[i * SUB : (i + 1) * SUB]


def call(kernel, outs, scratch, name):
    return pl.pallas_call(
        kernel,
        out_shape=[jax.ShapeDtypeStruct(s, jnp.float32) for s in outs],
        scratch_shapes=[pltpu.VMEM(s, jnp.float32) for s in scratch],
        compiler_params=pltpu.CompilerParams(vmem_limit_bytes=24 * 1024 * 1024),
        name=name,
    )


def padded(rows):
    return -(-rows // SUB) * SUB


def on_device(x_ranks, y_ranks, fields, viscosity, diffusivity):
    _, _, x_cells, y_cells = fields.shape
    blocks = y_cells // LANES
    half_x, half_y = 0.5 * float(x_cells * x_cells), 0.5 * float(y_cells * y_cells)
    x_rows, y_rows = padded(QUANTITIES * blocks), padded(QUANTITIES)
    block, pairs, turned = (FIELDS, blocks, x_cells, LANES), (2, blocks, x_cells, LANES), (y_cells, x_cells)
    args = [tiles(a) for a in (fields, viscosity, diffusivity)]

    (message,) = call(
        functools.partial(x_ends_kernel, half_x, x_cells, blocks, x_ranks, x_rows),
        [(x_ranks * x_rows, LANES)], [(x_rows, LANES)], "x_ends",
    )(*args)
    received = lax.all_to_all(message.reshape(x_ranks, x_rows, LANES), "gx", 0, 0, tiled=True)
    inner, x_a, x_b, y_a, y_b, y_coefs = call(
        functools.partial(local_kernel, half_x, half_y, x_cells, blocks),
        [block, pairs, pairs, pairs, pairs, (y_rows, LANES)], [turned, turned], "local",
    )(*args)
    swept, message = call(
        functools.partial(x_join_kernel, half_x, "gx", x_ranks, x_rows, y_ranks, y_rows),
        [block, (y_ranks * y_rows, LANES)],
        [(x_ranks * x_rows, LANES), (y_rows, LANES)], "x_join",
    )(received.reshape(x_ranks * x_rows, LANES), inner, x_a, x_b, y_a, y_b, y_coefs)
    received = lax.all_to_all(message.reshape(y_ranks, y_rows, LANES), "gy", 0, 0, tiled=True)
    (inner,) = call(functools.partial(y_inside_kernel, half_y), [block], [turned, turned], "y_inside")(swept, *args[1:])
    (updated,) = call(
        functools.partial(y_join_kernel, half_y, "gy", y_ranks, y_rows),
        [(FIELDS * x_cells * blocks, LANES)], [(y_ranks * y_rows, LANES)], "y_join",
    )(received.reshape(y_ranks * y_rows, LANES), inner, y_a, y_b)
    return untiles(updated, fields.shape)


def solution(mesh):
    placed = (P(None, None, "gx", "gy"), P(None, "gx", "gy"), P(None, "gx", "gy"))
    return jax.shard_map(
        functools.partial(on_device, mesh.shape["gx"], mesh.shape["gy"]),
        mesh=mesh, in_specs=placed, out_specs=P(None, None, "gx", "gy"), check_vma=False,
    )
```

```python
import functools

import jax
import jax.numpy as jnp
from jax import lax
from jax.experimental import pallas as pl
from jax.experimental.pallas import tpu as pltpu
from jax.sharding import PartitionSpec as P


FIELDS = 4
KIND = (0, 0, 0, 1)
LANES = 128
SUB = 8
COEF_ROWS = 5
QUANTITIES = 2 * COEF_ROWS + 2 * FIELDS


def recip(value):
    guess = pl.reciprocal(value, approx=True)
    return guess * (2.0 - value * guess)


def up(rows, step):
    step %= rows.shape[0]
    return pltpu.roll(rows, rows.shape[0] - step, 0) if step else rows


def down(rows, step):
    return pltpu.roll(rows, step, 0)


def row_index(rows):
    return lax.broadcasted_iota(jnp.int32, (rows, LANES), 0)


def pair(left, ground_u, link, ground_v, right):
    total_u, total_v = left + ground_u, right + ground_v
    scale = recip(total_u * total_v + link * (total_u + total_v))
    return (total_v + link) * scale, link * scale, (total_u + link) * scale


def join(link, ground_a, ground_b, face, shift):
    right, ground_v = up(link, shift), up(ground_a, shift)
    uu, uv, vv = pair(link, ground_b, face, ground_v, right)
    u_left, v_left, u_right, v_right = link * uu, link * uv, right * uv, right * vv
    joined = (
        v_left * right,
        ground_a + ground_b * u_left + ground_v * v_left,
        up(ground_b, shift) + ground_b * u_right + ground_v * v_right,
    )
    return joined, (uu, uv, vv, u_left, v_left, u_right, v_right)


def join_sources(source_a, source_b, weights, shift):
    _, _, _, u_left, v_left, u_right, v_right = weights
    source_v = up(source_a, shift)
    return (
        source_a + source_b * u_left + source_v * v_left,
        up(source_b, shift) + source_b * u_right + source_v * v_right,
    )


def eliminate(coefs, half):
    count = len(coefs)
    ground = [1.0] * count
    links = [half * (coefs[i] + coefs[i + 1]) for i in range(count - 1)]
    nodes, plan = list(range(count)), []
    while len(nodes) > 2:
        kept, kept_links, i = [nodes[0]], [], 1
        while i <= len(nodes) - 2:
            low, cell, high = kept[-1], nodes[i], nodes[i + 1]
            scale = recip(links[i - 1] + links[i] + ground[cell])
            to_low, to_high = links[i - 1] * scale, links[i] * scale
            ground[low] = ground[low] + to_low * ground[cell]
            ground[high] = ground[high] + to_high * ground[cell]
            kept.append(high)
            kept_links.append(to_low * links[i])
            plan.append((cell, low, high, scale, to_low, to_high))
            i += 2
        if i == len(nodes) - 1:
            kept.append(nodes[i])
            kept_links.append(links[i - 1])
        nodes, links = kept, kept_links
    face = half * (coefs[-1] + up(coefs[0], 1))
    chain, joins = (links[0], ground[0], ground[-1]), []
    for shift in (1, 2, 4):
        chain, weights = join(*chain, up(face, shift - 1), shift)
        joins.append((shift, weights))
    return plan, joins, chain


def push_sources(plan, joins, sources):
    sources = list(sources)
    for cell, low, high, _, to_low, to_high in plan:
        sources[low] = sources[low] + to_low * sources[cell]
        sources[high] = sources[high] + to_high * sources[cell]
    ends, history = (sources[0], sources[-1]), []
    for shift, weights in joins:
        history.append(ends)
        ends = join_sources(*ends, weights, shift)
    return sources, history, ends


def pull_values(plan, joins, count, end_a, end_b, sources=None, history=None):
    row = row_index(SUB)
    for index in reversed(range(len(joins))):
        shift, (uu, uv, vv, u_left, v_left, u_right, v_right) = joins[index]
        value_u = u_left * end_a + u_right * end_b
        value_v = v_left * end_a + v_right * end_b
        if history is not None:
            source_u, source_v = history[index][1], up(history[index][0], shift)
            value_u = value_u + uu * source_u + uv * source_v
            value_v = value_v + uv * source_u + vv * source_v
        on_right = (row // shift) % 2 == 1
        end_a = jnp.where(on_right, down(value_v, shift), end_a)
        end_b = jnp.where(on_right, down(end_b, shift), value_u)
    values = [None] * count
    values[0], values[-1] = end_a, end_b
    for cell, low, high, scale, to_low, to_high in reversed(plan):
        value = to_low * values[low] + to_high * values[high]
        values[cell] = value if sources is None else value + scale * sources[cell]
    return values


def responses(plan, joins, count):
    one = jnp.ones((SUB, LANES), jnp.float32)
    zero = jnp.zeros((SUB, LANES), jnp.float32)
    return (
        pull_values(plan, joins, count, one, zero),
        pull_values(plan, joins, count, zero, one),
    )


def inside(plan, joins, count, sources):
    zero = jnp.zeros((SUB, LANES), jnp.float32)
    pushed, history, _ = push_sources(plan, joins, sources)
    return pull_values(plan, joins, count, zero, zero, pushed, history)


def load_cells(ref, count):
    return [ref[pl.ds(t, SUB, stride=count), :] for t in range(count)]


def store_cells(ref, values):
    for t, value in enumerate(values):
        ref[pl.ds(t, SUB, stride=len(values)), :] = value


def tiles(array):
    x_cells, y_cells = array.shape[-2:]
    split = array.reshape(-1, x_cells // SUB, SUB, y_cells // LANES, LANES)
    return split.transpose(0, 1, 3, 2, 4).reshape(-1, LANES)


def untiles(flat, shape):
    split = flat.reshape(-1, shape[-2] // SUB, shape[-1] // LANES, SUB, LANES)
    return split.transpose(0, 1, 3, 2, 4).reshape(shape)


def tile_at(field, x_tile, block, x_cells, blocks):
    return ((field * (x_cells // SUB) + x_tile) * blocks + block) * SUB


def load_x_cells(ref, field, block, x_cells, blocks):
    count = x_cells // SUB
    return [
        ref[pl.ds(tile_at(field, t // SUB, block, x_cells, blocks) + t % SUB, SUB, stride=count * blocks), :]
        for t in range(count)
    ]


def load_block(ref, field, block, x_cells, blocks):
    return jnp.concatenate(
        [ref[pl.ds(tile_at(field, i, block, x_cells, blocks), SUB), :] for i in range(x_cells // SUB)]
    )


def load_turned(ref, field, x_cells, blocks, turned):
    for block in range(blocks):
        turned[pl.ds(block * LANES, LANES), :] = load_block(ref, field, block, x_cells, blocks).T


def solve_ring(quantity, ranks, rank, half):
    row = row_index(ranks)
    device = lax.rem(row + (rank + 1), ranks)
    first, last = device == 0, device == ranks - 1
    results = []
    for kind in range(2):
        first_coef, last_coef, link, ground_a, ground_b = [
            quantity(kind * COEF_ROWS + i) for i in range(COEF_ROWS)
        ]
        ground_a = ground_a + jnp.where(first, half * first_coef, 0.0)
        ground_b = ground_b + jnp.where(last, half * last_coef, 0.0)
        face = jnp.where(last, 0.0, half * (last_coef + up(first_coef, 1)))
        own = [up(x, ranks - 1) for x in (link, ground_a, ground_b)]
        left, right = up(face, ranks - 1), up(face, ranks - 2)
        fields = [f for f in range(FIELDS) if KIND[f] == kind]
        sources = [
            (quantity(2 * COEF_ROWS + 2 * f), quantity(2 * COEF_ROWS + 2 * f + 1)) for f in fields
        ]
        own_sources = [[up(x, ranks - 1) for x in pair_] for pair_ in sources]
        chain, shift = (link, ground_a, ground_b), 1
        while shift < ranks:
            joined, weights = join(*chain, up(face, shift - 1), shift)
            joined_sources = [join_sources(*s, weights, shift) for s in sources]
            if shift == 1:
                alone = row == ranks - 2
                joined = [jnp.where(alone, a, b) for a, b in zip(chain, joined)]
                joined_sources = [
                    [jnp.where(alone, a, b) for a, b in zip(old, new)]
                    for old, new in zip(sources, joined_sources)
                ]
            chain, sources, shift = joined, joined_sources, 2 * shift
        link, ground_u, ground_v = chain
        uu, uv, vv = pair(left, ground_u, link, ground_v, right)
        u_b, v_b, u_a, v_a = left * uu, left * uv, right * uv, right * vv
        link = own[0] + v_b * right
        ground_a = own[1] + ground_u * u_a + ground_v * v_a
        ground_b = own[2] + ground_u * u_b + ground_v * v_b
        scale = recip(ground_a * ground_b + link * (ground_a + ground_b))
        aa, ab, bb = (ground_b + link) * scale, link * scale, (ground_a + link) * scale
        for (source_u, source_v), (source_a, source_b) in zip(sources, own_sources):
            source_a = source_a + source_u * u_a + source_v * v_a
            source_b = source_b + source_u * u_b + source_v * v_b
            results.append((aa * source_a + ab * source_b, ab * source_a + bb * source_b))
    return results


def rotate(received, turned, ranks, rows, rank):
    for k in range(ranks):
        source = pl.multiple_of(lax.rem(rank + 1 + k, ranks) * rows, SUB)
        turned[pl.ds(k * rows, rows), :] = received[pl.ds(source, rows), :]


def coef_rows(coefs, chain):
    return (coefs[0][:1], coefs[-1][SUB - 1 :], chain[0][:1], chain[1][:1], chain[2][:1])


def x_ends_kernel(
    half, x_cells, blocks, ranks, rows,
    fields, viscosity, diffusivity, message, line, fields_here, viscosity_here, diffusivity_here, arrived,
):
    per_field = x_cells * blocks
    copies = [
        pltpu.make_async_copy(viscosity, viscosity_here, arrived.at[0]),
        pltpu.make_async_copy(diffusivity, diffusivity_here, arrived.at[1]),
    ]
    for f in range(FIELDS):
        part = pl.ds(f * per_field, per_field)
        copies.append(pltpu.make_async_copy(fields.at[part], fields_here.at[part], arrived.at[2 + f]))
    for copy in copies:
        copy.start()
    line[...] = jnp.zeros_like(line)

    def put(quantity, block, value):
        at = quantity * blocks + block
        line[at : at + 1, :] = value

    plans = {}
    for kind, coef in enumerate((viscosity_here, diffusivity_here)):
        copies[kind].wait()
        for block in range(blocks):
            coefs = load_x_cells(coef, 0, block, x_cells, blocks)
            plan, joins, chain = eliminate(coefs, half)
            plans[kind, block] = plan, joins
            for i, value in enumerate(coef_rows(coefs, chain)):
                put(kind * COEF_ROWS + i, block, value)
    for f in range(FIELDS):
        copies[2 + f].wait()
        for block in range(blocks):
            sources = load_x_cells(fields_here, f, block, x_cells, blocks)
            _, _, ends = push_sources(*plans[KIND[f], block], sources)
            put(2 * COEF_ROWS + 2 * f, block, ends[0][:1])
            put(2 * COEF_ROWS + 2 * f + 1, block, ends[1][:1])
    for k in range(ranks):
        message[pl.ds(k * rows, rows), :] = line[...]


def local_kernel(
    half_x, half_y, x_cells, blocks,
    fields, viscosity, diffusivity, inner, x_a, x_b, y_a, y_b, y_rows, turned, result,
):
    count, y_count = x_cells // SUB, blocks * LANES // SUB
    y_rows[...] = jnp.zeros_like(y_rows)
    for kind, coef in enumerate((viscosity, diffusivity)):
        for block in range(blocks):
            plan, joins, _ = eliminate(load_x_cells(coef, 0, block, x_cells, blocks), half_x)
            from_a, from_b = responses(plan, joins, count)
            store_cells(x_a.at[kind, block], from_a)
            store_cells(x_b.at[kind, block], from_b)
            for f in range(FIELDS):
                if KIND[f] == kind:
                    sources = load_x_cells(fields, f, block, x_cells, blocks)
                    store_cells(inner.at[f, block], inside(plan, joins, count, sources))
        load_turned(coef, 0, x_cells, blocks, turned)
        coefs = load_cells(turned, y_count)
        plan, joins, chain = eliminate(coefs, half_y)
        for i, value in enumerate(coef_rows(coefs, chain)):
            y_rows[kind * COEF_ROWS + i : kind * COEF_ROWS + i + 1, :] = value
        for out, values in zip((y_a, y_b), responses(plan, joins, y_count)):
            store_cells(result, values)
            for block in range(blocks):
                out[kind, block] = result[pl.ds(block * LANES, LANES), :].T


def x_join_kernel(
    half, axis, ranks, rows, y_ranks, y_rows_count,
    received, inner, x_a, x_b, y_a, y_b, y_rows, swept, message, turned, line,
):
    blocks, x_cells = inner.shape[1:3]
    rank = lax.axis_index(axis)
    rotate(received, turned, ranks, rows, rank)
    for block in range(blocks):
        ends = solve_ring(
            lambda q: turned[pl.ds(q * blocks + block, ranks, stride=rows), :], ranks, rank, half
        )
        for f in range(FIELDS):
            end_a, end_b = ends[f]
            swept[f, block] = inner[f, block] + x_a[KIND[f], block] * end_a[:1] + x_b[KIND[f], block] * end_b[:1]
    line[...] = y_rows[...]
    diagonal = row_index(x_cells) == lax.broadcasted_iota(jnp.int32, (x_cells, LANES), 1)
    for f in range(FIELDS):
        for end, weights in enumerate((y_a, y_b)):
            total = sum(weights[KIND[f], block] * swept[f, block] for block in range(blocks))
            sums = jnp.sum(total, axis=1, keepdims=True)
            at = 2 * COEF_ROWS + 2 * f + end
            line[at : at + 1, :] = jnp.sum(jnp.where(diagonal, sums, 0.0), axis=0, keepdims=True)
    for k in range(y_ranks):
        message[pl.ds(k * y_rows_count, y_rows_count), :] = line[...]


def y_inside_kernel(half, swept, viscosity, diffusivity, inner, turned, result):
    blocks, x_cells = swept.shape[1:3]
    count = blocks * LANES // SUB
    for kind, coef in enumerate((viscosity, diffusivity)):
        load_turned(coef, 0, x_cells, blocks, turned)
        plan, joins, _ = eliminate(load_cells(turned, count), half)
        for f in range(FIELDS):
            if KIND[f] == kind:
                for block in range(blocks):
                    turned[pl.ds(block * LANES, LANES), :] = swept[f, block].T
                store_cells(result, inside(plan, joins, count, load_cells(turned, count)))
                for block in range(blocks):
                    inner[f, block] = result[pl.ds(block * LANES, LANES), :].T


def y_join_kernel(half, axis, ranks, rows, received, inner, y_a, y_b, updated, turned, here, left):
    blocks, x_cells = inner.shape[1:3]
    per_field = x_cells * blocks
    rank = lax.axis_index(axis)
    rotate(received, turned, ranks, rows, rank)
    ends = solve_ring(lambda q: turned[pl.ds(q, ranks, stride=rows), :], ranks, rank, half)
    copies = []
    for f in range(FIELDS):
        end_a, end_b = [jnp.broadcast_to(e[:1], (x_cells, LANES)).T for e in ends[f]]
        for block in range(blocks):
            value = inner[f, block] + y_a[KIND[f], block] * end_a + y_b[KIND[f], block] * end_b
            for i in range(x_cells // SUB):
                here[pl.ds(tile_at(f, i, block, x_cells, blocks), SUB), :] = value[i * SUB : (i + 1) * SUB]
        part = pl.ds(f * per_field, per_field)
        copies.append(pltpu.make_async_copy(here.at[part], updated.at[part], left.at[f]))
        copies[-1].start()
    for copy in copies:
        copy.wait()


def call(kernel, outs, scratch, name, **kw):
    return pl.pallas_call(
        kernel,
        out_shape=outs,
        scratch_shapes=[pltpu.VMEM(s, jnp.float32) if isinstance(s, tuple) else s for s in scratch],
        compiler_params=pltpu.CompilerParams(vmem_limit_bytes=24 * 1024 * 1024),
        name=name,
        **kw,
    )


def near(shape):
    return pltpu.VMEM(shape, jnp.float32)


def far(shape):
    return pltpu.HBM(shape, jnp.float32)


def padded(rows):
    return -(-rows // SUB) * SUB


def on_device(x_ranks, y_ranks, fields, viscosity, diffusivity):
    _, _, x_cells, y_cells = fields.shape
    blocks = y_cells // LANES
    half_x, half_y = 0.5 * float(x_cells * x_cells), 0.5 * float(y_cells * y_cells)
    x_rows, y_rows = padded(QUANTITIES * blocks), padded(QUANTITIES)
    block, pairs, turned = (FIELDS, blocks, x_cells, LANES), (2, blocks, x_cells, LANES), (y_cells, x_cells)
    args = [tiles(a) for a in (fields, viscosity, diffusivity)]

    sizes = [a.shape for a in args]
    in_hbm = [pltpu.with_memory_space_constraint(a, pltpu.HBM) for a in args]

    (message,) = call(
        functools.partial(x_ends_kernel, half_x, x_cells, blocks, x_ranks, x_rows),
        [near((x_ranks * x_rows, LANES))],
        [(x_rows, LANES), *sizes, pltpu.SemaphoreType.DMA((2 + FIELDS,))], "x_ends",
        in_specs=[pl.BlockSpec(memory_space=pltpu.HBM)] * 3,
    )(*in_hbm)
    received = lax.all_to_all(message.reshape(x_ranks, x_rows, LANES), "gx", 0, 0, tiled=True)
    inner, x_a, x_b, y_a, y_b, y_coefs = call(
        functools.partial(local_kernel, half_x, half_y, x_cells, blocks),
        [near(s) for s in (block, pairs, pairs, pairs, pairs, (y_rows, LANES))], [turned, turned], "local",
    )(*args)
    swept, message = call(
        functools.partial(x_join_kernel, half_x, "gx", x_ranks, x_rows, y_ranks, y_rows),
        [near(block), near((y_ranks * y_rows, LANES))],
        [(x_ranks * x_rows, LANES), (y_rows, LANES)], "x_join",
    )(received.reshape(x_ranks * x_rows, LANES), inner, x_a, x_b, y_a, y_b, y_coefs)
    received = lax.all_to_all(message.reshape(y_ranks, y_rows, LANES), "gy", 0, 0, tiled=True)
    (inner,) = call(
        functools.partial(y_inside_kernel, half_y), [near(block)], [turned, turned], "y_inside"
    )(swept, *args[1:])
    (updated,) = call(
        functools.partial(y_join_kernel, half_y, "gy", y_ranks, y_rows),
        [far(sizes[0])],
        [(y_ranks * y_rows, LANES), sizes[0], pltpu.SemaphoreType.DMA((FIELDS,))], "y_join",
        out_specs=[pl.BlockSpec(memory_space=pltpu.HBM)],
    )(received.reshape(y_ranks * y_rows, LANES), inner, y_a, y_b)
    return untiles(updated, fields.shape)


def solution(mesh):
    placed = (P(None, None, "gx", "gy"), P(None, "gx", "gy"), P(None, "gx", "gy"))
    return jax.shard_map(
        functools.partial(on_device, mesh.shape["gx"], mesh.shape["gy"]),
        mesh=mesh, in_specs=placed, out_specs=P(None, None, "gx", "gy"), check_vma=False,
    )
```

```python
import functools

import jax
import jax.numpy as jnp
from jax import lax
from jax.experimental import pallas as pl
from jax.experimental.pallas import tpu as pltpu
from jax.sharding import PartitionSpec as P


FIELDS = 4
KIND = (0, 0, 0, 1)
LANES = 128
SUB = 8
COEF_ROWS = 5
QUANTITIES = 2 * COEF_ROWS + 2 * FIELDS


def recip(value):
    guess = pl.reciprocal(value, approx=True)
    return guess * (2.0 - value * guess)


def up(rows, step):
    step %= rows.shape[0]
    return pltpu.roll(rows, rows.shape[0] - step, 0) if step else rows


def down(rows, step):
    return pltpu.roll(rows, step, 0)


def row_index(rows):
    return lax.broadcasted_iota(jnp.int32, (rows, LANES), 0)


def pair(left, ground_u, link, ground_v, right):
    total_u, total_v = left + ground_u, right + ground_v
    scale = recip(total_u * total_v + link * (total_u + total_v))
    return (total_v + link) * scale, link * scale, (total_u + link) * scale


def join(link, ground_a, ground_b, face, shift):
    right, ground_v = up(link, shift), up(ground_a, shift)
    uu, uv, vv = pair(link, ground_b, face, ground_v, right)
    u_left, v_left, u_right, v_right = link * uu, link * uv, right * uv, right * vv
    joined = (
        v_left * right,
        ground_a + ground_b * u_left + ground_v * v_left,
        up(ground_b, shift) + ground_b * u_right + ground_v * v_right,
    )
    return joined, (uu, uv, vv, u_left, v_left, u_right, v_right)


def join_sources(source_a, source_b, weights, shift):
    _, _, _, u_left, v_left, u_right, v_right = weights
    source_v = up(source_a, shift)
    return (
        source_a + source_b * u_left + source_v * v_left,
        up(source_b, shift) + source_b * u_right + source_v * v_right,
    )


def schedule(count):
    nodes, rounds = list(range(count)), []
    while len(nodes) > 2:
        gone = range(1, len(nodes) - 1, 2)
        rounds.append([(nodes[i], nodes[i - 1], nodes[i + 1]) for i in gone])
        nodes = [n for i, n in enumerate(nodes) if i not in gone]
    return rounds


SHIFTS = (1, 2, 4)


def eliminate(coefs, half):
    count = len(coefs)
    ground = [1.0] * count
    link = {i: half * (coefs[i] + coefs[i + 1]) for i in range(count - 1)}
    cells, scales = {}, {}
    for round_ in schedule(count):
        for cell, low, high in round_:
            scale = recip(link[low] + link[cell] + ground[cell])
            to_low, to_high = link[low] * scale, link[cell] * scale
            ground[low] = ground[low] + to_low * ground[cell]
            ground[high] = ground[high] + to_high * ground[cell]
            link[low] = to_low * link[cell]
            cells[cell], scales[cell] = (to_low, to_high), scale
    face = half * (coefs[-1] + up(coefs[0], 1))
    chain, joins = (link[0], ground[0], ground[-1]), []
    for shift in SHIFTS:
        chain, weights = join(*chain, up(face, shift - 1), shift)
        joins.append(weights)
    return cells, scales, joins, chain


def push_sources(cells, scales, joins, sources):
    sources, scaled = list(sources), {}
    for round_ in schedule(len(sources)):
        for cell, low, high in round_:
            to_low, to_high = cells[cell]
            sources[low] = sources[low] + to_low * sources[cell]
            sources[high] = sources[high] + to_high * sources[cell]
            scaled[cell] = scales[cell] * sources[cell]
    ends, joined = (sources[0], sources[-1]), []
    for shift, weights in zip(SHIFTS, joins):
        uu, uv, vv = weights[:3]
        source_u, source_v = ends[1], up(ends[0], shift)
        joined.append((uu * source_u + uv * source_v, uv * source_u + vv * source_v))
        ends = join_sources(*ends, weights, shift)
    return scaled, joined, ends


def pull_values(cells, joins, scaled, joined, end_a, end_b):
    row = row_index(SUB)
    for shift, (u_left, v_left, u_right, v_right), (from_u, from_v) in reversed(list(zip(SHIFTS, joins, joined))):
        value_u = from_u + u_left * end_a + u_right * end_b
        value_v = from_v + v_left * end_a + v_right * end_b
        on_right = (row // shift) % 2 == 1
        end_a = jnp.where(on_right, down(value_v, shift), end_a)
        end_b = jnp.where(on_right, down(end_b, shift), value_u)
    count = len(cells) + 2
    values = {0: end_a, count - 1: end_b}
    for round_ in reversed(schedule(count)):
        for cell, low, high in round_:
            to_low, to_high = cells[cell]
            values[cell] = scaled[cell] + to_low * values[low] + to_high * values[high]
    return [values[t] for t in range(count)]


def weight_rows(count):
    return (2 * (count - 2) + 4 * len(SHIFTS)) * SUB


def source_rows(count):
    return (count - 2 + 2 * len(SHIFTS)) * SUB


def save(ref, arrays):
    for i, array in enumerate(arrays):
        ref[pl.ds(i * SUB, SUB), :] = array


def save_weights(ref, cells, joins):
    save(ref, [w for c in sorted(cells) for w in cells[c]] + [w for weights in joins for w in weights[3:]])


def save_sources(ref, scaled, joined):
    save(ref, [scaled[c] for c in sorted(scaled)] + [v for two in joined for v in two])


def load_weights(ref, count):
    def at(i):
        return ref[pl.ds(i * SUB, SUB), :]

    base = 2 * (count - 2)
    cells = {c: (at(2 * c - 2), at(2 * c - 1)) for c in range(1, count - 1)}
    return cells, [tuple(at(base + 4 * j + i) for i in range(4)) for j in range(len(SHIFTS))]


def load_sources(ref, count):
    def at(i):
        return ref[pl.ds(i * SUB, SUB), :]

    base = count - 2
    return {c: at(c - 1) for c in range(1, count - 1)}, [
        (at(base + 2 * j), at(base + 2 * j + 1)) for j in range(len(SHIFTS))
    ]


def spread(row):
    return jnp.broadcast_to(row[:1], (SUB, LANES))


def to_cells(rows):
    parts = jnp.swapaxes(rows.reshape(SUB, -1, LANES), 0, 1)
    return [parts[t] for t in range(parts.shape[0])]


def from_cells(cells):
    return jnp.swapaxes(jnp.stack(cells), 0, 1).reshape(-1, LANES)


def tiles(array):
    x_cells, y_cells = array.shape[-2:]
    split = array.reshape(-1, x_cells // SUB, SUB, y_cells // LANES, LANES)
    return split.transpose(0, 1, 3, 2, 4).reshape(-1, LANES)


def untiles(flat, shape):
    split = flat.reshape(-1, shape[-2] // SUB, shape[-1] // LANES, SUB, LANES)
    return split.transpose(0, 1, 3, 2, 4).reshape(shape)


def tile_at(field, x_tile, block, x_cells, blocks):
    return ((field * (x_cells // SUB) + x_tile) * blocks + block) * SUB


def load_x_cells(ref, field, x_cells, blocks):
    parts = to_cells(ref[pl.ds(field * x_cells * blocks, x_cells * blocks), :])
    return [
        [parts[(t // SUB * blocks + block) * SUB + t % SUB] for t in range(x_cells // SUB)] for block in range(blocks)
    ]


def load_block(ref, field, block, x_cells, blocks):
    return jnp.concatenate(
        [ref[pl.ds(tile_at(field, i, block, x_cells, blocks), SUB), :] for i in range(x_cells // SUB)]
    )


def solve_ring(quantity, ranks, rank, half):
    row = row_index(ranks)
    device = lax.rem(row + (rank + 1), ranks)
    first, last = device == 0, device == ranks - 1
    results = []
    for kind in range(2):
        first_coef, last_coef, link, ground_a, ground_b = [
            quantity(kind * COEF_ROWS + i) for i in range(COEF_ROWS)
        ]
        ground_a = ground_a + jnp.where(first, half * first_coef, 0.0)
        ground_b = ground_b + jnp.where(last, half * last_coef, 0.0)
        face = jnp.where(last, 0.0, half * (last_coef + up(first_coef, 1)))
        own = [up(x, ranks - 1) for x in (link, ground_a, ground_b)]
        left, right = up(face, ranks - 1), up(face, ranks - 2)
        fields = [f for f in range(FIELDS) if KIND[f] == kind]
        sources = [
            (quantity(2 * COEF_ROWS + 2 * f), quantity(2 * COEF_ROWS + 2 * f + 1)) for f in fields
        ]
        own_sources = [[up(x, ranks - 1) for x in pair_] for pair_ in sources]
        chain, shift = (link, ground_a, ground_b), 1
        while shift < ranks:
            joined, weights = join(*chain, up(face, shift - 1), shift)
            joined_sources = [join_sources(*s, weights, shift) for s in sources]
            if shift == 1:
                alone = row == ranks - 2
                joined = [jnp.where(alone, a, b) for a, b in zip(chain, joined)]
                joined_sources = [
                    [jnp.where(alone, a, b) for a, b in zip(old, new)]
                    for old, new in zip(sources, joined_sources)
                ]
            chain, sources, shift = joined, joined_sources, 2 * shift
        link, ground_u, ground_v = chain
        uu, uv, vv = pair(left, ground_u, link, ground_v, right)
        u_b, v_b, u_a, v_a = left * uu, left * uv, right * uv, right * vv
        link = own[0] + v_b * right
        ground_a = own[1] + ground_u * u_a + ground_v * v_a
        ground_b = own[2] + ground_u * u_b + ground_v * v_b
        scale = recip(ground_a * ground_b + link * (ground_a + ground_b))
        aa, ab, bb = (ground_b + link) * scale, link * scale, (ground_a + link) * scale
        for (source_u, source_v), (source_a, source_b) in zip(sources, own_sources):
            source_a = source_a + source_u * u_a + source_v * v_a
            source_b = source_b + source_u * u_b + source_v * v_b
            results.append((aa * source_a + ab * source_b, ab * source_a + bb * source_b))
    return results


def rotate(received, turned, ranks, rows, rank):
    for k in range(ranks):
        source = pl.multiple_of(lax.rem(rank + 1 + k, ranks) * rows, SUB)
        turned[pl.ds(k * rows, rows), :] = received[pl.ds(source, rows), :]


def coef_rows(coefs, chain):
    return (coefs[0][:1], coefs[-1][SUB - 1 :], chain[0][:1], chain[1][:1], chain[2][:1])


def x_ends_kernel(
    half, x_cells, blocks, ranks, rows,
    fields, viscosity, diffusivity, message, weights, pushed,
    line, fields_here, viscosity_here, diffusivity_here, arrived,
):
    per_field = x_cells * blocks
    copies = [
        pltpu.make_async_copy(viscosity, viscosity_here, arrived.at[0]),
        pltpu.make_async_copy(diffusivity, diffusivity_here, arrived.at[1]),
    ]
    for f in range(FIELDS):
        part = pl.ds(f * per_field, per_field)
        copies.append(pltpu.make_async_copy(fields.at[part], fields_here.at[part], arrived.at[2 + f]))
    for copy in copies:
        copy.start()
    line[...] = jnp.zeros_like(line)

    def put(quantity, block, value):
        at = quantity * blocks + block
        line[at : at + 1, :] = value

    plans = {}
    for copy in copies[:2]:
        copy.wait()
    for kind, coef in enumerate((viscosity_here, diffusivity_here)):
        for block, coefs in enumerate(load_x_cells(coef, 0, x_cells, blocks)):
            *plan, chain = eliminate(coefs, half)
            plans[kind, block] = plan
            save_weights(weights.at[kind, block], plan[0], plan[2])
            for i, value in enumerate(coef_rows(coefs, chain)):
                put(kind * COEF_ROWS + i, block, value)
    for copy in copies[2:]:
        copy.wait()
    for f in range(FIELDS):
        for block, sources in enumerate(load_x_cells(fields_here, f, x_cells, blocks)):
            scaled, joined, ends = push_sources(*plans[KIND[f], block], sources)
            save_sources(pushed.at[f, block], scaled, joined)
            put(2 * COEF_ROWS + 2 * f, block, ends[0][:1])
            put(2 * COEF_ROWS + 2 * f + 1, block, ends[1][:1])
    for k in range(ranks):
        message[pl.ds(k * rows, rows), :] = line[...]


def x_join_kernel(
    half_x, half_y, x_cells, blocks, axis, ranks, rows, y_ranks, y_rows,
    received, x_weights, x_pushed, viscosity, diffusivity, message, weights, pushed,
    turned, line,
):
    rank = lax.axis_index(axis)
    count, y_count = x_cells // SUB, blocks * LANES // SUB
    rotate(received, turned, ranks, rows, rank)
    line[...] = jnp.zeros_like(line)
    plans = []
    for kind, coef in enumerate((viscosity, diffusivity)):
        coefs = to_cells(jnp.concatenate([load_block(coef, 0, b, x_cells, blocks).T for b in range(blocks)]))
        *plan, chain = eliminate(coefs, half_y)
        plans.append(plan)
        save_weights(weights.at[kind], plan[0], plan[2])
        for i, value in enumerate(coef_rows(coefs, chain)):
            line[kind * COEF_ROWS + i : kind * COEF_ROWS + i + 1, :] = value
    lines = [[] for _ in range(FIELDS)]
    for block in range(blocks):
        ends = solve_ring(
            lambda q: turned[pl.ds(q * blocks + block, ranks, stride=rows), :], ranks, rank, half_x
        )
        for f in range(FIELDS):
            end_a, end_b = [spread(e) for e in ends[f]]
            values = pull_values(
                *load_weights(x_weights.at[KIND[f], block], count), *load_sources(x_pushed.at[f, block], count), end_a, end_b
            )
            lines[f].append(from_cells(values).T)
    for f in range(FIELDS):
        scaled, joined, ends = push_sources(*plans[KIND[f]], to_cells(jnp.concatenate(lines[f])))
        save_sources(pushed.at[f], scaled, joined)
        at = 2 * COEF_ROWS + 2 * f
        line[at : at + 1, :] = ends[0][:1]
        line[at + 1 : at + 2, :] = ends[1][:1]
    for k in range(y_ranks):
        message[pl.ds(k * y_rows, y_rows), :] = line[...]


def y_join_kernel(
    half, x_cells, blocks, axis, ranks, rows,
    received, weights, pushed, updated, turned, here, left,
):
    per_field = x_cells * blocks
    count = blocks * LANES // SUB
    rank = lax.axis_index(axis)
    rotate(received, turned, ranks, rows, rank)
    ends = solve_ring(lambda q: turned[pl.ds(q, ranks, stride=rows), :], ranks, rank, half)
    copies = []
    for f in range(FIELDS):
        end_a, end_b = [spread(e) for e in ends[f]]
        values = pull_values(
            *load_weights(weights.at[KIND[f]], count), *load_sources(pushed.at[f], count), end_a, end_b
        )
        lines = from_cells(values)
        for block in range(blocks):
            value = lines[block * LANES : (block + 1) * LANES].T
            for i in range(x_cells // SUB):
                here[pl.ds(tile_at(f, i, block, x_cells, blocks), SUB), :] = value[i * SUB : (i + 1) * SUB]
        part = pl.ds(f * per_field, per_field)
        copies.append(pltpu.make_async_copy(here.at[part], updated.at[part], left.at[f]))
        copies[-1].start()
    for copy in copies:
        copy.wait()


def call(kernel, outs, scratch, name, **kw):
    return pl.pallas_call(
        kernel,
        out_shape=outs,
        scratch_shapes=[pltpu.VMEM(s, jnp.float32) if isinstance(s, tuple) else s for s in scratch],
        compiler_params=pltpu.CompilerParams(vmem_limit_bytes=24 * 1024 * 1024),
        name=name,
        **kw,
    )


def near(shape):
    return pltpu.VMEM(shape, jnp.float32)


def far(shape):
    return pltpu.HBM(shape, jnp.float32)


def padded(rows):
    return -(-rows // SUB) * SUB


def on_device(x_ranks, y_ranks, fields, viscosity, diffusivity):
    _, _, x_cells, y_cells = fields.shape
    blocks = y_cells // LANES
    half_x, half_y = 0.5 * float(x_cells * x_cells), 0.5 * float(y_cells * y_cells)
    x_rows, y_rows = padded(QUANTITIES * blocks), padded(QUANTITIES)
    x_count, y_count = x_cells // SUB, y_cells // SUB
    args = [tiles(a) for a in (fields, viscosity, diffusivity)]
    sizes = [a.shape for a in args]
    in_hbm = [pltpu.with_memory_space_constraint(a, pltpu.HBM) for a in args]

    message, x_weights, x_pushed = call(
        functools.partial(x_ends_kernel, half_x, x_cells, blocks, x_ranks, x_rows),
        [
            near((x_ranks * x_rows, LANES)),
            near((2, blocks, weight_rows(x_count), LANES)),
            near((FIELDS, blocks, source_rows(x_count), LANES)),
        ],
        [(x_rows, LANES), *sizes, pltpu.SemaphoreType.DMA((2 + FIELDS,))], "x_ends",
        in_specs=[pl.BlockSpec(memory_space=pltpu.HBM)] * 3,
    )(*in_hbm)
    received = lax.all_to_all(message.reshape(x_ranks, x_rows, LANES), "gx", 0, 0, tiled=True)
    message, y_weights, y_pushed = call(
        functools.partial(x_join_kernel, half_x, half_y, x_cells, blocks, "gx", x_ranks, x_rows, y_ranks, y_rows),
        [
            near((y_ranks * y_rows, LANES)),
            near((2, weight_rows(y_count), LANES)),
            near((FIELDS, source_rows(y_count), LANES)),
        ],
        [(x_ranks * x_rows, LANES), (y_rows, LANES)],
        "x_join",
    )(received.reshape(x_ranks * x_rows, LANES), x_weights, x_pushed, *args[1:])
    received = lax.all_to_all(message.reshape(y_ranks, y_rows, LANES), "gy", 0, 0, tiled=True)
    (updated,) = call(
        functools.partial(y_join_kernel, half_y, x_cells, blocks, "gy", y_ranks, y_rows),
        [far(sizes[0])],
        [(y_ranks * y_rows, LANES), sizes[0], pltpu.SemaphoreType.DMA((FIELDS,))], "y_join",
        out_specs=[pl.BlockSpec(memory_space=pltpu.HBM)],
    )(received.reshape(y_ranks * y_rows, LANES), y_weights, y_pushed)
    return untiles(updated, fields.shape)


def solution(mesh):
    placed = (P(None, None, "gx", "gy"), P(None, "gx", "gy"), P(None, "gx", "gy"))
    return jax.shard_map(
        functools.partial(on_device, mesh.shape["gx"], mesh.shape["gy"]),
        mesh=mesh, in_specs=placed, out_specs=P(None, None, "gx", "gy"), check_vma=False,
    )
```

```python
import functools

import jax
import jax.numpy as jnp
from jax import lax
from jax.experimental import pallas as pl
from jax.experimental.pallas import tpu as pltpu
from jax.sharding import PartitionSpec as P


FIELDS = 4
KIND = (0, 0, 0, 1)
LANES = 128
SUB = 8
COEF_ROWS = 5
QUANTITIES = 2 * COEF_ROWS + 2 * FIELDS


def recip(value):
    guess = pl.reciprocal(value, approx=True)
    return guess * (2.0 - value * guess)


def up(rows, step):
    step %= rows.shape[0]
    return pltpu.roll(rows, rows.shape[0] - step, 0) if step else rows


def down(rows, step):
    return pltpu.roll(rows, step, 0)


def row_index(rows):
    return lax.broadcasted_iota(jnp.int32, (rows, LANES), 0)


def pair(left, ground_u, link, ground_v, right):
    total_u, total_v = left + ground_u, right + ground_v
    scale = recip(total_u * total_v + link * (total_u + total_v))
    return (total_v + link) * scale, link * scale, (total_u + link) * scale


def join_two(low, face, high):
    link, ground_a, ground_u = low
    right, ground_v, ground_b = high
    uu, uv, vv = pair(link, ground_u, face, ground_v, right)
    u_left, v_left, u_right, v_right = link * uu, link * uv, right * uv, right * vv
    joined = (
        v_left * right,
        ground_a + ground_u * u_left + ground_v * v_left,
        ground_b + ground_u * u_right + ground_v * v_right,
    )
    return joined, (uu, uv, vv, u_left, v_left, u_right, v_right)


def join_two_sources(low, weights, high):
    _, _, _, u_left, v_left, u_right, v_right = weights
    (source_a, source_u), (source_v, source_b) = low, high
    return (
        source_a + source_u * u_left + source_v * v_left,
        source_b + source_u * u_right + source_v * v_right,
    )


def shifted(arrays, shift):
    return [up(x, shift) for x in arrays]


def join(chain, face, shift):
    return join_two(chain, face, shifted(chain, shift))


def join_sources(ends, weights, shift):
    return join_two_sources(ends, weights, shifted(ends, shift))


def schedule(count):
    nodes, rounds = list(range(count)), []
    while len(nodes) > 2:
        gone = range(1, len(nodes) - 1, 2)
        rounds.append([(nodes[i], nodes[i - 1], nodes[i + 1]) for i in gone])
        nodes = [n for i, n in enumerate(nodes) if i not in gone]
    return rounds


SHIFTS = (1, 2, 4)


def eliminate(coefs, half):
    count = len(coefs)
    ground = [1.0] * count
    link = {i: half * (coefs[i] + coefs[i + 1]) for i in range(count - 1)}
    cells, scales = {}, {}
    for round_ in schedule(count):
        for cell, low, high in round_:
            scale = recip(link[low] + link[cell] + ground[cell])
            to_low, to_high = link[low] * scale, link[cell] * scale
            ground[low] = ground[low] + to_low * ground[cell]
            ground[high] = ground[high] + to_high * ground[cell]
            link[low] = to_low * link[cell]
            cells[cell], scales[cell] = (to_low, to_high), scale
    face = half * (coefs[-1] + up(coefs[0], 1))
    chain, joins = (link[0], ground[0], ground[-1]), []
    for shift in SHIFTS:
        chain, weights = join(chain, up(face, shift - 1), shift)
        joins.append(weights)
    return cells, scales, joins, chain


def push_sources(cells, scales, joins, sources):
    sources, scaled = list(sources), {}
    for round_ in schedule(len(sources)):
        for cell, low, high in round_:
            to_low, to_high = cells[cell]
            sources[low] = sources[low] + to_low * sources[cell]
            sources[high] = sources[high] + to_high * sources[cell]
            scaled[cell] = scales[cell] * sources[cell]
    ends, joined = (sources[0], sources[-1]), []
    for shift, weights in zip(SHIFTS, joins):
        uu, uv, vv = weights[:3]
        source_u, source_v = ends[1], up(ends[0], shift)
        joined.append((uu * source_u + uv * source_v, uv * source_u + vv * source_v))
        ends = join_sources(ends, weights, shift)
    return scaled, joined, ends


def pull_values(cells, joins, scaled, joined, end_a, end_b):
    row = row_index(SUB)
    for shift, (u_left, v_left, u_right, v_right), (from_u, from_v) in reversed(list(zip(SHIFTS, joins, joined))):
        value_u = from_u + u_left * end_a + u_right * end_b
        value_v = from_v + v_left * end_a + v_right * end_b
        on_right = (row // shift) % 2 == 1
        end_a = jnp.where(on_right, down(value_v, shift), end_a)
        end_b = jnp.where(on_right, down(end_b, shift), value_u)
    count = len(cells) + 2
    values = {0: end_a, count - 1: end_b}
    for round_ in reversed(schedule(count)):
        for cell, low, high in round_:
            to_low, to_high = cells[cell]
            values[cell] = scaled[cell] + to_low * values[low] + to_high * values[high]
    return [values[t] for t in range(count)]


def weight_rows(count):
    return (2 * (count - 2) + 4 * len(SHIFTS)) * SUB


def source_rows(count):
    return (count - 2 + 2 * len(SHIFTS)) * SUB


def save(ref, arrays):
    for i, array in enumerate(arrays):
        ref[pl.ds(i * SUB, SUB), :] = array


def save_weights(ref, cells, joins):
    save(ref, [w for c in sorted(cells) for w in cells[c]] + [w for weights in joins for w in weights[3:]])


def save_sources(ref, scaled, joined):
    save(ref, [scaled[c] for c in sorted(scaled)] + [v for two in joined for v in two])


def load_weights(ref, count):
    def at(i):
        return ref[pl.ds(i * SUB, SUB), :]

    base = 2 * (count - 2)
    cells = {c: (at(2 * c - 2), at(2 * c - 1)) for c in range(1, count - 1)}
    return cells, [tuple(at(base + 4 * j + i) for i in range(4)) for j in range(len(SHIFTS))]


def load_sources(ref, count):
    def at(i):
        return ref[pl.ds(i * SUB, SUB), :]

    base = count - 2
    return {c: at(c - 1) for c in range(1, count - 1)}, [
        (at(base + 2 * j), at(base + 2 * j + 1)) for j in range(len(SHIFTS))
    ]


def spread(row):
    return jnp.broadcast_to(row[:1], (SUB, LANES))


def to_cells(rows):
    parts = jnp.swapaxes(rows.reshape(SUB, -1, LANES), 0, 1)
    return [parts[t] for t in range(parts.shape[0])]


def from_cells(cells):
    return jnp.swapaxes(jnp.stack(cells), 0, 1).reshape(-1, LANES)


def tiles(array):
    x_cells, y_cells = array.shape[-2:]
    split = array.reshape(-1, x_cells // SUB, SUB, y_cells // LANES, LANES)
    return split.transpose(0, 1, 3, 2, 4).reshape(-1, LANES)


def untiles(flat, shape):
    split = flat.reshape(-1, shape[-2] // SUB, shape[-1] // LANES, SUB, LANES)
    return split.transpose(0, 1, 3, 2, 4).reshape(shape)


def tile_at(field, x_tile, block, x_cells, blocks):
    return ((field * (x_cells // SUB) + x_tile) * blocks + block) * SUB


def load_x_cells(ref, field, x_cells, blocks):
    parts = to_cells(ref[pl.ds(field * x_cells * blocks, x_cells * blocks), :])
    return [
        [parts[(t // SUB * blocks + block) * SUB + t % SUB] for t in range(x_cells // SUB)] for block in range(blocks)
    ]


def load_block(ref, field, block, x_cells, blocks):
    return jnp.concatenate(
        [ref[pl.ds(tile_at(field, i, block, x_cells, blocks), SUB), :] for i in range(x_cells // SUB)]
    )


def solve_ring(quantity, ranks, rank, half):
    step = max(1, ranks // SUB)
    count = ranks // step
    device = [lax.rem(row_index(count) * step + (rank + 1 + k), ranks) for k in range(step)]
    last_row = row_index(count) == count - 1
    results = []
    for kind in range(2):
        chains, sources, first_coefs, last_coefs = [], [], [], []
        fields = [f for f in range(FIELDS) if KIND[f] == kind]
        for k in range(step):
            first, last, link, ground_a, ground_b = [
                quantity(kind * COEF_ROWS + i, k, step) for i in range(COEF_ROWS)
            ]
            ground_a = ground_a + jnp.where(device[k] == 0, half * first, 0.0)
            ground_b = ground_b + jnp.where(device[k] == ranks - 1, half * last, 0.0)
            chains.append((link, ground_a, ground_b))
            first_coefs.append(first)
            last_coefs.append(last)
            sources.append([[quantity(2 * COEF_ROWS + 2 * f + end, k, step) for end in range(2)] for f in fields])
        first_coefs.append(up(first_coefs[0], 1))
        faces = [
            jnp.where(device[k] == ranks - 1, 0.0, half * (last_coefs[k] + first_coefs[k + 1])) for k in range(step)
        ]
        own = shifted(chains[-1], count - 1)
        own_sources = [shifted(s, count - 1) for s in sources[-1]]
        left = up(faces[-1], count - 1)
        right = up(faces[step - 2], count - 1) if step > 1 else up(faces[0], count - 2)

        if step == 1:
            (chain,), (ends,), shift = chains, sources, 1
        else:
            joined, weights = join_two(chains[0], faces[0], chains[1])
            chain = [jnp.where(last_row, a, b) for a, b in zip(chains[0], joined)]
            ends = [
                [jnp.where(last_row, a, b) for a, b in zip(low, join_two_sources(low, weights, high))]
                for low, high in zip(*sources)
            ]
            shift = 1
        while shift < count:
            joined, weights = join(chain, up(faces[-1], shift - 1), shift)
            joined_ends = [join_sources(s, weights, shift) for s in ends]
            if shift == 1 and step == 1:
                alone = row_index(count) == count - 2
                joined = [jnp.where(alone, a, b) for a, b in zip(chain, joined)]
                joined_ends = [[jnp.where(alone, a, b) for a, b in zip(*two)] for two in zip(ends, joined_ends)]
            chain, ends, shift = joined, joined_ends, 2 * shift
        link, ground_u, ground_v = chain
        uu, uv, vv = pair(left, ground_u, link, ground_v, right)
        u_b, v_b, u_a, v_a = left * uu, left * uv, right * uv, right * vv
        link = own[0] + v_b * right
        ground_a = own[1] + ground_u * u_a + ground_v * v_a
        ground_b = own[2] + ground_u * u_b + ground_v * v_b
        scale = recip(ground_a * ground_b + link * (ground_a + ground_b))
        aa, ab, bb = (ground_b + link) * scale, link * scale, (ground_a + link) * scale
        for (source_u, source_v), (source_a, source_b) in zip(ends, own_sources):
            source_a = source_a + source_u * u_a + source_v * v_a
            source_b = source_b + source_u * u_b + source_v * v_b
            results.append((aa * source_a + ab * source_b, ab * source_a + bb * source_b))
    return results


def received_rows(turned, ranks, rows, blocks, block):
    def quantity(q, k, step):
        at = k * spaced(rows) + q * blocks + block
        return turned[pl.ds(at, ranks // step, stride=step * spaced(rows)), :]

    return quantity


def spaced(rows):
    return rows | 1


def rotate(received, turned, ranks, rows, rank):
    for k in range(ranks):
        source = lax.rem(rank + 1 + k, ranks) * rows
        turned[pl.ds(k * spaced(rows), rows), :] = received[pl.ds(source, rows), :]


def coef_rows(coefs, chain):
    return (coefs[0][:1], coefs[-1][SUB - 1 :], chain[0][:1], chain[1][:1], chain[2][:1])


def x_ends_kernel(
    half, x_cells, blocks, ranks, rows,
    fields, viscosity, diffusivity, message, weights, pushed,
    line, fields_here, viscosity_here, diffusivity_here, arrived,
):
    per_field = x_cells * blocks
    copies = [
        pltpu.make_async_copy(viscosity, viscosity_here, arrived.at[0]),
        pltpu.make_async_copy(diffusivity, diffusivity_here, arrived.at[1]),
    ]
    for f in range(FIELDS):
        part = pl.ds(f * per_field, per_field)
        copies.append(pltpu.make_async_copy(fields.at[part], fields_here.at[part], arrived.at[2 + f]))
    for copy in copies:
        copy.start()

    def put(quantity, block, value):
        at = quantity * blocks + block
        line[at : at + 1, :] = value

    plans = {}
    for copy in copies[:2]:
        copy.wait()
    for kind, coef in enumerate((viscosity_here, diffusivity_here)):
        for block, coefs in enumerate(load_x_cells(coef, 0, x_cells, blocks)):
            *plan, chain = eliminate(coefs, half)
            plans[kind, block] = plan
            save_weights(weights.at[kind, block], plan[0], plan[2])
            for i, value in enumerate(coef_rows(coefs, chain)):
                put(kind * COEF_ROWS + i, block, value)
    for copy in copies[2:]:
        copy.wait()
    for f in range(FIELDS):
        for block, sources in enumerate(load_x_cells(fields_here, f, x_cells, blocks)):
            scaled, joined, ends = push_sources(*plans[KIND[f], block], sources)
            save_sources(pushed.at[f, block], scaled, joined)
            put(2 * COEF_ROWS + 2 * f, block, ends[0][:1])
            put(2 * COEF_ROWS + 2 * f + 1, block, ends[1][:1])
    for k in range(ranks):
        message[pl.ds(k * rows, rows), :] = line[...]


def x_join_kernel(
    half_x, half_y, x_cells, blocks, axis, ranks, rows, y_ranks, y_rows,
    received, x_weights, x_pushed, viscosity, diffusivity, message, weights, pushed,
    turned, line,
):
    rank = lax.axis_index(axis)
    count, y_count = x_cells // SUB, blocks * LANES // SUB
    rotate(received, turned, ranks, rows, rank)
    plans = []
    for kind, coef in enumerate((viscosity, diffusivity)):
        coefs = to_cells(jnp.concatenate([load_block(coef, 0, b, x_cells, blocks).T for b in range(blocks)]))
        *plan, chain = eliminate(coefs, half_y)
        plans.append(plan)
        save_weights(weights.at[kind], plan[0], plan[2])
        for i, value in enumerate(coef_rows(coefs, chain)):
            line[kind * COEF_ROWS + i : kind * COEF_ROWS + i + 1, :] = value
    lines = [[] for _ in range(FIELDS)]
    for block in range(blocks):
        ends = solve_ring(received_rows(turned, ranks, rows, blocks, block), ranks, rank, half_x)
        for f in range(FIELDS):
            end_a, end_b = [spread(e) for e in ends[f]]
            values = pull_values(
                *load_weights(x_weights.at[KIND[f], block], count), *load_sources(x_pushed.at[f, block], count), end_a, end_b
            )
            lines[f].append(from_cells(values).T)
    for f in range(FIELDS):
        scaled, joined, ends = push_sources(*plans[KIND[f]], to_cells(jnp.concatenate(lines[f])))
        save_sources(pushed.at[f], scaled, joined)
        at = 2 * COEF_ROWS + 2 * f
        line[at : at + 1, :] = ends[0][:1]
        line[at + 1 : at + 2, :] = ends[1][:1]
    for k in range(y_ranks):
        message[pl.ds(k * y_rows, y_rows), :] = line[...]


def y_join_kernel(
    half, x_cells, blocks, axis, ranks, rows,
    received, weights, pushed, updated, turned, here, left,
):
    per_field = x_cells * blocks
    count = blocks * LANES // SUB
    rank = lax.axis_index(axis)
    rotate(received, turned, ranks, rows, rank)
    ends = solve_ring(received_rows(turned, ranks, rows, 1, 0), ranks, rank, half)
    copies = []
    for f in range(FIELDS):
        end_a, end_b = [spread(e) for e in ends[f]]
        values = pull_values(
            *load_weights(weights.at[KIND[f]], count), *load_sources(pushed.at[f], count), end_a, end_b
        )
        lines = from_cells(values)
        for block in range(blocks):
            value = lines[block * LANES : (block + 1) * LANES].T
            for i in range(x_cells // SUB):
                here[pl.ds(tile_at(f, i, block, x_cells, blocks), SUB), :] = value[i * SUB : (i + 1) * SUB]
        part = pl.ds(f * per_field, per_field)
        copies.append(pltpu.make_async_copy(here.at[part], updated.at[part], left.at[f]))
        copies[-1].start()
    for copy in copies:
        copy.wait()


def call(kernel, outs, scratch, name, **kw):
    return pl.pallas_call(
        kernel,
        out_shape=outs,
        scratch_shapes=[pltpu.VMEM(s, jnp.float32) if isinstance(s, tuple) else s for s in scratch],
        compiler_params=pltpu.CompilerParams(vmem_limit_bytes=24 * 1024 * 1024),
        name=name,
        **kw,
    )


def near(shape):
    return pltpu.VMEM(shape, jnp.float32)


def far(shape):
    return pltpu.HBM(shape, jnp.float32)


def exchange(message, ranks, axis):
    flat = message.reshape(ranks, 1, -1)
    return lax.all_to_all(flat, axis, 0, 0, tiled=True).reshape(-1, LANES)


def on_device(x_ranks, y_ranks, fields, viscosity, diffusivity):
    _, _, x_cells, y_cells = fields.shape
    blocks = y_cells // LANES
    half_x, half_y = 0.5 * float(x_cells * x_cells), 0.5 * float(y_cells * y_cells)
    x_rows, y_rows = QUANTITIES * blocks, QUANTITIES
    x_count, y_count = x_cells // SUB, y_cells // SUB
    args = [tiles(a) for a in (fields, viscosity, diffusivity)]
    sizes = [a.shape for a in args]
    in_hbm = [pltpu.with_memory_space_constraint(a, pltpu.HBM) for a in args]

    message, x_weights, x_pushed = call(
        functools.partial(x_ends_kernel, half_x, x_cells, blocks, x_ranks, x_rows),
        [
            near((x_ranks * x_rows, LANES)),
            near((2, blocks, weight_rows(x_count), LANES)),
            near((FIELDS, blocks, source_rows(x_count), LANES)),
        ],
        [(x_rows, LANES), *sizes, pltpu.SemaphoreType.DMA((2 + FIELDS,))], "x_ends",
        in_specs=[pl.BlockSpec(memory_space=pltpu.HBM)] * 3,
    )(*in_hbm)
    received = exchange(message, x_ranks, "gx")
    message, y_weights, y_pushed = call(
        functools.partial(x_join_kernel, half_x, half_y, x_cells, blocks, "gx", x_ranks, x_rows, y_ranks, y_rows),
        [
            near((y_ranks * y_rows, LANES)),
            near((2, weight_rows(y_count), LANES)),
            near((FIELDS, source_rows(y_count), LANES)),
        ],
        [(x_ranks * spaced(x_rows), LANES), (y_rows, LANES)],
        "x_join",
    )(received, x_weights, x_pushed, *args[1:])
    received = exchange(message, y_ranks, "gy")
    (updated,) = call(
        functools.partial(y_join_kernel, half_y, x_cells, blocks, "gy", y_ranks, y_rows),
        [far(sizes[0])],
        [(y_ranks * spaced(y_rows), LANES), sizes[0], pltpu.SemaphoreType.DMA((FIELDS,))], "y_join",
        out_specs=[pl.BlockSpec(memory_space=pltpu.HBM)],
    )(received, y_weights, y_pushed)
    return untiles(updated, fields.shape)


def solution(mesh):
    placed = (P(None, None, "gx", "gy"), P(None, "gx", "gy"), P(None, "gx", "gy"))
    return jax.shard_map(
        functools.partial(on_device, mesh.shape["gx"], mesh.shape["gy"]),
        mesh=mesh, in_specs=placed, out_specs=P(None, None, "gx", "gy"), check_vma=False,
    )
```

```python
import functools

import jax
import jax.numpy as jnp
from jax import lax
from jax.experimental import pallas as pl
from jax.experimental.pallas import tpu as pltpu
from jax.sharding import PartitionSpec as P


FIELDS = 4
KIND = (0, 0, 0, 1)
LANES = 128
SUB = 8
COEF_ROWS = 5
QUANTITIES = 2 * COEF_ROWS + 2 * FIELDS


def recip(value):
    guess = pl.reciprocal(value, approx=True)
    return guess * (2.0 - value * guess)


def up(rows, step):
    step %= rows.shape[0]
    return pltpu.roll(rows, rows.shape[0] - step, 0) if step else rows


def down(rows, step):
    return pltpu.roll(rows, step, 0)


def row_index(rows):
    return lax.broadcasted_iota(jnp.int32, (rows, LANES), 0)


def pair(left, ground_u, link, ground_v, right):
    total_u, total_v = left + ground_u, right + ground_v
    scale = recip(total_u * total_v + link * (total_u + total_v))
    return (total_v + link) * scale, link * scale, (total_u + link) * scale


def join_two(low, face, high):
    link, ground_a, ground_u = low
    right, ground_v, ground_b = high
    uu, uv, vv = pair(link, ground_u, face, ground_v, right)
    u_left, v_left, u_right, v_right = link * uu, link * uv, right * uv, right * vv
    joined = (
        v_left * right,
        ground_a + ground_u * u_left + ground_v * v_left,
        ground_b + ground_u * u_right + ground_v * v_right,
    )
    return joined, (uu, uv, vv, u_left, v_left, u_right, v_right)


def join_two_sources(low, weights, high):
    _, _, _, u_left, v_left, u_right, v_right = weights
    (source_a, source_u), (source_v, source_b) = low, high
    return (
        source_a + source_u * u_left + source_v * v_left,
        source_b + source_u * u_right + source_v * v_right,
    )


def shifted(arrays, shift):
    return [up(x, shift) for x in arrays]


def join(chain, face, shift):
    return join_two(chain, face, shifted(chain, shift))


def join_sources(ends, weights, shift):
    return join_two_sources(ends, weights, shifted(ends, shift))


def schedule(count):
    nodes, rounds = list(range(count)), []
    while len(nodes) > 2:
        gone = range(1, len(nodes) - 1, 2)
        rounds.append([(nodes[i], nodes[i - 1], nodes[i + 1]) for i in gone])
        nodes = [n for i, n in enumerate(nodes) if i not in gone]
    return rounds


SHIFTS = (1, 2, 4)


def eliminate(coefs, half):
    count = len(coefs)
    ground = [1.0] * count
    link = {i: half * (coefs[i] + coefs[i + 1]) for i in range(count - 1)}
    cells, scales = {}, {}
    for round_ in schedule(count):
        for cell, low, high in round_:
            scale = recip(link[low] + link[cell] + ground[cell])
            to_low, to_high = link[low] * scale, link[cell] * scale
            ground[low] = ground[low] + to_low * ground[cell]
            ground[high] = ground[high] + to_high * ground[cell]
            link[low] = to_low * link[cell]
            cells[cell], scales[cell] = (to_low, to_high), scale
    face = half * (coefs[-1] + up(coefs[0], 1))
    chain, joins = (link[0], ground[0], ground[-1]), []
    for shift in SHIFTS:
        chain, weights = join(chain, up(face, shift - 1), shift)
        joins.append(weights)
    return cells, scales, joins, chain


def push_sources(cells, scales, joins, sources):
    sources, scaled = list(sources), {}
    for round_ in schedule(len(sources)):
        for cell, low, high in round_:
            to_low, to_high = cells[cell]
            sources[low] = sources[low] + to_low * sources[cell]
            sources[high] = sources[high] + to_high * sources[cell]
            scaled[cell] = scales[cell] * sources[cell]
    ends, joined = (sources[0], sources[-1]), []
    for shift, weights in zip(SHIFTS, joins):
        uu, uv, vv = weights[:3]
        source_u, source_v = ends[1], up(ends[0], shift)
        joined.append((uu * source_u + uv * source_v, uv * source_u + vv * source_v))
        ends = join_sources(ends, weights, shift)
    return scaled, joined, ends


def pull_values(cells, joins, scaled, joined, end_a, end_b):
    row = row_index(SUB)
    for shift, (u_left, v_left, u_right, v_right), (from_u, from_v) in reversed(list(zip(SHIFTS, joins, joined))):
        value_u = from_u + u_left * end_a + u_right * end_b
        value_v = from_v + v_left * end_a + v_right * end_b
        on_right = (row // shift) % 2 == 1
        end_a = jnp.where(on_right, down(value_v, shift), end_a)
        end_b = jnp.where(on_right, down(end_b, shift), value_u)
    count = len(cells) + 2
    values = {0: end_a, count - 1: end_b}
    for round_ in reversed(schedule(count)):
        for cell, low, high in round_:
            to_low, to_high = cells[cell]
            values[cell] = scaled[cell] + to_low * values[low] + to_high * values[high]
    return [values[t] for t in range(count)]


def weight_rows(count):
    return (2 * (count - 2) + 4 * len(SHIFTS)) * SUB


def source_rows(count):
    return (count - 2 + 2 * len(SHIFTS)) * SUB


def save(ref, arrays):
    for i, array in enumerate(arrays):
        ref[pl.ds(i * SUB, SUB), :] = array


def save_weights(ref, cells, joins):
    save(ref, [w for c in sorted(cells) for w in cells[c]] + [w for weights in joins for w in weights[3:]])


def save_sources(ref, scaled, joined):
    save(ref, [scaled[c] for c in sorted(scaled)] + [v for two in joined for v in two])


def load_weights(ref, count):
    def at(i):
        return ref[pl.ds(i * SUB, SUB), :]

    base = 2 * (count - 2)
    cells = {c: (at(2 * c - 2), at(2 * c - 1)) for c in range(1, count - 1)}
    return cells, [tuple(at(base + 4 * j + i) for i in range(4)) for j in range(len(SHIFTS))]


def load_sources(ref, count):
    def at(i):
        return ref[pl.ds(i * SUB, SUB), :]

    base = count - 2
    return {c: at(c - 1) for c in range(1, count - 1)}, [
        (at(base + 2 * j), at(base + 2 * j + 1)) for j in range(len(SHIFTS))
    ]


def spread(row):
    return jnp.broadcast_to(row[:1], (SUB, LANES))


def to_cells(rows):
    parts = jnp.swapaxes(rows.reshape(SUB, -1, LANES), 0, 1)
    return [parts[t] for t in range(parts.shape[0])]


def from_cells(cells):
    return jnp.swapaxes(jnp.stack(cells), 0, 1).reshape(-1, LANES)


def tiles(array):
    x_cells, y_cells = array.shape[-2:]
    split = array.reshape(-1, x_cells // SUB, SUB, y_cells // LANES, LANES)
    return split.transpose(0, 1, 3, 2, 4).reshape(-1, LANES)


def untiles(flat, shape):
    split = flat.reshape(-1, shape[-2] // SUB, shape[-1] // LANES, SUB, LANES)
    return split.transpose(0, 1, 3, 2, 4).reshape(shape)


def tile_at(field, x_tile, block, x_cells, blocks):
    return ((field * (x_cells // SUB) + x_tile) * blocks + block) * SUB


def load_x_cells(ref, field, x_cells, blocks):
    parts = to_cells(ref[pl.ds(field * x_cells * blocks, x_cells * blocks), :])
    return [
        [parts[(t // SUB * blocks + block) * SUB + t % SUB] for t in range(x_cells // SUB)] for block in range(blocks)
    ]


def load_block(ref, field, block, x_cells, blocks):
    return jnp.concatenate(
        [ref[pl.ds(tile_at(field, i, block, x_cells, blocks), SUB), :] for i in range(x_cells // SUB)]
    )


def solve_ring(quantity, ranks, rank, half):
    step = max(1, ranks // SUB)
    count = ranks // step
    device = [lax.rem(row_index(count) * step + (rank + 1 + k), ranks) for k in range(step)]
    last_row = row_index(count) == count - 1
    results = []
    for kind in range(2):
        chains, sources, first_coefs, last_coefs = [], [], [], []
        fields = [f for f in range(FIELDS) if KIND[f] == kind]
        for k in range(step):
            first, last, link, ground_a, ground_b = [
                quantity(kind * COEF_ROWS + i, k, step) for i in range(COEF_ROWS)
            ]
            ground_a = ground_a + jnp.where(device[k] == 0, half * first, 0.0)
            ground_b = ground_b + jnp.where(device[k] == ranks - 1, half * last, 0.0)
            chains.append((link, ground_a, ground_b))
            first_coefs.append(first)
            last_coefs.append(last)
            sources.append([[quantity(2 * COEF_ROWS + 2 * f + end, k, step) for end in range(2)] for f in fields])
        first_coefs.append(up(first_coefs[0], 1))
        faces = [
            jnp.where(device[k] == ranks - 1, 0.0, half * (last_coefs[k] + first_coefs[k + 1])) for k in range(step)
        ]
        own = shifted(chains[-1], count - 1)
        own_sources = [shifted(s, count - 1) for s in sources[-1]]
        left = up(faces[-1], count - 1)
        right = up(faces[step - 2], count - 1) if step > 1 else up(faces[0], count - 2)

        if step == 1:
            (chain,), (ends,), shift = chains, sources, 1
        else:
            joined, weights = join_two(chains[0], faces[0], chains[1])
            chain = [jnp.where(last_row, a, b) for a, b in zip(chains[0], joined)]
            ends = [
                [jnp.where(last_row, a, b) for a, b in zip(low, join_two_sources(low, weights, high))]
                for low, high in zip(*sources)
            ]
            shift = 1
        while shift < count:
            joined, weights = join(chain, up(faces[-1], shift - 1), shift)
            joined_ends = [join_sources(s, weights, shift) for s in ends]
            if shift == 1 and step == 1:
                alone = row_index(count) == count - 2
                joined = [jnp.where(alone, a, b) for a, b in zip(chain, joined)]
                joined_ends = [[jnp.where(alone, a, b) for a, b in zip(*two)] for two in zip(ends, joined_ends)]
            chain, ends, shift = joined, joined_ends, 2 * shift
        link, ground_u, ground_v = chain
        uu, uv, vv = pair(left, ground_u, link, ground_v, right)
        u_b, v_b, u_a, v_a = left * uu, left * uv, right * uv, right * vv
        link = own[0] + v_b * right
        ground_a = own[1] + ground_u * u_a + ground_v * v_a
        ground_b = own[2] + ground_u * u_b + ground_v * v_b
        scale = recip(ground_a * ground_b + link * (ground_a + ground_b))
        aa, ab, bb = (ground_b + link) * scale, link * scale, (ground_a + link) * scale
        for (source_u, source_v), (source_a, source_b) in zip(ends, own_sources):
            source_a = source_a + source_u * u_a + source_v * v_a
            source_b = source_b + source_u * u_b + source_v * v_b
            results.append((aa * source_a + ab * source_b, ab * source_a + bb * source_b))
    return results


def received_rows(turned, ranks, rows, blocks, block):
    def quantity(q, k, step):
        at = k * spaced(rows) + q * blocks + block
        return turned[pl.ds(at, ranks // step, stride=step * spaced(rows)), :]

    return quantity


def spaced(rows):
    return rows | 1


def rotate(received, turned, ranks, rows, rank):
    for k in range(ranks):
        source = lax.rem(rank + 1 + k, ranks) * rows
        turned[pl.ds(k * spaced(rows), rows), :] = received[pl.ds(source, rows), :]


def place(parts, turned, ranks, rows, rank):
    for k, other, message in parts:
        chip = lax.bitwise_xor(lax.div(rank, 2), k)
        device = 2 * chip + lax.bitwise_xor(lax.rem(rank, 2), int(other))
        at = lax.rem(device + ranks - rank - 1, ranks) * spaced(rows)
        turned[pl.ds(at, rows), :] = message


def coef_rows(coefs, chain):
    return (coefs[0][:1], coefs[-1][SUB - 1 :], chain[0][:1], chain[1][:1], chain[2][:1])


def x_ends_kernel(
    half, x_cells, blocks, ranks, rows,
    fields, viscosity, diffusivity, message, weights, pushed,
    line, fields_here, viscosity_here, diffusivity_here, arrived,
):
    per_field = x_cells * blocks
    copies = [
        pltpu.make_async_copy(viscosity, viscosity_here, arrived.at[0]),
        pltpu.make_async_copy(diffusivity, diffusivity_here, arrived.at[1]),
    ]
    for f in range(FIELDS):
        part = pl.ds(f * per_field, per_field)
        copies.append(pltpu.make_async_copy(fields.at[part], fields_here.at[part], arrived.at[2 + f]))
    for copy in copies:
        copy.start()

    def put(quantity, block, value):
        at = quantity * blocks + block
        line[at : at + 1, :] = value

    plans = {}
    for copy in copies[:2]:
        copy.wait()
    for kind, coef in enumerate((viscosity_here, diffusivity_here)):
        for block, coefs in enumerate(load_x_cells(coef, 0, x_cells, blocks)):
            *plan, chain = eliminate(coefs, half)
            plans[kind, block] = plan
            save_weights(weights.at[kind, block], plan[0], plan[2])
            for i, value in enumerate(coef_rows(coefs, chain)):
                put(kind * COEF_ROWS + i, block, value)
    for copy in copies[2:]:
        copy.wait()
    for f in range(FIELDS):
        for block, sources in enumerate(load_x_cells(fields_here, f, x_cells, blocks)):
            scaled, joined, ends = push_sources(*plans[KIND[f], block], sources)
            save_sources(pushed.at[f, block], scaled, joined)
            put(2 * COEF_ROWS + 2 * f, block, ends[0][:1])
            put(2 * COEF_ROWS + 2 * f + 1, block, ends[1][:1])
    for k in range(ranks):
        message[pl.ds(k * rows, rows), :] = line[...]


def x_join_kernel(
    half_x, half_y, x_cells, blocks, axis, ranks, rows,
    received, x_weights, x_pushed, viscosity, diffusivity, message, weights, pushed,
    turned,
):
    rank = lax.axis_index(axis)
    count, y_count = x_cells // SUB, blocks * LANES // SUB
    rotate(received, turned, ranks, rows, rank)
    plans = []
    for kind, coef in enumerate((viscosity, diffusivity)):
        coefs = to_cells(jnp.concatenate([load_block(coef, 0, b, x_cells, blocks).T for b in range(blocks)]))
        *plan, chain = eliminate(coefs, half_y)
        plans.append(plan)
        save_weights(weights.at[kind], plan[0], plan[2])
        for i, value in enumerate(coef_rows(coefs, chain)):
            message[kind * COEF_ROWS + i : kind * COEF_ROWS + i + 1, :] = value
    lines = [[] for _ in range(FIELDS)]
    for block in range(blocks):
        ends = solve_ring(received_rows(turned, ranks, rows, blocks, block), ranks, rank, half_x)
        for f in range(FIELDS):
            end_a, end_b = [spread(e) for e in ends[f]]
            values = pull_values(
                *load_weights(x_weights.at[KIND[f], block], count), *load_sources(x_pushed.at[f, block], count), end_a, end_b
            )
            lines[f].append(from_cells(values).T)
    for f in range(FIELDS):
        scaled, joined, ends = push_sources(*plans[KIND[f]], to_cells(jnp.concatenate(lines[f])))
        save_sources(pushed.at[f], scaled, joined)
        at = 2 * COEF_ROWS + 2 * f
        message[at : at + 1, :] = ends[0][:1]
        message[at + 1 : at + 2, :] = ends[1][:1]


def y_join_kernel(
    half, x_cells, blocks, axis, ranks, rows, layout,
    *refs,
):
    *chips, weights, pushed, updated, turned, here, left = refs
    per_field = x_cells * blocks
    count = blocks * LANES // SUB
    rank = lax.axis_index(axis)
    parts = []
    for (k, others), ref in zip(layout, chips):
        for i, other in enumerate(others):
            parts.append((k, other, ref[pl.ds(i * rows, rows), :]))
    place(parts, turned, ranks, rows, rank)
    ends = solve_ring(received_rows(turned, ranks, rows, 1, 0), ranks, rank, half)
    copies = []
    for f in range(FIELDS):
        end_a, end_b = [spread(e) for e in ends[f]]
        values = pull_values(
            *load_weights(weights.at[KIND[f]], count), *load_sources(pushed.at[f], count), end_a, end_b
        )
        lines = from_cells(values)
        for block in range(blocks):
            value = lines[block * LANES : (block + 1) * LANES].T
            for i in range(x_cells // SUB):
                here[pl.ds(tile_at(f, i, block, x_cells, blocks), SUB), :] = value[i * SUB : (i + 1) * SUB]
        part = pl.ds(f * per_field, per_field)
        copies.append(pltpu.make_async_copy(here.at[part], updated.at[part], left.at[f]))
        copies[-1].start()
    for copy in copies:
        copy.wait()


def call(kernel, outs, scratch, name, **kw):
    return pl.pallas_call(
        kernel,
        out_shape=outs,
        scratch_shapes=[pltpu.VMEM(s, jnp.float32) if isinstance(s, tuple) else s for s in scratch],
        compiler_params=pltpu.CompilerParams(vmem_limit_bytes=24 * 1024 * 1024),
        name=name,
        **kw,
    )


def near(shape):
    return pltpu.VMEM(shape, jnp.float32)


def far(shape):
    return pltpu.HBM(shape, jnp.float32)


def exchange(message, ranks, axis):
    flat = message.reshape(ranks, 1, -1)
    return lax.all_to_all(flat, axis, 0, 0, tiled=True).reshape(-1, LANES)


def exchange_chips(message, ranks, axis):
    def send(array, step):
        return lax.ppermute(array, axis, [(i, i ^ step) for i in range(ranks)])

    chips = range(1, ranks // 2)
    early = chips[2 - 1]
    near_chip = send(message, 2 * early)
    other = send(message, 1)
    both = jnp.concatenate([message, other])
    layout, arrays = [(0, (False, True))], [both]
    for k in chips:
        if k != early:
            layout.append((k, (False, True)))
            arrays.append(send(both, 2 * k))
    layout += [(early, (False,)), (early, (True,))]
    arrays += [near_chip, send(near_chip, 1)]
    return layout, arrays


def on_device(x_ranks, y_ranks, fields, viscosity, diffusivity):
    _, _, x_cells, y_cells = fields.shape
    blocks = y_cells // LANES
    half_x, half_y = 0.5 * float(x_cells * x_cells), 0.5 * float(y_cells * y_cells)
    x_rows, y_rows = QUANTITIES * blocks, QUANTITIES
    x_count, y_count = x_cells // SUB, y_cells // SUB
    args = [tiles(a) for a in (fields, viscosity, diffusivity)]
    sizes = [a.shape for a in args]
    in_hbm = [pltpu.with_memory_space_constraint(a, pltpu.HBM) for a in args]

    message, x_weights, x_pushed = call(
        functools.partial(x_ends_kernel, half_x, x_cells, blocks, x_ranks, x_rows),
        [
            near((x_ranks * x_rows, LANES)),
            near((2, blocks, weight_rows(x_count), LANES)),
            near((FIELDS, blocks, source_rows(x_count), LANES)),
        ],
        [(x_rows, LANES), *sizes, pltpu.SemaphoreType.DMA((2 + FIELDS,))], "x_ends",
        in_specs=[pl.BlockSpec(memory_space=pltpu.HBM)] * 3,
    )(*in_hbm)
    received = exchange(message, x_ranks, "gx")
    message, y_weights, y_pushed = call(
        functools.partial(x_join_kernel, half_x, half_y, x_cells, blocks, "gx", x_ranks, x_rows),
        [
            near((y_rows, LANES)),
            near((2, weight_rows(y_count), LANES)),
            near((FIELDS, source_rows(y_count), LANES)),
        ],
        [(x_ranks * spaced(x_rows), LANES)],
        "x_join",
    )(received, x_weights, x_pushed, *args[1:])
    layout, chips = exchange_chips(message, y_ranks, "gy")
    (updated,) = call(
        functools.partial(y_join_kernel, half_y, x_cells, blocks, "gy", y_ranks, y_rows, layout),
        [far(sizes[0])],
        [(y_ranks * spaced(y_rows), LANES), sizes[0], pltpu.SemaphoreType.DMA((FIELDS,))], "y_join",
        out_specs=[pl.BlockSpec(memory_space=pltpu.HBM)],
    )(*chips, y_weights, y_pushed)
    return untiles(updated, fields.shape)


def solution(mesh):
    placed = (P(None, None, "gx", "gy"), P(None, "gx", "gy"), P(None, "gx", "gy"))
    return jax.shard_map(
        functools.partial(on_device, mesh.shape["gx"], mesh.shape["gy"]),
        mesh=mesh, in_specs=placed, out_specs=P(None, None, "gx", "gy"), check_vma=False,
    )
```

```python
import functools

import jax
import jax.numpy as jnp
from jax import lax
from jax.experimental import pallas as pl
from jax.experimental.pallas import tpu as pltpu
from jax.sharding import PartitionSpec as P


FIELDS = 4
KIND = (0, 0, 0, 1)
LANES = 128
SUB = 8
COEF_ROWS = 5
QUANTITIES = 2 * COEF_ROWS + 2 * FIELDS


def recip(value):
    return pl.reciprocal(value, approx=True)


def up(rows, step):
    step %= rows.shape[0]
    return pltpu.roll(rows, rows.shape[0] - step, 0) if step else rows


def down(rows, step):
    return pltpu.roll(rows, step, 0)


def row_index(rows):
    return lax.broadcasted_iota(jnp.int32, (rows, LANES), 0)


def pair(left, ground_u, link, ground_v, right):
    total_u, total_v = left + ground_u, right + ground_v
    scale = recip(total_u * total_v + link * (total_u + total_v))
    return (total_v + link) * scale, link * scale, (total_u + link) * scale


def join_two(low, face, high):
    link, ground_a, ground_u = low
    right, ground_v, ground_b = high
    uu, uv, vv = pair(link, ground_u, face, ground_v, right)
    u_left, v_left, u_right, v_right = link * uu, link * uv, right * uv, right * vv
    joined = (
        v_left * right,
        ground_a + ground_u * u_left + ground_v * v_left,
        ground_b + ground_u * u_right + ground_v * v_right,
    )
    return joined, (uu, uv, vv, u_left, v_left, u_right, v_right)


def join_two_sources(low, weights, high):
    _, _, _, u_left, v_left, u_right, v_right = weights
    (source_a, source_u), (source_v, source_b) = low, high
    return (
        source_a + source_u * u_left + source_v * v_left,
        source_b + source_u * u_right + source_v * v_right,
    )


def shifted(arrays, shift):
    return [up(x, shift) for x in arrays]


def join(chain, face, shift):
    return join_two(chain, face, shifted(chain, shift))


def join_sources(ends, weights, shift):
    return join_two_sources(ends, weights, shifted(ends, shift))


def schedule(count):
    nodes, rounds = list(range(count)), []
    while len(nodes) > 2:
        gone = range(1, len(nodes) - 1, 2)
        rounds.append([(nodes[i], nodes[i - 1], nodes[i + 1]) for i in gone])
        nodes = [n for i, n in enumerate(nodes) if i not in gone]
    return rounds


SHIFTS = (1, 2, 4)


def eliminate(coefs, half):
    count = len(coefs)
    ground = [1.0] * count
    link = {i: half * (coefs[i] + coefs[i + 1]) for i in range(count - 1)}
    cells, scales = {}, {}
    for round_ in schedule(count):
        for cell, low, high in round_:
            scale = recip(link[low] + link[cell] + ground[cell])
            to_low, to_high = link[low] * scale, link[cell] * scale
            ground[low] = ground[low] + to_low * ground[cell]
            ground[high] = ground[high] + to_high * ground[cell]
            link[low] = to_low * link[cell]
            cells[cell], scales[cell] = (to_low, to_high), scale
    face = half * (coefs[-1] + up(coefs[0], 1))
    chain, joins = (link[0], ground[0], ground[-1]), []
    for shift in SHIFTS:
        chain, weights = join(chain, up(face, shift - 1), shift)
        joins.append(weights)
    return cells, scales, joins, chain


def push_sources(cells, scales, joins, sources):
    sources, scaled = list(sources), {}
    for round_ in schedule(len(sources)):
        for cell, low, high in round_:
            to_low, to_high = cells[cell]
            sources[low] = sources[low] + to_low * sources[cell]
            sources[high] = sources[high] + to_high * sources[cell]
            scaled[cell] = scales[cell] * sources[cell]
    ends, joined = (sources[0], sources[-1]), []
    for shift, weights in zip(SHIFTS, joins):
        uu, uv, vv = weights[:3]
        source_u, source_v = ends[1], up(ends[0], shift)
        joined.append((uu * source_u + uv * source_v, uv * source_u + vv * source_v))
        ends = join_sources(ends, weights, shift)
    return scaled, joined, ends


def pull_values(cells, joins, scaled, joined, end_a, end_b):
    row = row_index(SUB)
    for shift, (u_left, v_left, u_right, v_right), (from_u, from_v) in reversed(list(zip(SHIFTS, joins, joined))):
        value_u = from_u + u_left * end_a + u_right * end_b
        value_v = from_v + v_left * end_a + v_right * end_b
        on_right = (row // shift) % 2 == 1
        end_a = jnp.where(on_right, down(value_v, shift), end_a)
        end_b = jnp.where(on_right, down(end_b, shift), value_u)
    count = len(cells) + 2
    values = {0: end_a, count - 1: end_b}
    for round_ in reversed(schedule(count)):
        for cell, low, high in round_:
            to_low, to_high = cells[cell]
            values[cell] = scaled[cell] + to_low * values[low] + to_high * values[high]
    return [values[t] for t in range(count)]


def weight_rows(count):
    return (2 * (count - 2) + 4 * len(SHIFTS)) * SUB


def source_rows(count):
    return (count - 2 + 2 * len(SHIFTS)) * SUB


def save(ref, arrays):
    for i, array in enumerate(arrays):
        ref[pl.ds(i * SUB, SUB), :] = array


def save_weights(ref, cells, joins):
    save(ref, [w for c in sorted(cells) for w in cells[c]] + [w for weights in joins for w in weights[3:]])


def save_sources(ref, scaled, joined):
    save(ref, [scaled[c] for c in sorted(scaled)] + [v for two in joined for v in two])


def load_weights(ref, count):
    def at(i):
        return ref[pl.ds(i * SUB, SUB), :]

    base = 2 * (count - 2)
    cells = {c: (at(2 * c - 2), at(2 * c - 1)) for c in range(1, count - 1)}
    return cells, [tuple(at(base + 4 * j + i) for i in range(4)) for j in range(len(SHIFTS))]


def load_sources(ref, count):
    def at(i):
        return ref[pl.ds(i * SUB, SUB), :]

    base = count - 2
    return {c: at(c - 1) for c in range(1, count - 1)}, [
        (at(base + 2 * j), at(base + 2 * j + 1)) for j in range(len(SHIFTS))
    ]


def spread(row):
    return jnp.broadcast_to(row[:1], (SUB, LANES))


def to_cells(rows):
    parts = jnp.swapaxes(rows.reshape(SUB, -1, LANES), 0, 1)
    return [parts[t] for t in range(parts.shape[0])]


def from_cells(cells):
    return jnp.swapaxes(jnp.stack(cells), 0, 1).reshape(-1, LANES)


def tiles(array):
    x_cells, y_cells = array.shape[-2:]
    split = array.reshape(-1, x_cells // SUB, SUB, y_cells // LANES, LANES)
    return split.transpose(0, 1, 3, 2, 4).reshape(-1, LANES)


def untiles(flat, shape):
    split = flat.reshape(-1, shape[-2] // SUB, shape[-1] // LANES, SUB, LANES)
    return split.transpose(0, 1, 3, 2, 4).reshape(shape)


def tile_at(field, x_tile, block, x_cells, blocks):
    return ((field * (x_cells // SUB) + x_tile) * blocks + block) * SUB


def load_x_cells(ref, field, x_cells, blocks):
    parts = to_cells(ref[pl.ds(field * x_cells * blocks, x_cells * blocks), :])
    return [
        [parts[(t // SUB * blocks + block) * SUB + t % SUB] for t in range(x_cells // SUB)] for block in range(blocks)
    ]


def load_block(ref, field, block, x_cells, blocks):
    return jnp.concatenate(
        [ref[pl.ds(tile_at(field, i, block, x_cells, blocks), SUB), :] for i in range(x_cells // SUB)]
    )


def solve_ring(quantity, ranks, rank, half):
    step = max(1, ranks // SUB)
    count = ranks // step
    device = [lax.rem(row_index(count) * step + (rank + 1 + k), ranks) for k in range(step)]
    last_row = row_index(count) == count - 1
    results = []
    for kind in range(2):
        chains, sources, first_coefs, last_coefs = [], [], [], []
        fields = [f for f in range(FIELDS) if KIND[f] == kind]
        for k in range(step):
            first, last, link, ground_a, ground_b = [
                quantity(kind * COEF_ROWS + i, k, step) for i in range(COEF_ROWS)
            ]
            ground_a = ground_a + jnp.where(device[k] == 0, half * first, 0.0)
            ground_b = ground_b + jnp.where(device[k] == ranks - 1, half * last, 0.0)
            chains.append((link, ground_a, ground_b))
            first_coefs.append(first)
            last_coefs.append(last)
            sources.append([[quantity(2 * COEF_ROWS + 2 * f + end, k, step) for end in range(2)] for f in fields])
        first_coefs.append(up(first_coefs[0], 1))
        faces = [
            jnp.where(device[k] == ranks - 1, 0.0, half * (last_coefs[k] + first_coefs[k + 1])) for k in range(step)
        ]
        own = shifted(chains[-1], count - 1)
        own_sources = [shifted(s, count - 1) for s in sources[-1]]
        left = up(faces[-1], count - 1)
        right = up(faces[step - 2], count - 1) if step > 1 else up(faces[0], count - 2)

        if step == 1:
            (chain,), (ends,), shift = chains, sources, 1
        else:
            joined, weights = join_two(chains[0], faces[0], chains[1])
            chain = [jnp.where(last_row, a, b) for a, b in zip(chains[0], joined)]
            ends = [
                [jnp.where(last_row, a, b) for a, b in zip(low, join_two_sources(low, weights, high))]
                for low, high in zip(*sources)
            ]
            shift = 1
        while shift < count:
            joined, weights = join(chain, up(faces[-1], shift - 1), shift)
            joined_ends = [join_sources(s, weights, shift) for s in ends]
            if shift == 1 and step == 1:
                alone = row_index(count) == count - 2
                joined = [jnp.where(alone, a, b) for a, b in zip(chain, joined)]
                joined_ends = [[jnp.where(alone, a, b) for a, b in zip(*two)] for two in zip(ends, joined_ends)]
            chain, ends, shift = joined, joined_ends, 2 * shift
        link, ground_u, ground_v = chain
        uu, uv, vv = pair(left, ground_u, link, ground_v, right)
        u_b, v_b, u_a, v_a = left * uu, left * uv, right * uv, right * vv
        link = own[0] + v_b * right
        ground_a = own[1] + ground_u * u_a + ground_v * v_a
        ground_b = own[2] + ground_u * u_b + ground_v * v_b
        scale = recip(ground_a * ground_b + link * (ground_a + ground_b))
        aa, ab, bb = (ground_b + link) * scale, link * scale, (ground_a + link) * scale
        for (source_u, source_v), (source_a, source_b) in zip(ends, own_sources):
            source_a = source_a + source_u * u_a + source_v * v_a
            source_b = source_b + source_u * u_b + source_v * v_b
            results.append((aa * source_a + ab * source_b, ab * source_a + bb * source_b))
    return results


def received_rows(turned, ranks, rows, blocks, block):
    def quantity(q, k, step):
        at = k * spaced(rows) + q * blocks + block
        return turned[pl.ds(at, ranks // step, stride=step * spaced(rows)), :]

    return quantity


def spaced(rows):
    return rows | 1


def rotate(received, turned, ranks, rows, rank):
    for k in range(ranks):
        source = lax.rem(rank + 1 + k, ranks) * rows
        turned[pl.ds(k * spaced(rows), rows), :] = received[pl.ds(source, rows), :]


def place(parts, turned, ranks, rows, rank):
    for k, other, message in parts:
        chip = lax.bitwise_xor(lax.div(rank, 2), k)
        device = 2 * chip + lax.bitwise_xor(lax.rem(rank, 2), int(other))
        at = lax.rem(device + ranks - rank - 1, ranks) * spaced(rows)
        turned[pl.ds(at, rows), :] = message


def coef_rows(coefs, chain):
    return (coefs[0][:1], coefs[-1][SUB - 1 :], chain[0][:1], chain[1][:1], chain[2][:1])


def x_ends_kernel(
    half, x_cells, blocks, ranks, rows,
    fields, viscosity, diffusivity, message, weights, pushed,
    line, fields_here, viscosity_here, diffusivity_here, arrived,
):
    per_field = x_cells * blocks
    copies = [
        pltpu.make_async_copy(viscosity, viscosity_here, arrived.at[0]),
        pltpu.make_async_copy(diffusivity, diffusivity_here, arrived.at[1]),
    ]
    for f in range(FIELDS):
        part = pl.ds(f * per_field, per_field)
        copies.append(pltpu.make_async_copy(fields.at[part], fields_here.at[part], arrived.at[2 + f]))
    for copy in copies:
        copy.start()

    def put(quantity, block, value):
        at = quantity * blocks + block
        line[at : at + 1, :] = value

    plans = {}
    for copy in copies[:2]:
        copy.wait()
    for kind, coef in enumerate((viscosity_here, diffusivity_here)):
        for block, coefs in enumerate(load_x_cells(coef, 0, x_cells, blocks)):
            *plan, chain = eliminate(coefs, half)
            plans[kind, block] = plan
            save_weights(weights.at[kind, block], plan[0], plan[2])
            for i, value in enumerate(coef_rows(coefs, chain)):
                put(kind * COEF_ROWS + i, block, value)
    for copy in copies[2:]:
        copy.wait()
    for f in range(FIELDS):
        for block, sources in enumerate(load_x_cells(fields_here, f, x_cells, blocks)):
            scaled, joined, ends = push_sources(*plans[KIND[f], block], sources)
            save_sources(pushed.at[f, block], scaled, joined)
            put(2 * COEF_ROWS + 2 * f, block, ends[0][:1])
            put(2 * COEF_ROWS + 2 * f + 1, block, ends[1][:1])
    for k in range(ranks):
        message[pl.ds(k * rows, rows), :] = line[...]


def x_join_kernel(
    half_x, half_y, x_cells, blocks, axis, ranks, rows,
    received, x_weights, x_pushed, viscosity, diffusivity, message, weights, pushed,
    turned,
):
    rank = lax.axis_index(axis)
    count, y_count = x_cells // SUB, blocks * LANES // SUB
    rotate(received, turned, ranks, rows, rank)
    plans = []
    for kind, coef in enumerate((viscosity, diffusivity)):
        coefs = to_cells(jnp.concatenate([load_block(coef, 0, b, x_cells, blocks).T for b in range(blocks)]))
        *plan, chain = eliminate(coefs, half_y)
        plans.append(plan)
        save_weights(weights.at[kind], plan[0], plan[2])
        for i, value in enumerate(coef_rows(coefs, chain)):
            message[kind * COEF_ROWS + i : kind * COEF_ROWS + i + 1, :] = value
    lines = [[] for _ in range(FIELDS)]
    for block in range(blocks):
        ends = solve_ring(received_rows(turned, ranks, rows, blocks, block), ranks, rank, half_x)
        for f in range(FIELDS):
            end_a, end_b = [spread(e) for e in ends[f]]
            values = pull_values(
                *load_weights(x_weights.at[KIND[f], block], count), *load_sources(x_pushed.at[f, block], count), end_a, end_b
            )
            lines[f].append(from_cells(values).T)
    for f in range(FIELDS):
        scaled, joined, ends = push_sources(*plans[KIND[f]], to_cells(jnp.concatenate(lines[f])))
        save_sources(pushed.at[f], scaled, joined)
        at = 2 * COEF_ROWS + 2 * f
        message[at : at + 1, :] = ends[0][:1]
        message[at + 1 : at + 2, :] = ends[1][:1]


def y_join_kernel(
    half, x_cells, blocks, axis, ranks, rows, layout,
    *refs,
):
    *chips, weights, pushed, updated, turned, here, left = refs
    per_field = x_cells * blocks
    count = blocks * LANES // SUB
    rank = lax.axis_index(axis)
    parts = []
    for (k, others), ref in zip(layout, chips):
        for i, other in enumerate(others):
            parts.append((k, other, ref[pl.ds(i * rows, rows), :]))
    place(parts, turned, ranks, rows, rank)
    ends = solve_ring(received_rows(turned, ranks, rows, 1, 0), ranks, rank, half)
    copies = []
    for f in range(FIELDS):
        end_a, end_b = [spread(e) for e in ends[f]]
        values = pull_values(
            *load_weights(weights.at[KIND[f]], count), *load_sources(pushed.at[f], count), end_a, end_b
        )
        lines = from_cells(values)
        for block in range(blocks):
            value = lines[block * LANES : (block + 1) * LANES].T
            for i in range(x_cells // SUB):
                here[pl.ds(tile_at(f, i, block, x_cells, blocks), SUB), :] = value[i * SUB : (i + 1) * SUB]
        part = pl.ds(f * per_field, per_field)
        copies.append(pltpu.make_async_copy(here.at[part], updated.at[part], left.at[f]))
        copies[-1].start()
    for copy in copies:
        copy.wait()


def call(kernel, outs, scratch, name, **kw):
    return pl.pallas_call(
        kernel,
        out_shape=outs,
        scratch_shapes=[pltpu.VMEM(s, jnp.float32) if isinstance(s, tuple) else s for s in scratch],
        compiler_params=pltpu.CompilerParams(vmem_limit_bytes=24 * 1024 * 1024),
        name=name,
        **kw,
    )


def near(shape):
    return pltpu.VMEM(shape, jnp.float32)


def far(shape):
    return pltpu.HBM(shape, jnp.float32)


def exchange(message, ranks, axis):
    flat = message.reshape(ranks, 1, -1)
    return lax.all_to_all(flat, axis, 0, 0, tiled=True).reshape(-1, LANES)


def exchange_chips(message, ranks, axis):
    def send(array, step):
        return lax.ppermute(array, axis, [(i, i ^ step) for i in range(ranks)])

    chips = range(1, ranks // 2)
    early = chips[3 - 1]
    near_chip = send(message, 2 * early)
    other = send(message, 1)
    both = jnp.concatenate([message, other])
    layout, arrays = [(0, (False, True))], [both]
    for k in chips:
        if k != early:
            layout.append((k, (False, True)))
            arrays.append(send(both, 2 * k))
    layout += [(early, (False,)), (early, (True,))]
    arrays += [near_chip, send(near_chip, 1)]
    return layout, arrays


def on_device(x_ranks, y_ranks, fields, viscosity, diffusivity):
    _, _, x_cells, y_cells = fields.shape
    blocks = y_cells // LANES
    half_x, half_y = 0.5 * float(x_cells * x_cells), 0.5 * float(y_cells * y_cells)
    x_rows, y_rows = QUANTITIES * blocks, QUANTITIES
    x_count, y_count = x_cells // SUB, y_cells // SUB
    args = [tiles(a) for a in (fields, viscosity, diffusivity)]
    sizes = [a.shape for a in args]
    in_hbm = [pltpu.with_memory_space_constraint(a, pltpu.HBM) for a in args]

    message, x_weights, x_pushed = call(
        functools.partial(x_ends_kernel, half_x, x_cells, blocks, x_ranks, x_rows),
        [
            near((x_ranks * x_rows, LANES)),
            near((2, blocks, weight_rows(x_count), LANES)),
            near((FIELDS, blocks, source_rows(x_count), LANES)),
        ],
        [(x_rows, LANES), *sizes, pltpu.SemaphoreType.DMA((2 + FIELDS,))], "x_ends",
        in_specs=[pl.BlockSpec(memory_space=pltpu.HBM)] * 3,
    )(*in_hbm)
    received = exchange(message, x_ranks, "gx")
    message, y_weights, y_pushed = call(
        functools.partial(x_join_kernel, half_x, half_y, x_cells, blocks, "gx", x_ranks, x_rows),
        [
            near((y_rows, LANES)),
            near((2, weight_rows(y_count), LANES)),
            near((FIELDS, source_rows(y_count), LANES)),
        ],
        [(x_ranks * spaced(x_rows), LANES)],
        "x_join",
    )(received, x_weights, x_pushed, *args[1:])
    layout, chips = exchange_chips(message, y_ranks, "gy")
    (updated,) = call(
        functools.partial(y_join_kernel, half_y, x_cells, blocks, "gy", y_ranks, y_rows, layout),
        [far(sizes[0])],
        [(y_ranks * spaced(y_rows), LANES), sizes[0], pltpu.SemaphoreType.DMA((FIELDS,))], "y_join",
        out_specs=[pl.BlockSpec(memory_space=pltpu.HBM)],
    )(*chips, y_weights, y_pushed)
    return untiles(updated, fields.shape)


def solution(mesh):
    placed = (P(None, None, "gx", "gy"), P(None, "gx", "gy"), P(None, "gx", "gy"))
    return jax.shard_map(
        functools.partial(on_device, mesh.shape["gx"], mesh.shape["gy"]),
        mesh=mesh, in_specs=placed, out_specs=P(None, None, "gx", "gy"), check_vma=False,
    )
```

```python
import functools

import jax
import jax.numpy as jnp
from jax import lax
from jax.experimental import pallas as pl
from jax.experimental.pallas import tpu as pltpu
from jax.sharding import PartitionSpec as P


FIELDS = 4
KIND = (0, 0, 0, 1)
LANES = 128
SUB = 8
COEF_ROWS = 5
QUANTITIES = 2 * COEF_ROWS + 2 * FIELDS


def recip(value):
    return pl.reciprocal(value, approx=True)


def up(rows, step):
    step %= rows.shape[0]
    return pltpu.roll(rows, rows.shape[0] - step, 0) if step else rows


def down(rows, step):
    return pltpu.roll(rows, step, 0)


def row_index(rows):
    return lax.broadcasted_iota(jnp.int32, (rows, LANES), 0)


def pair(left, ground_u, link, ground_v, right):
    total_u, total_v = left + ground_u, right + ground_v
    scale = recip(total_u * total_v + link * (total_u + total_v))
    return (total_v + link) * scale, link * scale, (total_u + link) * scale


def join_two(low, face, high):
    link, ground_a, ground_u = low
    right, ground_v, ground_b = high
    uu, uv, vv = pair(link, ground_u, face, ground_v, right)
    u_left, v_left, u_right, v_right = link * uu, link * uv, right * uv, right * vv
    joined = (
        v_left * right,
        ground_a + ground_u * u_left + ground_v * v_left,
        ground_b + ground_u * u_right + ground_v * v_right,
    )
    return joined, (uu, uv, vv, u_left, v_left, u_right, v_right)


def join_two_sources(low, weights, high):
    _, _, _, u_left, v_left, u_right, v_right = weights
    (source_a, source_u), (source_v, source_b) = low, high
    return (
        source_a + source_u * u_left + source_v * v_left,
        source_b + source_u * u_right + source_v * v_right,
    )


def shifted(arrays, shift):
    return [up(x, shift) for x in arrays]


def join(chain, face, shift):
    return join_two(chain, face, shifted(chain, shift))


def join_sources(ends, weights, shift):
    return join_two_sources(ends, weights, shifted(ends, shift))


def schedule(count):
    nodes, rounds = list(range(count)), []
    while len(nodes) > 2:
        gone = range(1, len(nodes) - 1, 2)
        rounds.append([(nodes[i], nodes[i - 1], nodes[i + 1]) for i in gone])
        nodes = [n for i, n in enumerate(nodes) if i not in gone]
    return rounds


SHIFTS = (1, 2, 4)


def eliminate(coefs, half):
    count = len(coefs)
    ground = [1.0] * count
    link = {i: half * (coefs[i] + coefs[i + 1]) for i in range(count - 1)}
    cells, scales = {}, {}
    for round_ in schedule(count):
        for cell, low, high in round_:
            scale = recip(link[low] + link[cell] + ground[cell])
            to_low, to_high = link[low] * scale, link[cell] * scale
            ground[low] = ground[low] + to_low * ground[cell]
            ground[high] = ground[high] + to_high * ground[cell]
            link[low] = to_low * link[cell]
            cells[cell], scales[cell] = (to_low, to_high), scale
    face = half * (coefs[-1] + up(coefs[0], 1))
    chain, joins = (link[0], ground[0], ground[-1]), []
    for shift in SHIFTS:
        chain, weights = join(chain, up(face, shift - 1), shift)
        joins.append(weights)
    return cells, scales, joins, chain


def push_sources(cells, scales, joins, sources):
    sources, scaled = list(sources), {}
    for round_ in schedule(len(sources)):
        for cell, low, high in round_:
            to_low, to_high = cells[cell]
            sources[low] = sources[low] + to_low * sources[cell]
            sources[high] = sources[high] + to_high * sources[cell]
            scaled[cell] = scales[cell] * sources[cell]
    ends, joined = (sources[0], sources[-1]), []
    for shift, weights in zip(SHIFTS, joins):
        uu, uv, vv = weights[:3]
        source_u, source_v = ends[1], up(ends[0], shift)
        joined.append((uu * source_u + uv * source_v, uv * source_u + vv * source_v))
        ends = join_sources(ends, weights, shift)
    return scaled, joined, ends


def pull_values(cells, joins, scaled, joined, end_a, end_b):
    row = row_index(SUB)
    for shift, (u_left, v_left, u_right, v_right), (from_u, from_v) in reversed(list(zip(SHIFTS, joins, joined))):
        value_u = from_u + u_left * end_a + u_right * end_b
        value_v = from_v + v_left * end_a + v_right * end_b
        on_right = (row // shift) % 2 == 1
        end_a = jnp.where(on_right, down(value_v, shift), end_a)
        end_b = jnp.where(on_right, down(end_b, shift), value_u)
    count = len(cells) + 2
    values = {0: end_a, count - 1: end_b}
    for round_ in reversed(schedule(count)):
        for cell, low, high in round_:
            to_low, to_high = cells[cell]
            values[cell] = scaled[cell] + to_low * values[low] + to_high * values[high]
    return [values[t] for t in range(count)]


def weight_rows(count):
    return (2 * (count - 2) + 4 * len(SHIFTS)) * SUB


def source_rows(count):
    return (count - 2 + 2 * len(SHIFTS)) * SUB


def save(ref, arrays):
    for i, array in enumerate(arrays):
        ref[pl.ds(i * SUB, SUB), :] = array


def save_weights(ref, cells, joins):
    save(ref, [w for c in sorted(cells) for w in cells[c]] + [w for weights in joins for w in weights[3:]])


def save_sources(ref, scaled, joined):
    save(ref, [scaled[c] for c in sorted(scaled)] + [v for two in joined for v in two])


def load_weights(ref, count):
    def at(i):
        return ref[pl.ds(i * SUB, SUB), :]

    base = 2 * (count - 2)
    cells = {c: (at(2 * c - 2), at(2 * c - 1)) for c in range(1, count - 1)}
    return cells, [tuple(at(base + 4 * j + i) for i in range(4)) for j in range(len(SHIFTS))]


def load_sources(ref, count):
    def at(i):
        return ref[pl.ds(i * SUB, SUB), :]

    base = count - 2
    return {c: at(c - 1) for c in range(1, count - 1)}, [
        (at(base + 2 * j), at(base + 2 * j + 1)) for j in range(len(SHIFTS))
    ]


def spread(row):
    return jnp.broadcast_to(row[:1], (SUB, LANES))


def to_cells(rows):
    parts = jnp.swapaxes(rows.reshape(SUB, -1, LANES), 0, 1)
    return [parts[t] for t in range(parts.shape[0])]


def from_cells(cells):
    return jnp.swapaxes(jnp.stack(cells), 0, 1).reshape(-1, LANES)


def tiles(array):
    x_cells, y_cells = array.shape[-2:]
    split = array.reshape(-1, x_cells // SUB, SUB, y_cells // LANES, LANES)
    return split.transpose(0, 1, 3, 2, 4).reshape(-1, LANES)


def untiles(flat, shape):
    split = flat.reshape(-1, shape[-2] // SUB, shape[-1] // LANES, SUB, LANES)
    return split.transpose(0, 1, 3, 2, 4).reshape(shape)


def tile_at(field, x_tile, block, x_cells, blocks):
    return ((field * (x_cells // SUB) + x_tile) * blocks + block) * SUB


def load_x_cells(ref, field, x_cells, blocks):
    parts = to_cells(ref[pl.ds(field * x_cells * blocks, x_cells * blocks), :])
    return [
        [parts[(t // SUB * blocks + block) * SUB + t % SUB] for t in range(x_cells // SUB)] for block in range(blocks)
    ]


def load_block(ref, field, block, x_cells, blocks):
    return jnp.concatenate(
        [ref[pl.ds(tile_at(field, i, block, x_cells, blocks), SUB), :] for i in range(x_cells // SUB)]
    )


def solve_ring(quantity, ranks, rank, half):
    step = max(1, ranks // SUB)
    count = ranks // step
    device = [lax.rem(row_index(count) * step + (rank + 1 + k), ranks) for k in range(step)]
    last_row = row_index(count) == count - 1
    results = []
    for kind in range(2):
        chains, sources, first_coefs, last_coefs = [], [], [], []
        fields = [f for f in range(FIELDS) if KIND[f] == kind]
        for k in range(step):
            first, last, link, ground_a, ground_b = [
                quantity(kind * COEF_ROWS + i, k, step) for i in range(COEF_ROWS)
            ]
            ground_a = ground_a + jnp.where(device[k] == 0, half * first, 0.0)
            ground_b = ground_b + jnp.where(device[k] == ranks - 1, half * last, 0.0)
            chains.append((link, ground_a, ground_b))
            first_coefs.append(first)
            last_coefs.append(last)
            sources.append([[quantity(2 * COEF_ROWS + 2 * f + end, k, step) for end in range(2)] for f in fields])
        first_coefs.append(up(first_coefs[0], 1))
        faces = [
            jnp.where(device[k] == ranks - 1, 0.0, half * (last_coefs[k] + first_coefs[k + 1])) for k in range(step)
        ]
        own = shifted(chains[-1], count - 1)
        own_sources = [shifted(s, count - 1) for s in sources[-1]]
        left = up(faces[-1], count - 1)
        right = up(faces[step - 2], count - 1) if step > 1 else up(faces[0], count - 2)

        if step == 1:
            (chain,), (ends,), shift = chains, sources, 1
        else:
            joined, weights = join_two(chains[0], faces[0], chains[1])
            chain = [jnp.where(last_row, a, b) for a, b in zip(chains[0], joined)]
            ends = [
                [jnp.where(last_row, a, b) for a, b in zip(low, join_two_sources(low, weights, high))]
                for low, high in zip(*sources)
            ]
            shift = 1
        while shift < count:
            joined, weights = join(chain, up(faces[-1], shift - 1), shift)
            joined_ends = [join_sources(s, weights, shift) for s in ends]
            if shift == 1 and step == 1:
                alone = row_index(count) == count - 2
                joined = [jnp.where(alone, a, b) for a, b in zip(chain, joined)]
                joined_ends = [[jnp.where(alone, a, b) for a, b in zip(*two)] for two in zip(ends, joined_ends)]
            chain, ends, shift = joined, joined_ends, 2 * shift
        link, ground_u, ground_v = chain
        uu, uv, vv = pair(left, ground_u, link, ground_v, right)
        u_b, v_b, u_a, v_a = left * uu, left * uv, right * uv, right * vv
        link = own[0] + v_b * right
        ground_a = own[1] + ground_u * u_a + ground_v * v_a
        ground_b = own[2] + ground_u * u_b + ground_v * v_b
        scale = recip(ground_a * ground_b + link * (ground_a + ground_b))
        aa, ab, bb = (ground_b + link) * scale, link * scale, (ground_a + link) * scale
        for (source_u, source_v), (source_a, source_b) in zip(ends, own_sources):
            source_a = source_a + source_u * u_a + source_v * v_a
            source_b = source_b + source_u * u_b + source_v * v_b
            results.append((aa * source_a + ab * source_b, ab * source_a + bb * source_b))
    return results


def received_rows(turned, ranks, rows, blocks, block):
    def quantity(q, k, step):
        at = k * spaced(rows) + q * blocks + block
        return turned[pl.ds(at, ranks // step, stride=step * spaced(rows)), :]

    return quantity


def spaced(rows):
    return rows | 1


def slot(device, ranks):
    return ranks - 1 - device


def rotate(received, turned, ranks, rows, rank):
    for k in range(ranks):
        source = slot(lax.rem(rank + 1 + k, ranks), ranks) * rows
        turned[pl.ds(k * spaced(rows), rows), :] = received[pl.ds(source, rows), :]


def place(parts, turned, ranks, rows, rank):
    for k, other, message in parts:
        chip = lax.bitwise_xor(lax.div(rank, 2), k)
        device = 2 * chip + lax.bitwise_xor(lax.rem(rank, 2), int(other))
        at = lax.rem(device + ranks - rank - 1, ranks) * spaced(rows)
        turned[pl.ds(at, rows), :] = message


def coef_rows(coefs, chain):
    return (coefs[0][:1], coefs[-1][SUB - 1 :], chain[0][:1], chain[1][:1], chain[2][:1])


def x_ends_kernel(
    half, x_cells, blocks, ranks, rows,
    fields, viscosity, diffusivity, message, weights, pushed,
    line, fields_here, viscosity_here, diffusivity_here, arrived,
):
    per_field = x_cells * blocks
    copies = [
        pltpu.make_async_copy(viscosity, viscosity_here, arrived.at[0]),
        pltpu.make_async_copy(diffusivity, diffusivity_here, arrived.at[1]),
    ]
    for f in range(FIELDS):
        part = pl.ds(f * per_field, per_field)
        copies.append(pltpu.make_async_copy(fields.at[part], fields_here.at[part], arrived.at[2 + f]))
    for copy in copies:
        copy.start()

    def put(quantity, block, value):
        at = quantity * blocks + block
        line[at : at + 1, :] = value

    plans = {}
    for copy in copies[:2]:
        copy.wait()
    for kind, coef in enumerate((viscosity_here, diffusivity_here)):
        for block, coefs in enumerate(load_x_cells(coef, 0, x_cells, blocks)):
            *plan, chain = eliminate(coefs, half)
            plans[kind, block] = plan
            save_weights(weights.at[kind, block], plan[0], plan[2])
            for i, value in enumerate(coef_rows(coefs, chain)):
                put(kind * COEF_ROWS + i, block, value)
    for copy in copies[2:]:
        copy.wait()
    for f in range(FIELDS):
        for block, sources in enumerate(load_x_cells(fields_here, f, x_cells, blocks)):
            scaled, joined, ends = push_sources(*plans[KIND[f], block], sources)
            save_sources(pushed.at[f, block], scaled, joined)
            put(2 * COEF_ROWS + 2 * f, block, ends[0][:1])
            put(2 * COEF_ROWS + 2 * f + 1, block, ends[1][:1])
    for k in range(ranks):
        message[pl.ds(k * rows, rows), :] = line[...]


def x_join_kernel(
    half_x, half_y, x_cells, blocks, axis, ranks, rows,
    received, x_weights, x_pushed, viscosity, diffusivity, message, weights, pushed,
    turned,
):
    rank = lax.axis_index(axis)
    count, y_count = x_cells // SUB, blocks * LANES // SUB
    rotate(received, turned, ranks, rows, rank)
    plans = []
    for kind, coef in enumerate((viscosity, diffusivity)):
        coefs = to_cells(jnp.concatenate([load_block(coef, 0, b, x_cells, blocks).T for b in range(blocks)]))
        *plan, chain = eliminate(coefs, half_y)
        plans.append(plan)
        save_weights(weights.at[kind], plan[0], plan[2])
        for i, value in enumerate(coef_rows(coefs, chain)):
            message[kind * COEF_ROWS + i : kind * COEF_ROWS + i + 1, :] = value
    lines = [[] for _ in range(FIELDS)]
    for block in range(blocks):
        ends = solve_ring(received_rows(turned, ranks, rows, blocks, block), ranks, rank, half_x)
        for f in range(FIELDS):
            end_a, end_b = [spread(e) for e in ends[f]]
            values = pull_values(
                *load_weights(x_weights.at[KIND[f], block], count), *load_sources(x_pushed.at[f, block], count), end_a, end_b
            )
            lines[f].append(from_cells(values).T)
    for f in range(FIELDS):
        scaled, joined, ends = push_sources(*plans[KIND[f]], to_cells(jnp.concatenate(lines[f])))
        save_sources(pushed.at[f], scaled, joined)
        at = 2 * COEF_ROWS + 2 * f
        message[at : at + 1, :] = ends[0][:1]
        message[at + 1 : at + 2, :] = ends[1][:1]


def y_join_kernel(
    half, x_cells, blocks, axis, ranks, rows, layout,
    *refs,
):
    *chips, weights, pushed, updated, turned, here, left = refs
    per_field = x_cells * blocks
    count = blocks * LANES // SUB
    rank = lax.axis_index(axis)
    parts = []
    for (k, others), ref in zip(layout, chips):
        for i, other in enumerate(others):
            parts.append((k, other, ref[pl.ds(i * rows, rows), :]))
    place(parts, turned, ranks, rows, rank)
    ends = solve_ring(received_rows(turned, ranks, rows, 1, 0), ranks, rank, half)
    copies = []
    for f in range(FIELDS):
        end_a, end_b = [spread(e) for e in ends[f]]
        values = pull_values(
            *load_weights(weights.at[KIND[f]], count), *load_sources(pushed.at[f], count), end_a, end_b
        )
        lines = from_cells(values)
        for block in range(blocks):
            value = lines[block * LANES : (block + 1) * LANES].T
            for i in range(x_cells // SUB):
                here[pl.ds(tile_at(f, i, block, x_cells, blocks), SUB), :] = value[i * SUB : (i + 1) * SUB]
        part = pl.ds(f * per_field, per_field)
        copies.append(pltpu.make_async_copy(here.at[part], updated.at[part], left.at[f]))
        copies[-1].start()
    for copy in copies:
        copy.wait()


def call(kernel, outs, scratch, name, **kw):
    return pl.pallas_call(
        kernel,
        out_shape=outs,
        scratch_shapes=[pltpu.VMEM(s, jnp.float32) if isinstance(s, tuple) else s for s in scratch],
        compiler_params=pltpu.CompilerParams(vmem_limit_bytes=24 * 1024 * 1024),
        name=name,
        **kw,
    )


def near(shape):
    return pltpu.VMEM(shape, jnp.float32)


def far(shape):
    return pltpu.HBM(shape, jnp.float32)


def exchange(message, ranks, axis):
    flat = message.reshape(ranks, 1, -1)
    order = sorted(range(ranks), key=lambda device: slot(device, ranks))
    return lax.all_to_all(flat, axis, 0, 0, tiled=True, axis_index_groups=[order]).reshape(-1, LANES)


def exchange_chips(message, ranks, axis):
    def send(array, step):
        return lax.ppermute(array, axis, [(i, i ^ step) for i in range(ranks)])

    chips = range(1, ranks // 2)
    early = chips[3 - 1]
    near_chip = send(message, 2 * early)
    other = send(message, 1)
    both = jnp.concatenate([message, other])
    layout, arrays = [(0, (False, True))], [both]
    for k in chips:
        if k != early:
            layout.append((k, (False, True)))
            arrays.append(send(both, 2 * k))
    layout += [(early, (False,)), (early, (True,))]
    arrays += [near_chip, send(near_chip, 1)]
    return layout, arrays


def on_device(x_ranks, y_ranks, fields, viscosity, diffusivity):
    _, _, x_cells, y_cells = fields.shape
    blocks = y_cells // LANES
    half_x, half_y = 0.5 * float(x_cells * x_cells), 0.5 * float(y_cells * y_cells)
    x_rows, y_rows = QUANTITIES * blocks, QUANTITIES
    x_count, y_count = x_cells // SUB, y_cells // SUB
    args = [tiles(a) for a in (fields, viscosity, diffusivity)]
    sizes = [a.shape for a in args]
    in_hbm = [pltpu.with_memory_space_constraint(a, pltpu.HBM) for a in args]

    message, x_weights, x_pushed = call(
        functools.partial(x_ends_kernel, half_x, x_cells, blocks, x_ranks, x_rows),
        [
            near((x_ranks * x_rows, LANES)),
            near((2, blocks, weight_rows(x_count), LANES)),
            near((FIELDS, blocks, source_rows(x_count), LANES)),
        ],
        [(x_rows, LANES), *sizes, pltpu.SemaphoreType.DMA((2 + FIELDS,))], "x_ends",
        in_specs=[pl.BlockSpec(memory_space=pltpu.HBM)] * 3,
    )(*in_hbm)
    received = exchange(message, x_ranks, "gx")
    message, y_weights, y_pushed = call(
        functools.partial(x_join_kernel, half_x, half_y, x_cells, blocks, "gx", x_ranks, x_rows),
        [
            near((y_rows, LANES)),
            near((2, weight_rows(y_count), LANES)),
            near((FIELDS, source_rows(y_count), LANES)),
        ],
        [(x_ranks * spaced(x_rows), LANES)],
        "x_join",
    )(received, x_weights, x_pushed, *args[1:])
    layout, chips = exchange_chips(message, y_ranks, "gy")
    (updated,) = call(
        functools.partial(y_join_kernel, half_y, x_cells, blocks, "gy", y_ranks, y_rows, layout),
        [far(sizes[0])],
        [(y_ranks * spaced(y_rows), LANES), sizes[0], pltpu.SemaphoreType.DMA((FIELDS,))], "y_join",
        out_specs=[pl.BlockSpec(memory_space=pltpu.HBM)],
    )(*chips, y_weights, y_pushed)
    return untiles(updated, fields.shape)


def solution(mesh):
    placed = (P(None, None, "gx", "gy"), P(None, "gx", "gy"), P(None, "gx", "gy"))
    return jax.shard_map(
        functools.partial(on_device, mesh.shape["gx"], mesh.shape["gy"]),
        mesh=mesh, in_specs=placed, out_specs=P(None, None, "gx", "gy"), check_vma=False,
    )
```

```python
import functools

import jax
import jax.numpy as jnp
from jax import lax
from jax.experimental import pallas as pl
from jax.experimental.pallas import tpu as pltpu
from jax.sharding import PartitionSpec as P


FIELDS = 4
KIND = (0, 0, 0, 1)
LANES = 128
SUB = 8
COEF_ROWS = 5
QUANTITIES = 2 * COEF_ROWS + 2 * FIELDS


def recip(value):
    return pl.reciprocal(value, approx=True)


def up(rows, step):
    step %= rows.shape[0]
    return pltpu.roll(rows, rows.shape[0] - step, 0) if step else rows


def down(rows, step):
    return pltpu.roll(rows, step, 0)


def row_index(rows):
    return lax.broadcasted_iota(jnp.int32, (rows, LANES), 0)


def pair(left, ground_u, link, ground_v, right):
    total_u, total_v = left + ground_u, right + ground_v
    scale = recip(total_u * total_v + link * (total_u + total_v))
    return (total_v + link) * scale, link * scale, (total_u + link) * scale


def join_two(low, face, high):
    link, ground_a, ground_u = low
    right, ground_v, ground_b = high
    uu, uv, vv = pair(link, ground_u, face, ground_v, right)
    u_left, v_left, u_right, v_right = link * uu, link * uv, right * uv, right * vv
    joined = (
        v_left * right,
        ground_a + ground_u * u_left + ground_v * v_left,
        ground_b + ground_u * u_right + ground_v * v_right,
    )
    return joined, (uu, uv, vv, u_left, v_left, u_right, v_right)


def join_two_sources(low, weights, high):
    _, _, _, u_left, v_left, u_right, v_right = weights
    (source_a, source_u), (source_v, source_b) = low, high
    return (
        source_a + source_u * u_left + source_v * v_left,
        source_b + source_u * u_right + source_v * v_right,
    )


def shifted(arrays, shift):
    return [up(x, shift) for x in arrays]


def join(chain, face, shift):
    return join_two(chain, face, shifted(chain, shift))


def join_sources(ends, weights, shift):
    return join_two_sources(ends, weights, shifted(ends, shift))


def schedule(count):
    nodes, rounds = list(range(count)), []
    while len(nodes) > 2:
        gone = range(1, len(nodes) - 1, 2)
        rounds.append([(nodes[i], nodes[i - 1], nodes[i + 1]) for i in gone])
        nodes = [n for i, n in enumerate(nodes) if i not in gone]
    return rounds


SHIFTS = (1, 2, 4)


def eliminate(coefs, half):
    count = len(coefs)
    ground = [1.0] * count
    link = {i: half * (coefs[i] + coefs[i + 1]) for i in range(count - 1)}
    cells, scales = {}, {}
    for round_ in schedule(count):
        for cell, low, high in round_:
            scale = recip(link[low] + link[cell] + ground[cell])
            to_low, to_high = link[low] * scale, link[cell] * scale
            ground[low] = ground[low] + to_low * ground[cell]
            ground[high] = ground[high] + to_high * ground[cell]
            link[low] = to_low * link[cell]
            cells[cell], scales[cell] = (to_low, to_high), scale
    face = half * (coefs[-1] + up(coefs[0], 1))
    chain, joins = (link[0], ground[0], ground[-1]), []
    for shift in SHIFTS:
        chain, weights = join(chain, up(face, shift - 1), shift)
        joins.append(weights)
    return cells, scales, joins, chain


def push_sources(cells, scales, joins, sources):
    sources, scaled = list(sources), {}
    for round_ in schedule(len(sources)):
        for cell, low, high in round_:
            to_low, to_high = cells[cell]
            sources[low] = sources[low] + to_low * sources[cell]
            sources[high] = sources[high] + to_high * sources[cell]
            scaled[cell] = scales[cell] * sources[cell]
    ends, joined = (sources[0], sources[-1]), []
    for shift, weights in zip(SHIFTS, joins):
        uu, uv, vv = weights[:3]
        source_u, source_v = ends[1], up(ends[0], shift)
        joined.append((uu * source_u + uv * source_v, uv * source_u + vv * source_v))
        ends = join_sources(ends, weights, shift)
    return scaled, joined, ends


def pull_values(cells, joins, scaled, joined, end_a, end_b):
    row = row_index(SUB)
    for shift, (u_left, v_left, u_right, v_right), (from_u, from_v) in reversed(list(zip(SHIFTS, joins, joined))):
        value_u = from_u + u_left * end_a + u_right * end_b
        value_v = from_v + v_left * end_a + v_right * end_b
        on_right = (row // shift) % 2 == 1
        end_a = jnp.where(on_right, down(value_v, shift), end_a)
        end_b = jnp.where(on_right, down(end_b, shift), value_u)
    count = len(cells) + 2
    values = {0: end_a, count - 1: end_b}
    for round_ in reversed(schedule(count)):
        for cell, low, high in round_:
            to_low, to_high = cells[cell]
            values[cell] = scaled[cell] + to_low * values[low] + to_high * values[high]
    return [values[t] for t in range(count)]


def weight_rows(count):
    return (2 * (count - 2) + 4 * len(SHIFTS)) * SUB


def source_rows(count):
    return (count - 2 + 2 * len(SHIFTS)) * SUB


def save(ref, arrays):
    for i, array in enumerate(arrays):
        ref[pl.ds(i * SUB, SUB), :] = array


def save_weights(ref, cells, joins):
    save(ref, [w for c in sorted(cells) for w in cells[c]] + [w for weights in joins for w in weights[3:]])


def save_sources(ref, scaled, joined):
    save(ref, [scaled[c] for c in sorted(scaled)] + [v for two in joined for v in two])


def load_weights(ref, count):
    def at(i):
        return ref[pl.ds(i * SUB, SUB), :]

    base = 2 * (count - 2)
    cells = {c: (at(2 * c - 2), at(2 * c - 1)) for c in range(1, count - 1)}
    return cells, [tuple(at(base + 4 * j + i) for i in range(4)) for j in range(len(SHIFTS))]


def load_sources(ref, count):
    def at(i):
        return ref[pl.ds(i * SUB, SUB), :]

    base = count - 2
    return {c: at(c - 1) for c in range(1, count - 1)}, [
        (at(base + 2 * j), at(base + 2 * j + 1)) for j in range(len(SHIFTS))
    ]


def spread(row):
    return jnp.broadcast_to(row[:1], (SUB, LANES))


def to_cells(rows):
    parts = jnp.swapaxes(rows.reshape(SUB, -1, LANES), 0, 1)
    return [parts[t] for t in range(parts.shape[0])]


def from_cells(cells):
    return jnp.swapaxes(jnp.stack(cells), 0, 1).reshape(-1, LANES)


def tiles(array):
    x_cells, y_cells = array.shape[-2:]
    split = array.reshape(-1, x_cells // SUB, SUB, y_cells // LANES, LANES)
    return split.transpose(0, 1, 3, 2, 4).reshape(-1, LANES)


def untiles(flat, shape):
    split = flat.reshape(-1, shape[-2] // SUB, shape[-1] // LANES, SUB, LANES)
    return split.transpose(0, 1, 3, 2, 4).reshape(shape)


def tile_at(field, x_tile, block, x_cells, blocks):
    return ((field * (x_cells // SUB) + x_tile) * blocks + block) * SUB


def load_x_cells(ref, field, x_cells, blocks):
    parts = to_cells(ref[pl.ds(field * x_cells * blocks, x_cells * blocks), :])
    return [
        [parts[(t // SUB * blocks + block) * SUB + t % SUB] for t in range(x_cells // SUB)] for block in range(blocks)
    ]


def load_block(ref, field, block, x_cells, blocks):
    return jnp.concatenate(
        [ref[pl.ds(tile_at(field, i, block, x_cells, blocks), SUB), :] for i in range(x_cells // SUB)]
    )


def solve_ring(quantity, ranks, rank, half):
    step = max(1, ranks // SUB)
    count = ranks // step
    device = [lax.rem(row_index(count) * step + (rank + 1 + k), ranks) for k in range(step)]
    last_row = row_index(count) == count - 1
    results = []
    for kind in range(2):
        chains, sources, first_coefs, last_coefs = [], [], [], []
        fields = [f for f in range(FIELDS) if KIND[f] == kind]
        for k in range(step):
            first, last, link, ground_a, ground_b = [
                quantity(kind * COEF_ROWS + i, k, step) for i in range(COEF_ROWS)
            ]
            ground_a = ground_a + jnp.where(device[k] == 0, half * first, 0.0)
            ground_b = ground_b + jnp.where(device[k] == ranks - 1, half * last, 0.0)
            chains.append((link, ground_a, ground_b))
            first_coefs.append(first)
            last_coefs.append(last)
            sources.append([[quantity(2 * COEF_ROWS + 2 * f + end, k, step) for end in range(2)] for f in fields])
        first_coefs.append(up(first_coefs[0], 1))
        faces = [
            jnp.where(device[k] == ranks - 1, 0.0, half * (last_coefs[k] + first_coefs[k + 1])) for k in range(step)
        ]
        own = shifted(chains[-1], count - 1)
        own_sources = [shifted(s, count - 1) for s in sources[-1]]
        left = up(faces[-1], count - 1)
        right = up(faces[step - 2], count - 1) if step > 1 else up(faces[0], count - 2)

        if step == 1:
            (chain,), (ends,), shift = chains, sources, 1
        else:
            joined, weights = join_two(chains[0], faces[0], chains[1])
            chain = [jnp.where(last_row, a, b) for a, b in zip(chains[0], joined)]
            ends = [
                [jnp.where(last_row, a, b) for a, b in zip(low, join_two_sources(low, weights, high))]
                for low, high in zip(*sources)
            ]
            shift = 1
        while shift < count:
            joined, weights = join(chain, up(faces[-1], shift - 1), shift)
            joined_ends = [join_sources(s, weights, shift) for s in ends]
            if shift == 1 and step == 1:
                alone = row_index(count) == count - 2
                joined = [jnp.where(alone, a, b) for a, b in zip(chain, joined)]
                joined_ends = [[jnp.where(alone, a, b) for a, b in zip(*two)] for two in zip(ends, joined_ends)]
            chain, ends, shift = joined, joined_ends, 2 * shift
        link, ground_u, ground_v = chain
        uu, uv, vv = pair(left, ground_u, link, ground_v, right)
        u_b, v_b, u_a, v_a = left * uu, left * uv, right * uv, right * vv
        link = own[0] + v_b * right
        ground_a = own[1] + ground_u * u_a + ground_v * v_a
        ground_b = own[2] + ground_u * u_b + ground_v * v_b
        scale = recip(ground_a * ground_b + link * (ground_a + ground_b))
        aa, ab, bb = (ground_b + link) * scale, link * scale, (ground_a + link) * scale
        for (source_u, source_v), (source_a, source_b) in zip(ends, own_sources):
            source_a = source_a + source_u * u_a + source_v * v_a
            source_b = source_b + source_u * u_b + source_v * v_b
            results.append((aa * source_a + ab * source_b, ab * source_a + bb * source_b))
    return results


def received_rows(turned, ranks, rows, blocks, block):
    def quantity(q, k, step):
        at = k * spaced(rows) + q * blocks + block
        return turned[pl.ds(at, ranks // step, stride=step * spaced(rows)), :]

    return quantity


def spaced(rows):
    return rows | 1


def rotate(received, turned, order, rows, rank):
    for at, device in enumerate(order):
        k = lax.rem(device + len(order) - 1 - rank, len(order))
        turned[pl.ds(k * spaced(rows), rows), :] = received[pl.ds(at * rows, rows), :]


def place(parts, turned, ranks, rows, rank):
    for k, other, message in parts:
        chip = lax.bitwise_xor(lax.div(rank, 2), k)
        device = 2 * chip + lax.bitwise_xor(lax.rem(rank, 2), int(other))
        at = lax.rem(device + ranks - rank - 1, ranks) * spaced(rows)
        turned[pl.ds(at, rows), :] = message


def coef_rows(coefs, chain):
    return (coefs[0][:1], coefs[-1][SUB - 1 :], chain[0][:1], chain[1][:1], chain[2][:1])


def x_ends_kernel(
    half, x_cells, blocks, ranks, rows,
    fields, viscosity, diffusivity, message, weights, pushed,
    line, fields_here, viscosity_here, diffusivity_here, arrived,
):
    per_field = x_cells * blocks
    copies = [
        pltpu.make_async_copy(viscosity, viscosity_here, arrived.at[0]),
        pltpu.make_async_copy(diffusivity, diffusivity_here, arrived.at[1]),
    ]
    for f in range(FIELDS):
        part = pl.ds(f * per_field, per_field)
        copies.append(pltpu.make_async_copy(fields.at[part], fields_here.at[part], arrived.at[2 + f]))
    for copy in copies:
        copy.start()

    def put(quantity, block, value):
        at = quantity * blocks + block
        line[at : at + 1, :] = value

    plans = {}
    for copy in copies[:2]:
        copy.wait()
    for kind, coef in enumerate((viscosity_here, diffusivity_here)):
        for block, coefs in enumerate(load_x_cells(coef, 0, x_cells, blocks)):
            *plan, chain = eliminate(coefs, half)
            plans[kind, block] = plan
            save_weights(weights.at[kind, block], plan[0], plan[2])
            for i, value in enumerate(coef_rows(coefs, chain)):
                put(kind * COEF_ROWS + i, block, value)
    for copy in copies[2:]:
        copy.wait()
    for f in range(FIELDS):
        for block, sources in enumerate(load_x_cells(fields_here, f, x_cells, blocks)):
            scaled, joined, ends = push_sources(*plans[KIND[f], block], sources)
            save_sources(pushed.at[f, block], scaled, joined)
            put(2 * COEF_ROWS + 2 * f, block, ends[0][:1])
            put(2 * COEF_ROWS + 2 * f + 1, block, ends[1][:1])
    for k in range(ranks):
        message[pl.ds(k * rows, rows), :] = line[...]


def x_join_kernel(
    half_x, half_y, x_cells, blocks, axis, order, rows,
    received, x_weights, x_pushed, viscosity, diffusivity, message, weights, pushed,
    turned,
):
    rank = lax.axis_index(axis)
    count, y_count = x_cells // SUB, blocks * LANES // SUB
    rotate(received, turned, order, rows, rank)
    ranks = len(order)
    plans = []
    for kind, coef in enumerate((viscosity, diffusivity)):
        coefs = to_cells(jnp.concatenate([load_block(coef, 0, b, x_cells, blocks).T for b in range(blocks)]))
        *plan, chain = eliminate(coefs, half_y)
        plans.append(plan)
        save_weights(weights.at[kind], plan[0], plan[2])
        for i, value in enumerate(coef_rows(coefs, chain)):
            message[kind * COEF_ROWS + i : kind * COEF_ROWS + i + 1, :] = value
    lines = [[] for _ in range(FIELDS)]
    for block in range(blocks):
        ends = solve_ring(received_rows(turned, ranks, rows, blocks, block), ranks, rank, half_x)
        for f in range(FIELDS):
            end_a, end_b = [spread(e) for e in ends[f]]
            values = pull_values(
                *load_weights(x_weights.at[KIND[f], block], count), *load_sources(x_pushed.at[f, block], count), end_a, end_b
            )
            lines[f].append(from_cells(values).T)
    for f in range(FIELDS):
        scaled, joined, ends = push_sources(*plans[KIND[f]], to_cells(jnp.concatenate(lines[f])))
        save_sources(pushed.at[f], scaled, joined)
        at = 2 * COEF_ROWS + 2 * f
        message[at : at + 1, :] = ends[0][:1]
        message[at + 1 : at + 2, :] = ends[1][:1]


def y_join_kernel(
    half, x_cells, blocks, axis, ranks, rows, layout,
    *refs,
):
    *chips, weights, pushed, updated, turned, here, left = refs
    per_field = x_cells * blocks
    count = blocks * LANES // SUB
    rank = lax.axis_index(axis)
    parts = []
    for (k, others), ref in zip(layout, chips):
        for i, other in enumerate(others):
            parts.append((k, other, ref[pl.ds(i * rows, rows), :]))
    place(parts, turned, ranks, rows, rank)
    ends = solve_ring(received_rows(turned, ranks, rows, 1, 0), ranks, rank, half)
    copies = []
    for f in range(FIELDS):
        end_a, end_b = [spread(e) for e in ends[f]]
        values = pull_values(
            *load_weights(weights.at[KIND[f]], count), *load_sources(pushed.at[f], count), end_a, end_b
        )
        lines = from_cells(values)
        for block in range(blocks):
            value = lines[block * LANES : (block + 1) * LANES].T
            for i in range(x_cells // SUB):
                here[pl.ds(tile_at(f, i, block, x_cells, blocks), SUB), :] = value[i * SUB : (i + 1) * SUB]
        part = pl.ds(f * per_field, per_field)
        copies.append(pltpu.make_async_copy(here.at[part], updated.at[part], left.at[f]))
        copies[-1].start()
    for copy in copies:
        copy.wait()


def call(kernel, outs, scratch, name, **kw):
    return pl.pallas_call(
        kernel,
        out_shape=outs,
        scratch_shapes=[pltpu.VMEM(s, jnp.float32) if isinstance(s, tuple) else s for s in scratch],
        compiler_params=pltpu.CompilerParams(vmem_limit_bytes=24 * 1024 * 1024),
        name=name,
        **kw,
    )


def near(shape):
    return pltpu.VMEM(shape, jnp.float32)


def far(shape):
    return pltpu.HBM(shape, jnp.float32)


def exchange(message, order, axis):
    flat = message.reshape(len(order), 1, -1)
    return lax.all_to_all(flat, axis, 0, 0, tiled=True, axis_index_groups=[list(order)]).reshape(-1, LANES)


def first_in_line(ranks, first):
    return (first, *(device for device in range(ranks) if device != first))


def exchange_chips(message, ranks, axis):
    def send(array, step):
        return lax.ppermute(array, axis, [(i, i ^ step) for i in range(ranks)])

    chips = range(1, ranks // 2)
    early = chips[3 - 1]
    near_chip = send(message, 2 * early)
    other = send(message, 1)
    both = jnp.concatenate([message, other])
    layout, arrays = [(0, (False, True))], [both]
    for k in chips:
        if k != early:
            layout.append((k, (False, True)))
            arrays.append(send(both, 2 * k))
    layout += [(early, (False,)), (early, (True,))]
    arrays += [near_chip, send(near_chip, 1)]
    return layout, arrays


def on_device(x_ranks, y_ranks, fields, viscosity, diffusivity):
    _, _, x_cells, y_cells = fields.shape
    blocks = y_cells // LANES
    half_x, half_y = 0.5 * float(x_cells * x_cells), 0.5 * float(y_cells * y_cells)
    x_rows, y_rows = QUANTITIES * blocks, QUANTITIES
    x_order = first_in_line(x_ranks, 10)
    x_count, y_count = x_cells // SUB, y_cells // SUB
    args = [tiles(a) for a in (fields, viscosity, diffusivity)]
    sizes = [a.shape for a in args]
    in_hbm = [pltpu.with_memory_space_constraint(a, pltpu.HBM) for a in args]

    message, x_weights, x_pushed = call(
        functools.partial(x_ends_kernel, half_x, x_cells, blocks, x_ranks, x_rows),
        [
            near((x_ranks * x_rows, LANES)),
            near((2, blocks, weight_rows(x_count), LANES)),
            near((FIELDS, blocks, source_rows(x_count), LANES)),
        ],
        [(x_rows, LANES), *sizes, pltpu.SemaphoreType.DMA((2 + FIELDS,))], "x_ends",
        in_specs=[pl.BlockSpec(memory_space=pltpu.HBM)] * 3,
    )(*in_hbm)
    received = exchange(message, x_order, "gx")
    message, y_weights, y_pushed = call(
        functools.partial(x_join_kernel, half_x, half_y, x_cells, blocks, "gx", x_order, x_rows),
        [
            near((y_rows, LANES)),
            near((2, weight_rows(y_count), LANES)),
            near((FIELDS, source_rows(y_count), LANES)),
        ],
        [(x_ranks * spaced(x_rows), LANES)],
        "x_join",
    )(received, x_weights, x_pushed, *args[1:])
    layout, chips = exchange_chips(message, y_ranks, "gy")
    (updated,) = call(
        functools.partial(y_join_kernel, half_y, x_cells, blocks, "gy", y_ranks, y_rows, layout),
        [far(sizes[0])],
        [(y_ranks * spaced(y_rows), LANES), sizes[0], pltpu.SemaphoreType.DMA((FIELDS,))], "y_join",
        out_specs=[pl.BlockSpec(memory_space=pltpu.HBM)],
    )(*chips, y_weights, y_pushed)
    return untiles(updated, fields.shape)


def solution(mesh):
    placed = (P(None, None, "gx", "gy"), P(None, "gx", "gy"), P(None, "gx", "gy"))
    return jax.shard_map(
        functools.partial(on_device, mesh.shape["gx"], mesh.shape["gy"]),
        mesh=mesh, in_specs=placed, out_specs=P(None, None, "gx", "gy"), check_vma=False,
    )
```

```python
import functools

import jax
import jax.numpy as jnp
from jax import lax
from jax.experimental import pallas as pl
from jax.experimental.pallas import tpu as pltpu
from jax.sharding import PartitionSpec as P


FIELDS = 4
KIND = (0, 0, 0, 1)
LANES = 128
SUB = 8
COEF_ROWS = 5
QUANTITIES = 2 * COEF_ROWS + 2 * FIELDS


def recip(value):
    return pl.reciprocal(value, approx=True)


def up(rows, step):
    step %= rows.shape[0]
    return pltpu.roll(rows, rows.shape[0] - step, 0) if step else rows


def down(rows, step):
    return pltpu.roll(rows, step, 0)


def row_index(rows):
    return lax.broadcasted_iota(jnp.int32, (rows, LANES), 0)


def pair(left, ground_u, link, ground_v, right):
    total_u, total_v = left + ground_u, right + ground_v
    scale = recip(total_u * total_v + link * (total_u + total_v))
    return (total_v + link) * scale, link * scale, (total_u + link) * scale


def join_two(low, face, high):
    link, ground_a, ground_u = low
    right, ground_v, ground_b = high
    uu, uv, vv = pair(link, ground_u, face, ground_v, right)
    u_left, v_left, u_right, v_right = link * uu, link * uv, right * uv, right * vv
    joined = (
        v_left * right,
        ground_a + ground_u * u_left + ground_v * v_left,
        ground_b + ground_u * u_right + ground_v * v_right,
    )
    return joined, (uu, uv, vv, u_left, v_left, u_right, v_right)


def join_two_sources(low, weights, high):
    _, _, _, u_left, v_left, u_right, v_right = weights
    (source_a, source_u), (source_v, source_b) = low, high
    return (
        source_a + source_u * u_left + source_v * v_left,
        source_b + source_u * u_right + source_v * v_right,
    )


def shifted(arrays, shift):
    return [up(x, shift) for x in arrays]


def join(chain, face, shift):
    return join_two(chain, face, shifted(chain, shift))


def join_sources(ends, weights, shift):
    return join_two_sources(ends, weights, shifted(ends, shift))


def schedule(count):
    nodes, rounds = list(range(count)), []
    while len(nodes) > 2:
        gone = range(1, len(nodes) - 1, 2)
        rounds.append([(nodes[i], nodes[i - 1], nodes[i + 1]) for i in gone])
        nodes = [n for i, n in enumerate(nodes) if i not in gone]
    return rounds


SHIFTS = (1, 2, 4)


def eliminate(coefs, half):
    count = len(coefs)
    ground = [1.0] * count
    link = {i: half * (coefs[i] + coefs[i + 1]) for i in range(count - 1)}
    cells, scales = {}, {}
    for round_ in schedule(count):
        for cell, low, high in round_:
            scale = recip(link[low] + link[cell] + ground[cell])
            to_low, to_high = link[low] * scale, link[cell] * scale
            ground[low] = ground[low] + to_low * ground[cell]
            ground[high] = ground[high] + to_high * ground[cell]
            link[low] = to_low * link[cell]
            cells[cell], scales[cell] = (to_low, to_high), scale
    face = half * (coefs[-1] + up(coefs[0], 1))
    chain, joins = (link[0], ground[0], ground[-1]), []
    for shift in SHIFTS:
        chain, weights = join(chain, up(face, shift - 1), shift)
        joins.append(weights)
    return cells, scales, joins, chain


def push_sources(cells, scales, joins, sources):
    sources, scaled = list(sources), {}
    for round_ in schedule(len(sources)):
        for cell, low, high in round_:
            to_low, to_high = cells[cell]
            sources[low] = sources[low] + to_low * sources[cell]
            sources[high] = sources[high] + to_high * sources[cell]
            scaled[cell] = scales[cell] * sources[cell]
    ends, joined = (sources[0], sources[-1]), []
    for shift, weights in zip(SHIFTS, joins):
        uu, uv, vv = weights[:3]
        source_u, source_v = ends[1], up(ends[0], shift)
        joined.append((uu * source_u + uv * source_v, uv * source_u + vv * source_v))
        ends = join_sources(ends, weights, shift)
    return scaled, joined, ends


def pull_values(cells, joins, scaled, joined, end_a, end_b):
    row = row_index(SUB)
    for shift, (u_left, v_left, u_right, v_right), (from_u, from_v) in reversed(list(zip(SHIFTS, joins, joined))):
        value_u = from_u + u_left * end_a + u_right * end_b
        value_v = from_v + v_left * end_a + v_right * end_b
        on_right = (row // shift) % 2 == 1
        end_a = jnp.where(on_right, down(value_v, shift), end_a)
        end_b = jnp.where(on_right, down(end_b, shift), value_u)
    count = len(cells) + 2
    values = {0: end_a, count - 1: end_b}
    for round_ in reversed(schedule(count)):
        for cell, low, high in round_:
            to_low, to_high = cells[cell]
            values[cell] = scaled[cell] + to_low * values[low] + to_high * values[high]
    return [values[t] for t in range(count)]


def weight_rows(count):
    return (2 * (count - 2) + 4 * len(SHIFTS)) * SUB


def source_rows(count):
    return (count - 2 + 2 * len(SHIFTS)) * SUB


def save(ref, arrays):
    for i, array in enumerate(arrays):
        ref[pl.ds(i * SUB, SUB), :] = array


def save_weights(ref, cells, joins):
    save(ref, [w for c in sorted(cells) for w in cells[c]] + [w for weights in joins for w in weights[3:]])


def save_sources(ref, scaled, joined):
    save(ref, [scaled[c] for c in sorted(scaled)] + [v for two in joined for v in two])


def load_weights(ref, count):
    def at(i):
        return ref[pl.ds(i * SUB, SUB), :]

    base = 2 * (count - 2)
    cells = {c: (at(2 * c - 2), at(2 * c - 1)) for c in range(1, count - 1)}
    return cells, [tuple(at(base + 4 * j + i) for i in range(4)) for j in range(len(SHIFTS))]


def load_sources(ref, count):
    def at(i):
        return ref[pl.ds(i * SUB, SUB), :]

    base = count - 2
    return {c: at(c - 1) for c in range(1, count - 1)}, [
        (at(base + 2 * j), at(base + 2 * j + 1)) for j in range(len(SHIFTS))
    ]


def spread(row):
    return jnp.broadcast_to(row[:1], (SUB, LANES))


def to_cells(rows):
    parts = jnp.swapaxes(rows.reshape(SUB, -1, LANES), 0, 1)
    return [parts[t] for t in range(parts.shape[0])]


def from_cells(cells):
    return jnp.swapaxes(jnp.stack(cells), 0, 1).reshape(-1, LANES)


def tiles(array):
    x_cells, y_cells = array.shape[-2:]
    split = array.reshape(-1, x_cells // SUB, SUB, y_cells // LANES, LANES)
    return split.transpose(0, 1, 3, 2, 4).reshape(-1, LANES)


def untiles(flat, shape):
    split = flat.reshape(-1, shape[-2] // SUB, shape[-1] // LANES, SUB, LANES)
    return split.transpose(0, 1, 3, 2, 4).reshape(shape)


def tile_at(field, x_tile, block, x_cells, blocks):
    return ((field * (x_cells // SUB) + x_tile) * blocks + block) * SUB


def load_x_cells(ref, field, x_cells, blocks):
    parts = to_cells(ref[pl.ds(field * x_cells * blocks, x_cells * blocks), :])
    return [
        [parts[(t // SUB * blocks + block) * SUB + t % SUB] for t in range(x_cells // SUB)] for block in range(blocks)
    ]


def load_block(ref, field, block, x_cells, blocks):
    return jnp.concatenate(
        [ref[pl.ds(tile_at(field, i, block, x_cells, blocks), SUB), :] for i in range(x_cells // SUB)]
    )


def solve_ring(quantity, ranks, rank, half):
    step = max(1, ranks // SUB)
    count = ranks // step
    device = [lax.rem(row_index(count) * step + (rank + 1 + k), ranks) for k in range(step)]
    last_row = row_index(count) == count - 1
    results = []
    for kind in range(2):
        chains, sources, first_coefs, last_coefs = [], [], [], []
        fields = [f for f in range(FIELDS) if KIND[f] == kind]
        for k in range(step):
            first, last, link, ground_a, ground_b = [
                quantity(kind * COEF_ROWS + i, k, step) for i in range(COEF_ROWS)
            ]
            ground_a = ground_a + jnp.where(device[k] == 0, half * first, 0.0)
            ground_b = ground_b + jnp.where(device[k] == ranks - 1, half * last, 0.0)
            chains.append((link, ground_a, ground_b))
            first_coefs.append(first)
            last_coefs.append(last)
            sources.append([[quantity(2 * COEF_ROWS + 2 * f + end, k, step) for end in range(2)] for f in fields])
        first_coefs.append(up(first_coefs[0], 1))
        faces = [
            jnp.where(device[k] == ranks - 1, 0.0, half * (last_coefs[k] + first_coefs[k + 1])) for k in range(step)
        ]
        own = shifted(chains[-1], count - 1)
        own_sources = [shifted(s, count - 1) for s in sources[-1]]
        left = up(faces[-1], count - 1)
        right = up(faces[step - 2], count - 1) if step > 1 else up(faces[0], count - 2)

        if step == 1:
            (chain,), (ends,), shift = chains, sources, 1
        else:
            joined, weights = join_two(chains[0], faces[0], chains[1])
            chain = [jnp.where(last_row, a, b) for a, b in zip(chains[0], joined)]
            ends = [
                [jnp.where(last_row, a, b) for a, b in zip(low, join_two_sources(low, weights, high))]
                for low, high in zip(*sources)
            ]
            shift = 1
        while shift < count:
            joined, weights = join(chain, up(faces[-1], shift - 1), shift)
            joined_ends = [join_sources(s, weights, shift) for s in ends]
            if shift == 1 and step == 1:
                alone = row_index(count) == count - 2
                joined = [jnp.where(alone, a, b) for a, b in zip(chain, joined)]
                joined_ends = [[jnp.where(alone, a, b) for a, b in zip(*two)] for two in zip(ends, joined_ends)]
            chain, ends, shift = joined, joined_ends, 2 * shift
        link, ground_u, ground_v = chain
        uu, uv, vv = pair(left, ground_u, link, ground_v, right)
        u_b, v_b, u_a, v_a = left * uu, left * uv, right * uv, right * vv
        link = own[0] + v_b * right
        ground_a = own[1] + ground_u * u_a + ground_v * v_a
        ground_b = own[2] + ground_u * u_b + ground_v * v_b
        scale = recip(ground_a * ground_b + link * (ground_a + ground_b))
        aa, ab, bb = (ground_b + link) * scale, link * scale, (ground_a + link) * scale
        for (source_u, source_v), (source_a, source_b) in zip(ends, own_sources):
            source_a = source_a + source_u * u_a + source_v * v_a
            source_b = source_b + source_u * u_b + source_v * v_b
            results.append((aa * source_a + ab * source_b, ab * source_a + bb * source_b))
    return results


def received_rows(turned, ranks, rows, blocks, block):
    def quantity(q, k, step):
        at = k * spaced(rows) + q * blocks + block
        return turned[pl.ds(at, ranks // step, stride=step * spaced(rows)), :]

    return quantity


def spaced(rows):
    return rows | 1


def rotate(received, turned, order, rows, rank):
    for at, device in enumerate(order):
        k = lax.rem(device + len(order) - 1 - rank, len(order))
        turned[pl.ds(k * spaced(rows), rows), :] = received[pl.ds(at * rows, rows), :]


def place(parts, turned, ranks, rows, rank):
    for k, other, message in parts:
        chip = lax.bitwise_xor(lax.div(rank, 2), k)
        device = 2 * chip + lax.bitwise_xor(lax.rem(rank, 2), int(other))
        at = lax.rem(device + ranks - rank - 1, ranks) * spaced(rows)
        turned[pl.ds(at, rows), :] = message


def coef_rows(coefs, chain):
    return (coefs[0][:1], coefs[-1][SUB - 1 :], chain[0][:1], chain[1][:1], chain[2][:1])


def x_ends_kernel(
    half, x_cells, blocks, ranks, rows,
    fields, viscosity, diffusivity, message, weights, pushed,
    line, fields_here, viscosity_here, diffusivity_here, arrived,
):
    per_field = x_cells * blocks
    copies = [
        pltpu.make_async_copy(viscosity, viscosity_here, arrived.at[0]),
        pltpu.make_async_copy(diffusivity, diffusivity_here, arrived.at[1]),
    ]
    for f in range(FIELDS):
        part = pl.ds(f * per_field, per_field)
        copies.append(pltpu.make_async_copy(fields.at[part], fields_here.at[part], arrived.at[2 + f]))
    for copy in copies:
        copy.start()

    def put(quantity, block, value):
        at = quantity * blocks + block
        line[at : at + 1, :] = value

    plans = {}
    for copy in copies[:2]:
        copy.wait()
    for kind, coef in enumerate((viscosity_here, diffusivity_here)):
        for block, coefs in enumerate(load_x_cells(coef, 0, x_cells, blocks)):
            *plan, chain = eliminate(coefs, half)
            plans[kind, block] = plan
            save_weights(weights.at[kind, block], plan[0], plan[2])
            for i, value in enumerate(coef_rows(coefs, chain)):
                put(kind * COEF_ROWS + i, block, value)
    for copy in copies[2:]:
        copy.wait()
    for f in range(FIELDS):
        for block, sources in enumerate(load_x_cells(fields_here, f, x_cells, blocks)):
            scaled, joined, ends = push_sources(*plans[KIND[f], block], sources)
            save_sources(pushed.at[f, block], scaled, joined)
            put(2 * COEF_ROWS + 2 * f, block, ends[0][:1])
            put(2 * COEF_ROWS + 2 * f + 1, block, ends[1][:1])
    for k in range(ranks):
        message[pl.ds(k * rows, rows), :] = line[...]


def x_join_kernel(
    half_x, half_y, x_cells, blocks, axis, order, rows,
    received, x_weights, x_pushed, viscosity, diffusivity, message, weights, pushed,
    turned,
):
    rank = lax.axis_index(axis)
    count, y_count = x_cells // SUB, blocks * LANES // SUB
    rotate(received, turned, order, rows, rank)
    ranks = len(order)
    plans = []
    for kind, coef in enumerate((viscosity, diffusivity)):
        coefs = to_cells(jnp.concatenate([load_block(coef, 0, b, x_cells, blocks).T for b in range(blocks)]))
        *plan, chain = eliminate(coefs, half_y)
        plans.append(plan)
        save_weights(weights.at[kind], plan[0], plan[2])
        for i, value in enumerate(coef_rows(coefs, chain)):
            message[kind * COEF_ROWS + i : kind * COEF_ROWS + i + 1, :] = value
    lines = [[] for _ in range(FIELDS)]
    for block in range(blocks):
        ends = solve_ring(received_rows(turned, ranks, rows, blocks, block), ranks, rank, half_x)
        for f in range(FIELDS):
            end_a, end_b = [spread(e) for e in ends[f]]
            values = pull_values(
                *load_weights(x_weights.at[KIND[f], block], count), *load_sources(x_pushed.at[f, block], count), end_a, end_b
            )
            lines[f].append(from_cells(values).T)
    for f in range(FIELDS):
        scaled, joined, ends = push_sources(*plans[KIND[f]], to_cells(jnp.concatenate(lines[f])))
        save_sources(pushed.at[f], scaled, joined)
        at = 2 * COEF_ROWS + 2 * f
        message[at : at + 1, :] = ends[0][:1]
        message[at + 1 : at + 2, :] = ends[1][:1]


def y_join_kernel(
    half, x_cells, blocks, axis, ranks, rows, layout,
    *refs,
):
    *chips, weights, pushed, updated, turned, here, left = refs
    per_field = x_cells * blocks
    count = blocks * LANES // SUB
    rank = lax.axis_index(axis)
    parts = []
    for (k, others), ref in zip(layout, chips):
        for i, other in enumerate(others):
            parts.append((k, other, ref[pl.ds(i * rows, rows), :]))
    place(parts, turned, ranks, rows, rank)
    ends = solve_ring(received_rows(turned, ranks, rows, 1, 0), ranks, rank, half)
    copies = []
    for f in range(FIELDS):
        end_a, end_b = [spread(e) for e in ends[f]]
        values = pull_values(
            *load_weights(weights.at[KIND[f]], count), *load_sources(pushed.at[f], count), end_a, end_b
        )
        lines = from_cells(values)
        for block in range(blocks):
            value = lines[block * LANES : (block + 1) * LANES].T
            for i in range(x_cells // SUB):
                here[pl.ds(tile_at(f, i, block, x_cells, blocks), SUB), :] = value[i * SUB : (i + 1) * SUB]
        part = pl.ds(f * per_field, per_field)
        copies.append(pltpu.make_async_copy(here.at[part], updated.at[part], left.at[f]))
        copies[-1].start()
    for copy in copies:
        copy.wait()


def call(kernel, outs, scratch, name, **kw):
    return pl.pallas_call(
        kernel,
        out_shape=outs,
        scratch_shapes=[pltpu.VMEM(s, jnp.float32) if isinstance(s, tuple) else s for s in scratch],
        compiler_params=pltpu.CompilerParams(vmem_limit_bytes=24 * 1024 * 1024),
        name=name,
        **kw,
    )


def near(shape):
    return pltpu.VMEM(shape, jnp.float32)


def far(shape):
    return pltpu.HBM(shape, jnp.float32)


def exchange(message, order, axis):
    flat = message.reshape(len(order), 1, -1)
    return lax.all_to_all(flat, axis, 0, 0, tiled=True, axis_index_groups=[list(order)]).reshape(-1, LANES)


X_ORDER = (10, 3, 1, 2, 0, 4, 5, 6, 7, 8, 9, 11, 12, 13, 14, 15)


def exchange_chips(message, ranks, axis):
    def send(array, step):
        return lax.ppermute(array, axis, [(i, i ^ step) for i in range(ranks)])

    chips = range(1, ranks // 2)
    early = chips[3 - 1]
    near_chip = send(message, 2 * early)
    other = send(message, 1)
    both = jnp.concatenate([message, other])
    layout, arrays = [(0, (False, True))], [both]
    for k in chips:
        if k != early:
            layout.append((k, (False, True)))
            arrays.append(send(both, 2 * k))
    layout += [(early, (False,)), (early, (True,))]
    arrays += [near_chip, send(near_chip, 1)]
    return layout, arrays


def on_device(x_ranks, y_ranks, fields, viscosity, diffusivity):
    _, _, x_cells, y_cells = fields.shape
    blocks = y_cells // LANES
    half_x, half_y = 0.5 * float(x_cells * x_cells), 0.5 * float(y_cells * y_cells)
    x_rows, y_rows = QUANTITIES * blocks, QUANTITIES
    x_order = X_ORDER
    assert sorted(x_order) == list(range(x_ranks))
    x_count, y_count = x_cells // SUB, y_cells // SUB
    args = [tiles(a) for a in (fields, viscosity, diffusivity)]
    sizes = [a.shape for a in args]
    in_hbm = [pltpu.with_memory_space_constraint(a, pltpu.HBM) for a in args]

    message, x_weights, x_pushed = call(
        functools.partial(x_ends_kernel, half_x, x_cells, blocks, x_ranks, x_rows),
        [
            near((x_ranks * x_rows, LANES)),
            near((2, blocks, weight_rows(x_count), LANES)),
            near((FIELDS, blocks, source_rows(x_count), LANES)),
        ],
        [(x_rows, LANES), *sizes, pltpu.SemaphoreType.DMA((2 + FIELDS,))], "x_ends",
        in_specs=[pl.BlockSpec(memory_space=pltpu.HBM)] * 3,
    )(*in_hbm)
    received = exchange(message, x_order, "gx")
    message, y_weights, y_pushed = call(
        functools.partial(x_join_kernel, half_x, half_y, x_cells, blocks, "gx", x_order, x_rows),
        [
            near((y_rows, LANES)),
            near((2, weight_rows(y_count), LANES)),
            near((FIELDS, source_rows(y_count), LANES)),
        ],
        [(x_ranks * spaced(x_rows), LANES)],
        "x_join",
    )(received, x_weights, x_pushed, *args[1:])
    layout, chips = exchange_chips(message, y_ranks, "gy")
    (updated,) = call(
        functools.partial(y_join_kernel, half_y, x_cells, blocks, "gy", y_ranks, y_rows, layout),
        [far(sizes[0])],
        [(y_ranks * spaced(y_rows), LANES), sizes[0], pltpu.SemaphoreType.DMA((FIELDS,))], "y_join",
        out_specs=[pl.BlockSpec(memory_space=pltpu.HBM)],
    )(*chips, y_weights, y_pushed)
    return untiles(updated, fields.shape)


def solution(mesh):
    placed = (P(None, None, "gx", "gy"), P(None, "gx", "gy"), P(None, "gx", "gy"))
    return jax.shard_map(
        functools.partial(on_device, mesh.shape["gx"], mesh.shape["gy"]),
        mesh=mesh, in_specs=placed, out_specs=P(None, None, "gx", "gy"), check_vma=False,
    )
```

```python
import functools

import jax
import jax.numpy as jnp
from jax import lax
from jax.experimental import pallas as pl
from jax.experimental.pallas import tpu as pltpu
from jax.sharding import PartitionSpec as P


FIELDS = 4
KIND = (0, 0, 0, 1)
LANES = 128
SUB = 8
COEF_ROWS = 5
QUANTITIES = 2 * COEF_ROWS + 2 * FIELDS


def recip(value):
    return pl.reciprocal(value, approx=True)


def up(rows, step):
    step %= rows.shape[0]
    return pltpu.roll(rows, rows.shape[0] - step, 0) if step else rows


def down(rows, step):
    return pltpu.roll(rows, step, 0)


def row_index(rows):
    return lax.broadcasted_iota(jnp.int32, (rows, LANES), 0)


def pair(left, ground_u, link, ground_v, right):
    total_u, total_v = left + ground_u, right + ground_v
    scale = recip(total_u * total_v + link * (total_u + total_v))
    return (total_v + link) * scale, link * scale, (total_u + link) * scale


def join_two(low, face, high):
    link, ground_a, ground_u = low
    right, ground_v, ground_b = high
    uu, uv, vv = pair(link, ground_u, face, ground_v, right)
    u_left, v_left, u_right, v_right = link * uu, link * uv, right * uv, right * vv
    joined = (
        v_left * right,
        ground_a + ground_u * u_left + ground_v * v_left,
        ground_b + ground_u * u_right + ground_v * v_right,
    )
    return joined, (uu, uv, vv, u_left, v_left, u_right, v_right)


def join_two_sources(low, weights, high):
    _, _, _, u_left, v_left, u_right, v_right = weights
    (source_a, source_u), (source_v, source_b) = low, high
    return (
        source_a + source_u * u_left + source_v * v_left,
        source_b + source_u * u_right + source_v * v_right,
    )


def shifted(arrays, shift):
    return [up(x, shift) for x in arrays]


def join(chain, face, shift):
    return join_two(chain, face, shifted(chain, shift))


def join_sources(ends, weights, shift):
    return join_two_sources(ends, weights, shifted(ends, shift))


def schedule(count):
    nodes, rounds = list(range(count)), []
    while len(nodes) > 2:
        gone = range(1, len(nodes) - 1, 2)
        rounds.append([(nodes[i], nodes[i - 1], nodes[i + 1]) for i in gone])
        nodes = [n for i, n in enumerate(nodes) if i not in gone]
    return rounds


SHIFTS = (1, 2, 4)


def eliminate(coefs, half):
    count = len(coefs)
    ground = [1.0] * count
    link = {i: half * (coefs[i] + coefs[i + 1]) for i in range(count - 1)}
    cells, scales = {}, {}
    for round_ in schedule(count):
        for cell, low, high in round_:
            scale = recip(link[low] + link[cell] + ground[cell])
            to_low, to_high = link[low] * scale, link[cell] * scale
            ground[low] = ground[low] + to_low * ground[cell]
            ground[high] = ground[high] + to_high * ground[cell]
            link[low] = to_low * link[cell]
            cells[cell], scales[cell] = (to_low, to_high), scale
    face = half * (coefs[-1] + up(coefs[0], 1))
    chain, joins = (link[0], ground[0], ground[-1]), []
    for shift in SHIFTS:
        chain, weights = join(chain, up(face, shift - 1), shift)
        joins.append(weights)
    return cells, scales, joins, chain


def push_sources(cells, scales, joins, sources):
    sources, scaled = list(sources), {}
    for round_ in schedule(len(sources)):
        for cell, low, high in round_:
            to_low, to_high = cells[cell]
            sources[low] = sources[low] + to_low * sources[cell]
            sources[high] = sources[high] + to_high * sources[cell]
            scaled[cell] = scales[cell] * sources[cell]
    ends, joined = (sources[0], sources[-1]), []
    for shift, weights in zip(SHIFTS, joins):
        uu, uv, vv = weights[:3]
        source_u, source_v = ends[1], up(ends[0], shift)
        joined.append((uu * source_u + uv * source_v, uv * source_u + vv * source_v))
        ends = join_sources(ends, weights, shift)
    return scaled, joined, ends


def pull_values(cells, joins, scaled, joined, end_a, end_b):
    row = row_index(SUB)
    for shift, (u_left, v_left, u_right, v_right), (from_u, from_v) in reversed(list(zip(SHIFTS, joins, joined))):
        value_u = from_u + u_left * end_a + u_right * end_b
        value_v = from_v + v_left * end_a + v_right * end_b
        on_right = (row // shift) % 2 == 1
        end_a = jnp.where(on_right, down(value_v, shift), end_a)
        end_b = jnp.where(on_right, down(end_b, shift), value_u)
    count = len(cells) + 2
    values = {0: end_a, count - 1: end_b}
    for round_ in reversed(schedule(count)):
        for cell, low, high in round_:
            to_low, to_high = cells[cell]
            values[cell] = scaled[cell] + to_low * values[low] + to_high * values[high]
    return [values[t] for t in range(count)]


def weight_rows(count):
    return (2 * (count - 2) + 4 * len(SHIFTS)) * SUB


def source_rows(count):
    return (count - 2 + 2 * len(SHIFTS)) * SUB


def save(ref, arrays):
    for i, array in enumerate(arrays):
        ref[pl.ds(i * SUB, SUB), :] = array


def save_weights(ref, cells, joins):
    save(ref, [w for c in sorted(cells) for w in cells[c]] + [w for weights in joins for w in weights[3:]])


def save_sources(ref, scaled, joined):
    save(ref, [scaled[c] for c in sorted(scaled)] + [v for two in joined for v in two])


def load_weights(ref, count):
    def at(i):
        return ref[pl.ds(i * SUB, SUB), :]

    base = 2 * (count - 2)
    cells = {c: (at(2 * c - 2), at(2 * c - 1)) for c in range(1, count - 1)}
    return cells, [tuple(at(base + 4 * j + i) for i in range(4)) for j in range(len(SHIFTS))]


def load_sources(ref, count):
    def at(i):
        return ref[pl.ds(i * SUB, SUB), :]

    base = count - 2
    return {c: at(c - 1) for c in range(1, count - 1)}, [
        (at(base + 2 * j), at(base + 2 * j + 1)) for j in range(len(SHIFTS))
    ]


def spread(row):
    return jnp.broadcast_to(row[:1], (SUB, LANES))


def to_cells(rows):
    parts = jnp.swapaxes(rows.reshape(SUB, -1, LANES), 0, 1)
    return [parts[t] for t in range(parts.shape[0])]


def from_cells(cells):
    return jnp.swapaxes(jnp.stack(cells), 0, 1).reshape(-1, LANES)


def tiles(array):
    x_cells, y_cells = array.shape[-2:]
    split = array.reshape(-1, x_cells // SUB, SUB, y_cells // LANES, LANES)
    return split.transpose(0, 1, 3, 2, 4).reshape(-1, LANES)


def untiles(flat, shape):
    split = flat.reshape(-1, shape[-2] // SUB, shape[-1] // LANES, SUB, LANES)
    return split.transpose(0, 1, 3, 2, 4).reshape(shape)


def tile_at(field, x_tile, block, x_cells, blocks):
    return ((field * (x_cells // SUB) + x_tile) * blocks + block) * SUB


def load_x_cells(ref, field, x_cells, blocks):
    parts = to_cells(ref[pl.ds(field * x_cells * blocks, x_cells * blocks), :])
    return [
        [parts[(t // SUB * blocks + block) * SUB + t % SUB] for t in range(x_cells // SUB)] for block in range(blocks)
    ]


def load_block(ref, field, block, x_cells, blocks):
    return jnp.concatenate(
        [ref[pl.ds(tile_at(field, i, block, x_cells, blocks), SUB), :] for i in range(x_cells // SUB)]
    )


def solve_ring(quantity, ranks, rank, half):
    step = max(1, ranks // SUB)
    count = ranks // step
    device = [lax.rem(row_index(count) * step + (rank + 1 + k), ranks) for k in range(step)]
    last_row = row_index(count) == count - 1
    results = []
    for kind in range(2):
        chains, sources, first_coefs, last_coefs = [], [], [], []
        fields = [f for f in range(FIELDS) if KIND[f] == kind]
        for k in range(step):
            first, last, link, ground_a, ground_b = [
                quantity(kind * COEF_ROWS + i, k, step) for i in range(COEF_ROWS)
            ]
            ground_a = ground_a + jnp.where(device[k] == 0, half * first, 0.0)
            ground_b = ground_b + jnp.where(device[k] == ranks - 1, half * last, 0.0)
            chains.append((link, ground_a, ground_b))
            first_coefs.append(first)
            last_coefs.append(last)
            sources.append([[quantity(2 * COEF_ROWS + 2 * f + end, k, step) for end in range(2)] for f in fields])
        first_coefs.append(up(first_coefs[0], 1))
        faces = [
            jnp.where(device[k] == ranks - 1, 0.0, half * (last_coefs[k] + first_coefs[k + 1])) for k in range(step)
        ]
        own = shifted(chains[-1], count - 1)
        own_sources = [shifted(s, count - 1) for s in sources[-1]]
        left = up(faces[-1], count - 1)
        right = up(faces[step - 2], count - 1) if step > 1 else up(faces[0], count - 2)

        if step == 1:
            (chain,), (ends,), shift = chains, sources, 1
        else:
            joined, weights = join_two(chains[0], faces[0], chains[1])
            chain = [jnp.where(last_row, a, b) for a, b in zip(chains[0], joined)]
            ends = [
                [jnp.where(last_row, a, b) for a, b in zip(low, join_two_sources(low, weights, high))]
                for low, high in zip(*sources)
            ]
            shift = 1
        while shift < count:
            joined, weights = join(chain, up(faces[-1], shift - 1), shift)
            joined_ends = [join_sources(s, weights, shift) for s in ends]
            if shift == 1 and step == 1:
                alone = row_index(count) == count - 2
                joined = [jnp.where(alone, a, b) for a, b in zip(chain, joined)]
                joined_ends = [[jnp.where(alone, a, b) for a, b in zip(*two)] for two in zip(ends, joined_ends)]
            chain, ends, shift = joined, joined_ends, 2 * shift
        link, ground_u, ground_v = chain
        uu, uv, vv = pair(left, ground_u, link, ground_v, right)
        u_b, v_b, u_a, v_a = left * uu, left * uv, right * uv, right * vv
        link = own[0] + v_b * right
        ground_a = own[1] + ground_u * u_a + ground_v * v_a
        ground_b = own[2] + ground_u * u_b + ground_v * v_b
        scale = recip(ground_a * ground_b + link * (ground_a + ground_b))
        aa, ab, bb = (ground_b + link) * scale, link * scale, (ground_a + link) * scale
        for (source_u, source_v), (source_a, source_b) in zip(ends, own_sources):
            source_a = source_a + source_u * u_a + source_v * v_a
            source_b = source_b + source_u * u_b + source_v * v_b
            results.append((aa * source_a + ab * source_b, ab * source_a + bb * source_b))
    return results


def received_rows(turned, ranks, rows, blocks, block):
    def quantity(q, k, step):
        at = k * spaced(rows) + q * blocks + block
        return turned[pl.ds(at, ranks // step, stride=step * spaced(rows)), :]

    return quantity


def spaced(rows):
    return rows | 1


def rotate(received, turned, order, rows, rank):
    for at, device in enumerate(order):
        k = lax.rem(device + len(order) - 1 - rank, len(order))
        turned[pl.ds(k * spaced(rows), rows), :] = received[pl.ds(at * rows, rows), :]


def place(parts, turned, ranks, rows, rank):
    mine = lax.div(rank, 2)
    for chips, other, message in parts:
        chip = sum(jnp.where(mine == i, source, 0) for i, source in enumerate(chips))
        device = 2 * chip + lax.bitwise_xor(lax.rem(rank, 2), int(other))
        at = lax.rem(device + ranks - rank - 1, ranks) * spaced(rows)
        turned[pl.ds(at, rows), :] = message


def coef_rows(coefs, chain):
    return (coefs[0][:1], coefs[-1][SUB - 1 :], chain[0][:1], chain[1][:1], chain[2][:1])


def x_ends_kernel(
    half, x_cells, blocks, ranks, rows,
    fields, viscosity, diffusivity, message, weights, pushed,
    line, fields_here, viscosity_here, diffusivity_here, arrived,
):
    per_field = x_cells * blocks
    copies = [
        pltpu.make_async_copy(viscosity, viscosity_here, arrived.at[0]),
        pltpu.make_async_copy(diffusivity, diffusivity_here, arrived.at[1]),
    ]
    for f in range(FIELDS):
        part = pl.ds(f * per_field, per_field)
        copies.append(pltpu.make_async_copy(fields.at[part], fields_here.at[part], arrived.at[2 + f]))
    for copy in copies:
        copy.start()

    def put(quantity, block, value):
        at = quantity * blocks + block
        line[at : at + 1, :] = value

    plans = {}
    for copy in copies[:2]:
        copy.wait()
    for kind, coef in enumerate((viscosity_here, diffusivity_here)):
        for block, coefs in enumerate(load_x_cells(coef, 0, x_cells, blocks)):
            *plan, chain = eliminate(coefs, half)
            plans[kind, block] = plan
            save_weights(weights.at[kind, block], plan[0], plan[2])
            for i, value in enumerate(coef_rows(coefs, chain)):
                put(kind * COEF_ROWS + i, block, value)
    for copy in copies[2:]:
        copy.wait()
    for f in range(FIELDS):
        for block, sources in enumerate(load_x_cells(fields_here, f, x_cells, blocks)):
            scaled, joined, ends = push_sources(*plans[KIND[f], block], sources)
            save_sources(pushed.at[f, block], scaled, joined)
            put(2 * COEF_ROWS + 2 * f, block, ends[0][:1])
            put(2 * COEF_ROWS + 2 * f + 1, block, ends[1][:1])
    for k in range(ranks):
        message[pl.ds(k * rows, rows), :] = line[...]


def x_join_kernel(
    half_x, half_y, x_cells, blocks, axis, order, rows,
    received, x_weights, x_pushed, viscosity, diffusivity, message, weights, pushed,
    turned,
):
    rank = lax.axis_index(axis)
    count, y_count = x_cells // SUB, blocks * LANES // SUB
    rotate(received, turned, order, rows, rank)
    ranks = len(order)
    plans = []
    for kind, coef in enumerate((viscosity, diffusivity)):
        coefs = to_cells(jnp.concatenate([load_block(coef, 0, b, x_cells, blocks).T for b in range(blocks)]))
        *plan, chain = eliminate(coefs, half_y)
        plans.append(plan)
        save_weights(weights.at[kind], plan[0], plan[2])
        for i, value in enumerate(coef_rows(coefs, chain)):
            message[kind * COEF_ROWS + i : kind * COEF_ROWS + i + 1, :] = value
    lines = [[] for _ in range(FIELDS)]
    for block in range(blocks):
        ends = solve_ring(received_rows(turned, ranks, rows, blocks, block), ranks, rank, half_x)
        for f in range(FIELDS):
            end_a, end_b = [spread(e) for e in ends[f]]
            values = pull_values(
                *load_weights(x_weights.at[KIND[f], block], count), *load_sources(x_pushed.at[f, block], count), end_a, end_b
            )
            lines[f].append(from_cells(values).T)
    for f in range(FIELDS):
        scaled, joined, ends = push_sources(*plans[KIND[f]], to_cells(jnp.concatenate(lines[f])))
        save_sources(pushed.at[f], scaled, joined)
        at = 2 * COEF_ROWS + 2 * f
        message[at : at + 1, :] = ends[0][:1]
        message[at + 1 : at + 2, :] = ends[1][:1]


def y_join_kernel(
    half, x_cells, blocks, axis, ranks, rows, layout,
    *refs,
):
    *chips, weights, pushed, updated, turned, here, left = refs
    per_field = x_cells * blocks
    count = blocks * LANES // SUB
    rank = lax.axis_index(axis)
    parts = []
    for (sources, others), ref in zip(layout, chips):
        for i, other in enumerate(others):
            parts.append((sources, other, ref[pl.ds(i * rows, rows), :]))
    place(parts, turned, ranks, rows, rank)
    ends = solve_ring(received_rows(turned, ranks, rows, 1, 0), ranks, rank, half)
    copies = []
    for f in range(FIELDS):
        end_a, end_b = [spread(e) for e in ends[f]]
        values = pull_values(
            *load_weights(weights.at[KIND[f]], count), *load_sources(pushed.at[f], count), end_a, end_b
        )
        lines = from_cells(values)
        for block in range(blocks):
            value = lines[block * LANES : (block + 1) * LANES].T
            for i in range(x_cells // SUB):
                here[pl.ds(tile_at(f, i, block, x_cells, blocks), SUB), :] = value[i * SUB : (i + 1) * SUB]
        part = pl.ds(f * per_field, per_field)
        copies.append(pltpu.make_async_copy(here.at[part], updated.at[part], left.at[f]))
        copies[-1].start()
    for copy in copies:
        copy.wait()


def call(kernel, outs, scratch, name, **kw):
    return pl.pallas_call(
        kernel,
        out_shape=outs,
        scratch_shapes=[pltpu.VMEM(s, jnp.float32) if isinstance(s, tuple) else s for s in scratch],
        compiler_params=pltpu.CompilerParams(vmem_limit_bytes=24 * 1024 * 1024),
        name=name,
        **kw,
    )


def near(shape):
    return pltpu.VMEM(shape, jnp.float32)


def far(shape):
    return pltpu.HBM(shape, jnp.float32)


def exchange(message, order, axis):
    flat = message.reshape(len(order), 1, -1)
    return lax.all_to_all(flat, axis, 0, 0, tiled=True, axis_index_groups=[list(order)]).reshape(-1, LANES)


X_ORDER = (10, 3, 1, 2, 0, 4, 5, 6, 7, 8, 9, 11, 12, 13, 14, 15)


Y_ROUNDS = ((3, 2, 0, 1), (2, 3, 1, 0), (1, 0, 3, 2))


def exchange_chips(message, ranks, axis):
    def swap(array):
        return lax.ppermute(array, axis, [(i, i ^ 1) for i in range(ranks)])

    def send(array, to):
        return lax.ppermute(array, axis, [(i, 2 * to[i // 2] + i % 2) for i in range(ranks)])

    def sources(to):
        return tuple(to.index(chip) for chip in range(len(to)))

    first, *later = Y_ROUNDS
    early = send(message, first)
    both = jnp.concatenate([message, swap(message)])
    layout, arrays = [(tuple(range(ranks // 2)), (False, True))], [both]
    for to in reversed(later):
        layout.append((sources(to), (False, True)))
        arrays.append(send(both, to))
    layout += [(sources(first), (False,)), (sources(first), (True,))]
    arrays += [early, swap(early)]
    return layout, arrays


def on_device(x_ranks, y_ranks, fields, viscosity, diffusivity):
    _, _, x_cells, y_cells = fields.shape
    blocks = y_cells // LANES
    half_x, half_y = 0.5 * float(x_cells * x_cells), 0.5 * float(y_cells * y_cells)
    x_rows, y_rows = QUANTITIES * blocks, QUANTITIES
    x_order = X_ORDER
    assert sorted(x_order) == list(range(x_ranks))
    x_count, y_count = x_cells // SUB, y_cells // SUB
    args = [tiles(a) for a in (fields, viscosity, diffusivity)]
    sizes = [a.shape for a in args]
    in_hbm = [pltpu.with_memory_space_constraint(a, pltpu.HBM) for a in args]

    message, x_weights, x_pushed = call(
        functools.partial(x_ends_kernel, half_x, x_cells, blocks, x_ranks, x_rows),
        [
            near((x_ranks * x_rows, LANES)),
            near((2, blocks, weight_rows(x_count), LANES)),
            near((FIELDS, blocks, source_rows(x_count), LANES)),
        ],
        [(x_rows, LANES), *sizes, pltpu.SemaphoreType.DMA((2 + FIELDS,))], "x_ends",
        in_specs=[pl.BlockSpec(memory_space=pltpu.HBM)] * 3,
    )(*in_hbm)
    received = exchange(message, x_order, "gx")
    message, y_weights, y_pushed = call(
        functools.partial(x_join_kernel, half_x, half_y, x_cells, blocks, "gx", x_order, x_rows),
        [
            near((y_rows, LANES)),
            near((2, weight_rows(y_count), LANES)),
            near((FIELDS, source_rows(y_count), LANES)),
        ],
        [(x_ranks * spaced(x_rows), LANES)],
        "x_join",
    )(received, x_weights, x_pushed, *args[1:])
    layout, chips = exchange_chips(message, y_ranks, "gy")
    (updated,) = call(
        functools.partial(y_join_kernel, half_y, x_cells, blocks, "gy", y_ranks, y_rows, layout),
        [far(sizes[0])],
        [(y_ranks * spaced(y_rows), LANES), sizes[0], pltpu.SemaphoreType.DMA((FIELDS,))], "y_join",
        out_specs=[pl.BlockSpec(memory_space=pltpu.HBM)],
    )(*chips, y_weights, y_pushed)
    return untiles(updated, fields.shape)


def solution(mesh):
    placed = (P(None, None, "gx", "gy"), P(None, "gx", "gy"), P(None, "gx", "gy"))
    return jax.shard_map(
        functools.partial(on_device, mesh.shape["gx"], mesh.shape["gy"]),
        mesh=mesh, in_specs=placed, out_specs=P(None, None, "gx", "gy"), check_vma=False,
    )
```

```python
import functools

import jax
import jax.numpy as jnp
from jax import lax
from jax.experimental import pallas as pl
from jax.experimental.pallas import tpu as pltpu
from jax.sharding import PartitionSpec as P


FIELDS = 4
KIND = (0, 0, 0, 1)
LANES = 128
SUB = 8
COEF_ROWS = 5
QUANTITIES = 2 * COEF_ROWS + 2 * FIELDS


def recip(value):
    return pl.reciprocal(value, approx=True)


def up(rows, step):
    step %= rows.shape[0]
    return pltpu.roll(rows, rows.shape[0] - step, 0) if step else rows


def down(rows, step):
    return pltpu.roll(rows, step, 0)


def row_index(rows):
    return lax.broadcasted_iota(jnp.int32, (rows, LANES), 0)


def pair(left, ground_u, link, ground_v, right):
    total_u, total_v = left + ground_u, right + ground_v
    scale = recip(total_u * total_v + link * (total_u + total_v))
    return (total_v + link) * scale, link * scale, (total_u + link) * scale


def join_two(low, face, high):
    link, ground_a, ground_u = low
    right, ground_v, ground_b = high
    uu, uv, vv = pair(link, ground_u, face, ground_v, right)
    u_left, v_left, u_right, v_right = link * uu, link * uv, right * uv, right * vv
    joined = (
        v_left * right,
        ground_a + ground_u * u_left + ground_v * v_left,
        ground_b + ground_u * u_right + ground_v * v_right,
    )
    return joined, (uu, uv, vv, u_left, v_left, u_right, v_right)


def join_two_sources(low, weights, high):
    _, _, _, u_left, v_left, u_right, v_right = weights
    (source_a, source_u), (source_v, source_b) = low, high
    return (
        source_a + source_u * u_left + source_v * v_left,
        source_b + source_u * u_right + source_v * v_right,
    )


def shifted(arrays, shift):
    return [up(x, shift) for x in arrays]


def join(chain, face, shift):
    return join_two(chain, face, shifted(chain, shift))


def join_sources(ends, weights, shift):
    return join_two_sources(ends, weights, shifted(ends, shift))


def schedule(count):
    nodes, rounds = list(range(count)), []
    while len(nodes) > 2:
        gone = range(1, len(nodes) - 1, 2)
        rounds.append([(nodes[i], nodes[i - 1], nodes[i + 1]) for i in gone])
        nodes = [n for i, n in enumerate(nodes) if i not in gone]
    return rounds


SHIFTS = (1, 2, 4)


def eliminate(coefs, half):
    count = len(coefs)
    ground = [1.0] * count
    link = {i: half * (coefs[i] + coefs[i + 1]) for i in range(count - 1)}
    cells, scales = {}, {}
    for round_ in schedule(count):
        for cell, low, high in round_:
            scale = recip(link[low] + link[cell] + ground[cell])
            to_low, to_high = link[low] * scale, link[cell] * scale
            ground[low] = ground[low] + to_low * ground[cell]
            ground[high] = ground[high] + to_high * ground[cell]
            link[low] = to_low * link[cell]
            cells[cell], scales[cell] = (to_low, to_high), scale
    face = half * (coefs[-1] + up(coefs[0], 1))
    chain, joins = (link[0], ground[0], ground[-1]), []
    for shift in SHIFTS:
        chain, weights = join(chain, up(face, shift - 1), shift)
        joins.append(weights)
    return cells, scales, joins, chain


def push_sources(cells, scales, joins, sources):
    sources, scaled = list(sources), {}
    for round_ in schedule(len(sources)):
        for cell, low, high in round_:
            to_low, to_high = cells[cell]
            sources[low] = sources[low] + to_low * sources[cell]
            sources[high] = sources[high] + to_high * sources[cell]
            scaled[cell] = scales[cell] * sources[cell]
    ends, joined = (sources[0], sources[-1]), []
    for shift, weights in zip(SHIFTS, joins):
        uu, uv, vv = weights[:3]
        source_u, source_v = ends[1], up(ends[0], shift)
        joined.append((uu * source_u + uv * source_v, uv * source_u + vv * source_v))
        ends = join_sources(ends, weights, shift)
    return scaled, joined, ends


def pull_values(cells, joins, scaled, joined, end_a, end_b):
    row = row_index(SUB)
    for shift, (u_left, v_left, u_right, v_right), (from_u, from_v) in reversed(list(zip(SHIFTS, joins, joined))):
        value_u = from_u + u_left * end_a + u_right * end_b
        value_v = from_v + v_left * end_a + v_right * end_b
        on_right = (row // shift) % 2 == 1
        end_a = jnp.where(on_right, down(value_v, shift), end_a)
        end_b = jnp.where(on_right, down(end_b, shift), value_u)
    count = len(cells) + 2
    values = {0: end_a, count - 1: end_b}
    for round_ in reversed(schedule(count)):
        for cell, low, high in round_:
            to_low, to_high = cells[cell]
            values[cell] = scaled[cell] + to_low * values[low] + to_high * values[high]
    return [values[t] for t in range(count)]


def weight_rows(count):
    return (2 * (count - 2) + 4 * len(SHIFTS)) * SUB


def source_rows(count):
    return (count - 2 + 2 * len(SHIFTS)) * SUB


def save(ref, arrays):
    for i, array in enumerate(arrays):
        ref[pl.ds(i * SUB, SUB), :] = array


def save_weights(ref, cells, joins):
    save(ref, [w for c in sorted(cells) for w in cells[c]] + [w for weights in joins for w in weights[3:]])


def save_sources(ref, scaled, joined):
    save(ref, [scaled[c] for c in sorted(scaled)] + [v for two in joined for v in two])


def load_weights(ref, count):
    def at(i):
        return ref[pl.ds(i * SUB, SUB), :]

    base = 2 * (count - 2)
    cells = {c: (at(2 * c - 2), at(2 * c - 1)) for c in range(1, count - 1)}
    return cells, [tuple(at(base + 4 * j + i) for i in range(4)) for j in range(len(SHIFTS))]


def load_sources(ref, count):
    def at(i):
        return ref[pl.ds(i * SUB, SUB), :]

    base = count - 2
    return {c: at(c - 1) for c in range(1, count - 1)}, [
        (at(base + 2 * j), at(base + 2 * j + 1)) for j in range(len(SHIFTS))
    ]


def spread(row):
    return jnp.broadcast_to(row[:1], (SUB, LANES))


def to_cells(rows):
    parts = jnp.swapaxes(rows.reshape(SUB, -1, LANES), 0, 1)
    return [parts[t] for t in range(parts.shape[0])]


def from_cells(cells):
    return jnp.swapaxes(jnp.stack(cells), 0, 1).reshape(-1, LANES)


def tiles(array):
    x_cells, y_cells = array.shape[-2:]
    split = array.reshape(-1, x_cells // SUB, SUB, y_cells // LANES, LANES)
    return split.transpose(0, 1, 3, 2, 4).reshape(-1, LANES)


def untiles(flat, shape):
    split = flat.reshape(-1, shape[-2] // SUB, shape[-1] // LANES, SUB, LANES)
    return split.transpose(0, 1, 3, 2, 4).reshape(shape)


def tile_at(field, x_tile, block, x_cells, blocks):
    return ((field * (x_cells // SUB) + x_tile) * blocks + block) * SUB


def load_x_cells(ref, field, x_cells, blocks):
    parts = to_cells(ref[pl.ds(field * x_cells * blocks, x_cells * blocks), :])
    return [
        [parts[(t // SUB * blocks + block) * SUB + t % SUB] for t in range(x_cells // SUB)] for block in range(blocks)
    ]


def load_block(ref, field, block, x_cells, blocks):
    return jnp.concatenate(
        [ref[pl.ds(tile_at(field, i, block, x_cells, blocks), SUB), :] for i in range(x_cells // SUB)]
    )


def solve_ring(quantity, ranks, rank, half):
    step = max(1, ranks // SUB)
    count = ranks // step
    device = [lax.rem(row_index(count) * step + (rank + 1 + k), ranks) for k in range(step)]
    last_row = row_index(count) == count - 1
    results = []
    for kind in range(2):
        chains, sources, first_coefs, last_coefs = [], [], [], []
        fields = [f for f in range(FIELDS) if KIND[f] == kind]
        for k in range(step):
            first, last, link, ground_a, ground_b = [
                quantity(kind * COEF_ROWS + i, k, step) for i in range(COEF_ROWS)
            ]
            ground_a = ground_a + jnp.where(device[k] == 0, half * first, 0.0)
            ground_b = ground_b + jnp.where(device[k] == ranks - 1, half * last, 0.0)
            chains.append((link, ground_a, ground_b))
            first_coefs.append(first)
            last_coefs.append(last)
            sources.append([[quantity(2 * COEF_ROWS + 2 * f + end, k, step) for end in range(2)] for f in fields])
        first_coefs.append(up(first_coefs[0], 1))
        faces = [
            jnp.where(device[k] == ranks - 1, 0.0, half * (last_coefs[k] + first_coefs[k + 1])) for k in range(step)
        ]
        own = shifted(chains[-1], count - 1)
        own_sources = [shifted(s, count - 1) for s in sources[-1]]
        left = up(faces[-1], count - 1)
        right = up(faces[step - 2], count - 1) if step > 1 else up(faces[0], count - 2)

        if step == 1:
            (chain,), (ends,), shift = chains, sources, 1
        else:
            joined, weights = join_two(chains[0], faces[0], chains[1])
            chain = [jnp.where(last_row, a, b) for a, b in zip(chains[0], joined)]
            ends = [
                [jnp.where(last_row, a, b) for a, b in zip(low, join_two_sources(low, weights, high))]
                for low, high in zip(*sources)
            ]
            shift = 1
        while shift < count:
            joined, weights = join(chain, up(faces[-1], shift - 1), shift)
            joined_ends = [join_sources(s, weights, shift) for s in ends]
            if shift == 1 and step == 1:
                alone = row_index(count) == count - 2
                joined = [jnp.where(alone, a, b) for a, b in zip(chain, joined)]
                joined_ends = [[jnp.where(alone, a, b) for a, b in zip(*two)] for two in zip(ends, joined_ends)]
            chain, ends, shift = joined, joined_ends, 2 * shift
        link, ground_u, ground_v = chain
        uu, uv, vv = pair(left, ground_u, link, ground_v, right)
        u_b, v_b, u_a, v_a = left * uu, left * uv, right * uv, right * vv
        link = own[0] + v_b * right
        ground_a = own[1] + ground_u * u_a + ground_v * v_a
        ground_b = own[2] + ground_u * u_b + ground_v * v_b
        scale = recip(ground_a * ground_b + link * (ground_a + ground_b))
        aa, ab, bb = (ground_b + link) * scale, link * scale, (ground_a + link) * scale
        for (source_u, source_v), (source_a, source_b) in zip(ends, own_sources):
            source_a = source_a + source_u * u_a + source_v * v_a
            source_b = source_b + source_u * u_b + source_v * v_b
            results.append((aa * source_a + ab * source_b, ab * source_a + bb * source_b))
    return results


def received_rows(turned, ranks, rows, blocks, block):
    def quantity(q, k, step):
        at = k * spaced(rows) + q * blocks + block
        return turned[pl.ds(at, ranks // step, stride=step * spaced(rows)), :]

    return quantity


def spaced(rows):
    return rows | 1


def rotate(received, turned, order, rows, rank):
    for at, device in enumerate(order):
        k = lax.rem(device + len(order) - 1 - rank, len(order))
        turned[pl.ds(k * spaced(rows), rows), :] = received[pl.ds(at * rows, rows), :]


def place(parts, turned, ranks, rows, rank):
    mine = lax.div(rank, 2)
    for chips, other, message in parts:
        chip = sum(jnp.where(mine == i, source, 0) for i, source in enumerate(chips))
        device = 2 * chip + lax.bitwise_xor(lax.rem(rank, 2), int(other))
        at = lax.rem(device + ranks - rank - 1, ranks) * spaced(rows)
        turned[pl.ds(at, rows), :] = message


def coef_rows(coefs, chain):
    return (coefs[0][:1], coefs[-1][SUB - 1 :], chain[0][:1], chain[1][:1], chain[2][:1])


def x_ends_kernel(
    half, x_cells, blocks, ranks, rows,
    fields, viscosity, diffusivity, message, weights, pushed,
    line, fields_here, viscosity_here, diffusivity_here, arrived,
):
    per_field = x_cells * blocks
    copies = [
        pltpu.make_async_copy(viscosity, viscosity_here, arrived.at[0]),
        pltpu.make_async_copy(diffusivity, diffusivity_here, arrived.at[1]),
    ]
    for f in range(FIELDS):
        part = pl.ds(f * per_field, per_field)
        copies.append(pltpu.make_async_copy(fields.at[part], fields_here.at[part], arrived.at[2 + f]))
    for copy in copies:
        copy.start()

    def put(quantity, block, value):
        at = quantity * blocks + block
        line[at : at + 1, :] = value

    plans = {}
    for copy in copies[:2]:
        copy.wait()
    for kind, coef in enumerate((viscosity_here, diffusivity_here)):
        for block, coefs in enumerate(load_x_cells(coef, 0, x_cells, blocks)):
            *plan, chain = eliminate(coefs, half)
            plans[kind, block] = plan
            save_weights(weights.at[kind, block], plan[0], plan[2])
            for i, value in enumerate(coef_rows(coefs, chain)):
                put(kind * COEF_ROWS + i, block, value)
    for copy in copies[2:]:
        copy.wait()
    for f in range(FIELDS):
        for block, sources in enumerate(load_x_cells(fields_here, f, x_cells, blocks)):
            scaled, joined, ends = push_sources(*plans[KIND[f], block], sources)
            save_sources(pushed.at[f, block], scaled, joined)
            put(2 * COEF_ROWS + 2 * f, block, ends[0][:1])
            put(2 * COEF_ROWS + 2 * f + 1, block, ends[1][:1])
    for k in range(ranks):
        message[pl.ds(k * rows, rows), :] = line[...]


def x_join_kernel(
    half_x, half_y, x_cells, blocks, axis, order, rows,
    received, x_weights, x_pushed, viscosity, diffusivity, message, weights, pushed,
    turned,
):
    rank = lax.axis_index(axis)
    count, y_count = x_cells // SUB, blocks * LANES // SUB
    rotate(received, turned, order, rows, rank)
    ranks = len(order)
    plans = []
    for kind, coef in enumerate((viscosity, diffusivity)):
        coefs = to_cells(jnp.concatenate([load_block(coef, 0, b, x_cells, blocks).T for b in range(blocks)]))
        *plan, chain = eliminate(coefs, half_y)
        plans.append(plan)
        save_weights(weights.at[kind], plan[0], plan[2])
        for i, value in enumerate(coef_rows(coefs, chain)):
            message[kind * COEF_ROWS + i : kind * COEF_ROWS + i + 1, :] = value
    lines = [[] for _ in range(FIELDS)]
    for block in range(blocks):
        ends = solve_ring(received_rows(turned, ranks, rows, blocks, block), ranks, rank, half_x)
        for f in range(FIELDS):
            end_a, end_b = [spread(e) for e in ends[f]]
            values = pull_values(
                *load_weights(x_weights.at[KIND[f], block], count), *load_sources(x_pushed.at[f, block], count), end_a, end_b
            )
            lines[f].append(from_cells(values).T)
    for f in range(FIELDS):
        scaled, joined, ends = push_sources(*plans[KIND[f]], to_cells(jnp.concatenate(lines[f])))
        save_sources(pushed.at[f], scaled, joined)
        at = 2 * COEF_ROWS + 2 * f
        message[at : at + 1, :] = ends[0][:1]
        message[at + 1 : at + 2, :] = ends[1][:1]


def y_join_kernel(
    half, x_cells, blocks, axis, ranks, rows, layout,
    *refs,
):
    *chips, weights, pushed, updated, turned, here, left = refs
    per_field = x_cells * blocks
    count = blocks * LANES // SUB
    rank = lax.axis_index(axis)
    parts = []
    for (sources, others), ref in zip(layout, chips):
        for i, other in enumerate(others):
            parts.append((sources, other, ref[pl.ds(i * rows, rows), :]))
    place(parts, turned, ranks, rows, rank)
    ends = solve_ring(received_rows(turned, ranks, rows, 1, 0), ranks, rank, half)
    copies = []
    for f in range(FIELDS):
        end_a, end_b = [spread(e) for e in ends[f]]
        values = pull_values(
            *load_weights(weights.at[KIND[f]], count), *load_sources(pushed.at[f], count), end_a, end_b
        )
        lines = from_cells(values)
        for block in range(blocks):
            value = lines[block * LANES : (block + 1) * LANES].T
            for i in range(x_cells // SUB):
                here[pl.ds(tile_at(f, i, block, x_cells, blocks), SUB), :] = value[i * SUB : (i + 1) * SUB]
        for low, high in ((0, 0), (1, 2), (3, 3)):
            if f == high:
                part = pl.ds(low * per_field, (high + 1 - low) * per_field)
                copies.append(pltpu.make_async_copy(here.at[part], updated.at[part], left.at[f]))
                copies[-1].start()
    for copy in copies:
        copy.wait()


def call(kernel, outs, scratch, name, **kw):
    return pl.pallas_call(
        kernel,
        out_shape=outs,
        scratch_shapes=[pltpu.VMEM(s, jnp.float32) if isinstance(s, tuple) else s for s in scratch],
        compiler_params=pltpu.CompilerParams(vmem_limit_bytes=24 * 1024 * 1024),
        name=name,
        **kw,
    )


def near(shape):
    return pltpu.VMEM(shape, jnp.float32)


def far(shape):
    return pltpu.HBM(shape, jnp.float32)


def exchange(message, order, axis):
    flat = message.reshape(len(order), 1, -1)
    return lax.all_to_all(flat, axis, 0, 0, tiled=True, axis_index_groups=[list(order)]).reshape(-1, LANES)


X_ORDER = (10, 3, 1, 2, 0, 4, 5, 6, 7, 8, 9, 11, 12, 13, 14, 15)


Y_ROUNDS = ((3, 2, 0, 1), (2, 3, 1, 0), (1, 0, 3, 2))


def exchange_chips(message, ranks, axis):
    def swap(array):
        return lax.ppermute(array, axis, [(i, i ^ 1) for i in range(ranks)])

    def send(array, to):
        return lax.ppermute(array, axis, [(i, 2 * to[i // 2] + i % 2) for i in range(ranks)])

    def sources(to):
        return tuple(to.index(chip) for chip in range(len(to)))

    first, *later = Y_ROUNDS
    early = send(message, first)
    both = jnp.concatenate([message, swap(message)])
    layout, arrays = [(tuple(range(ranks // 2)), (False, True))], [both]
    for to in reversed(later):
        layout.append((sources(to), (False, True)))
        arrays.append(send(both, to))
    layout += [(sources(first), (False,)), (sources(first), (True,))]
    arrays += [early, swap(early)]
    return layout, arrays


def on_device(x_ranks, y_ranks, fields, viscosity, diffusivity):
    _, _, x_cells, y_cells = fields.shape
    blocks = y_cells // LANES
    half_x, half_y = 0.5 * float(x_cells * x_cells), 0.5 * float(y_cells * y_cells)
    x_rows, y_rows = QUANTITIES * blocks, QUANTITIES
    x_order = X_ORDER
    assert sorted(x_order) == list(range(x_ranks))
    x_count, y_count = x_cells // SUB, y_cells // SUB
    args = [tiles(a) for a in (fields, viscosity, diffusivity)]
    sizes = [a.shape for a in args]
    in_hbm = [pltpu.with_memory_space_constraint(a, pltpu.HBM) for a in args]

    message, x_weights, x_pushed = call(
        functools.partial(x_ends_kernel, half_x, x_cells, blocks, x_ranks, x_rows),
        [
            near((x_ranks * x_rows, LANES)),
            near((2, blocks, weight_rows(x_count), LANES)),
            near((FIELDS, blocks, source_rows(x_count), LANES)),
        ],
        [(x_rows, LANES), *sizes, pltpu.SemaphoreType.DMA((2 + FIELDS,))], "x_ends",
        in_specs=[pl.BlockSpec(memory_space=pltpu.HBM)] * 3,
    )(*in_hbm)
    received = exchange(message, x_order, "gx")
    message, y_weights, y_pushed = call(
        functools.partial(x_join_kernel, half_x, half_y, x_cells, blocks, "gx", x_order, x_rows),
        [
            near((y_rows, LANES)),
            near((2, weight_rows(y_count), LANES)),
            near((FIELDS, source_rows(y_count), LANES)),
        ],
        [(x_ranks * spaced(x_rows), LANES)],
        "x_join",
    )(received, x_weights, x_pushed, *args[1:])
    layout, chips = exchange_chips(message, y_ranks, "gy")
    (updated,) = call(
        functools.partial(y_join_kernel, half_y, x_cells, blocks, "gy", y_ranks, y_rows, layout),
        [far(sizes[0])],
        [(y_ranks * spaced(y_rows), LANES), sizes[0], pltpu.SemaphoreType.DMA((FIELDS,))], "y_join",
        out_specs=[pl.BlockSpec(memory_space=pltpu.HBM)],
    )(*chips, y_weights, y_pushed)
    return untiles(updated, fields.shape)


def solution(mesh):
    placed = (P(None, None, "gx", "gy"), P(None, "gx", "gy"), P(None, "gx", "gy"))
    return jax.shard_map(
        functools.partial(on_device, mesh.shape["gx"], mesh.shape["gy"]),
        mesh=mesh, in_specs=placed, out_specs=P(None, None, "gx", "gy"), check_vma=False,
    )
```
